32 devices in a mesh: replica: 16 (over z, y, x), shard: 2 (over core).
Axes of the slice: x: 2, y: 2, z: 4, core: 2. Of those that a mesh axis runs over, the one named last changes fastest.
Arguments:
- inputs: bfloat16 [6304, 512], P(('replica', 'shard')), may hold values from -6 to 6
- norm1_gain: bfloat16 [512], P('shard'), may hold values from 0.5 to 1.5
- norm1_bias: bfloat16 [512], P('shard'), may hold values from -1.25 to 1.25
- qkv_weight: bfloat16 [512, 1536], P('shard'), may hold values from -0.25 to 0.25
- query_bias: bfloat16 [512], P('shard'), may hold values from -1.25 to 1.25
- value_bias: bfloat16 [512], P('shard'), may hold values from -1.25 to 1.25
- out_weight: bfloat16 [512, 512], P('shard'), may hold values from -0.5 to 0.5
- out_bias: bfloat16 [512], P('shard'), may hold values from -1.25 to 1.25
- norm2_gain: bfloat16 [512], P('shard'), may hold values from 0.5 to 1.5
- norm2_bias: bfloat16 [512], P('shard'), may hold values from -1.25 to 1.25
- router_weight: bfloat16 [512, 4], P('shard'), may hold values from -0.125 to 0.125
- noise: float32 [6304, 4], P(('replica', 'shard')), may hold values from -1.75 to 1.75
- expert_in: bfloat16 [4, 512, 2048], P('shard'), may hold values from -0.25 to 0.25
- expert_in_bias: bfloat16 [4, 2048], P('shard'), may hold values from -0.625 to 0.625
- expert_out: bfloat16 [4, 2048, 512], P('shard'), may hold values from -0.5 to 0.5
- expert_out_bias: bfloat16 [4, 512], P('shard'), may hold values from -1.25 to 1.25
- routes: int32 [6304, 2], P(('replica', 'shard')), may hold values from 0 to 3, all different within a row
- priority: int32 [32, 394], P(('replica', 'shard')), may hold values from 0 to 393, each once within a row
- cotangent: bfloat16 [6304, 512], P(('replica', 'shard')), may hold values from -6 to 6
Outputs:
- output: bfloat16 [6304, 512], P(('replica', 'shard'))
- input_grad: float32 [6304, 512], P(('replica', 'shard'))
- grad_norm1_gain: float32 [512], P('shard')
- grad_norm1_bias: float32 [512], P('shard')
- grad_qkv_weight: float32 [512, 1536], P('shard')
- grad_query_bias: float32 [512], P('shard')
- grad_value_bias: float32 [512], P('shard')
- grad_out_weight: float32 [512, 512], P('shard')
- grad_out_bias: float32 [512], P('shard')
- grad_norm2_gain: float32 [512], P('shard')
- grad_norm2_bias: float32 [512], P('shard')
- grad_router_weight: float32 [512, 4], P('shard')
- grad_expert_in: float32 [4, 512, 2048], P('shard')
- grad_expert_in_bias: float32 [4, 2048], P('shard')
- grad_expert_out: float32 [4, 2048, 512], P('shard')
- grad_expert_out_bias: float32 [4, 512], P('shard')
The draws below stay inside these ranges and needn't reach their ends.
Inputs may be any that keep to these rules, and one draw needn't show every extreme that they name: `routes`: each token names two different experts; every expert is named by some token. `priority`: each row is a permutation; it ranks the pairs of the tokens of the device of that row, pair 2 t + k being token t's k-th route.
All inputs are finite; a program needn't handle non-finite values.
Results may differ from the reference program's by a relative error of at most 0.017.
Values may be sent and summed in bfloat16 or wider, within the bound.
A program may use at most 192 MiB of HBM per device.

```python
import jax
import jax.numpy as jnp
from jax import lax

D = 512
HEADS = 8
HEAD_DIM = 64
H = 2048
PATCHES = 197
IMG_DEV = 1
E = 4
TOK_DEV = 197
TOKENS = 6304
CAP = 3152
DEVICES = 32


def block_scale(rng, shape, cuts, smallest, high):
    gain, own = 1.0, jax.random.fold_in(rng, 6)
    for dim, blocks in cuts:
        draws = jnp.exp(jax.random.uniform(jax.random.fold_in(own, dim), (blocks,), jnp.float32, smallest / len(cuts), high / len(cuts)))
        gain = gain * jnp.repeat(draws, shape[dim] // blocks).reshape([-1 if axis == dim else 1 for axis in range(len(shape))])
    return gain


def different_ones(own_key, rows, count, top, lift):
    sequence = jax.random.permutation(jax.random.fold_in(own_key, 1), count)
    favour = sequence
    for power in range(3):
        favour = favour * favour // count
    favour = favour * lift // count
    chance = jax.random.randint(jax.random.fold_in(own_key, 2), (rows, count), 0, 4096) + favour
    fixed_rows = jax.random.permutation(jax.random.fold_in(own_key, 3), rows)[jnp.arange(count) % rows]
    chance = jnp.where(jnp.arange(rows)[:, None] == fixed_rows[None, :], 1 << 14, chance)
    score = chance * count + jnp.arange(count)
    return lax.top_k(score.astype(jnp.int32), top)[1].astype(jnp.int32)


def gaussian(key, extent, deviation, limit, cuts=(), held_as=jnp.bfloat16):
    values = deviation * jax.random.normal(key, extent, jnp.float32)
    if cuts:
        values = values * block_scale(key, extent, cuts, -0.22, 0.18)
    return jnp.clip(values, -limit, limit).astype(held_as)


def setup_inputs(seed: int = 0) -> dict:
    key_list = jax.random.split(jax.random.key(seed), 20)
    inputs = gaussian(key_list[0], (TOKENS, D), 1.0, 6.0, ((0, 32),))
    norm1_gain = jnp.clip(1.0 + 0.1 * jax.random.normal(key_list[1], (D,), jnp.float32), 0.5, 1.5).astype(jnp.bfloat16)
    norm1_bias = gaussian(key_list[2], (D,), 0.2, 1.25, ((0, 2),))
    qkv_weight = gaussian(key_list[3], (D, 3 * D), D ** -0.5, 0.25, ((0, 2),))
    query_bias = gaussian(key_list[4], (D,), 0.2, 1.25, ((0, 2),))
    value_bias = gaussian(key_list[5], (D,), 0.2, 1.25, ((0, 2),))
    out_weight = gaussian(key_list[6], (D, D), (D // 4) ** -0.5, 0.5, ((0, 2),))
    out_bias = gaussian(key_list[7], (D,), 0.2, 1.25, ((0, 2),))
    norm2_gain = jnp.clip(1.0 + 0.1 * jax.random.normal(key_list[8], (D,), jnp.float32), 0.5, 1.5).astype(jnp.bfloat16)
    norm2_bias = gaussian(key_list[9], (D,), 0.2, 1.25, ((0, 2),))
    router_weight = gaussian(key_list[10], (D, E), (4 * D) ** -0.5, 0.125, ((0, 2),))
    noise = gaussian(key_list[11], (TOKENS, E), 0.3, 1.75, ((0, 32),), jnp.float32)
    expert_in = gaussian(key_list[12], (E, D, H), D ** -0.5, 0.25, ((0, 2),))
    expert_in_bias = gaussian(key_list[13], (E, H), 0.1, 0.625, ((0, 2),))
    expert_out = gaussian(key_list[14], (E, H, D), (H // 16) ** -0.5, 0.5, ((0, 2),))
    expert_out_bias = gaussian(key_list[15], (E, D), 0.2, 1.25, ((0, 2),))
    routes = different_ones(key_list[16], TOKENS, E, 2, 4096)
    priority = jax.vmap(lambda own: jax.random.permutation(own, 2 * TOK_DEV))(jax.random.split(key_list[17], DEVICES)).reshape((DEVICES, 2 * TOK_DEV)).astype(jnp.int32)
    cotangent = gaussian(key_list[18], (TOKENS, D), 1.0, 6.0, ((0, 32),))
    return {"inputs": inputs, "norm1_gain": norm1_gain, "norm1_bias": norm1_bias, "qkv_weight": qkv_weight, "query_bias": query_bias, "value_bias": value_bias, "out_weight": out_weight, "out_bias": out_bias, "norm2_gain": norm2_gain, "norm2_bias": norm2_bias, "router_weight": router_weight, "noise": noise, "expert_in": expert_in, "expert_in_bias": expert_in_bias, "expert_out": expert_out, "expert_out_bias": expert_out_bias, "routes": routes, "priority": priority, "cotangent": cotangent}


LN_EPS = 1e-06
HIGH = lax.Precision.HIGHEST

@jax.custom_vjp
def low(v):
    return lax.optimization_barrier(v.astype(jnp.bfloat16)).astype(jnp.float32)

@jax.custom_vjp
def low_back(v):
    return v

def low_keep(v):
    return (low(v), None)

def low_pass(kept, grad):
    return (grad,)

def back_keep(v):
    return (v, None)

def back_low(kept, grad):
    return (low(grad),)
low.defvjp(low_keep, low_pass)
low_back.defvjp(back_keep, back_low)

def layer_norm(values, gain_vector, bias_vector):
    centered = values - lax.optimization_barrier(jnp.mean(values, axis=-1, keepdims=True))
    spread = lax.rsqrt(lax.optimization_barrier(jnp.mean(centered * centered, axis=-1, keepdims=True)) + LN_EPS)
    return centered * spread * gain_vector + bias_vector

def kept_gates(pair_expert, ranks, offsets, capacity, expert_count):
    same = pair_expert[:, None] == pair_expert[None, :]
    earlier = ranks[None, :] < ranks[:, None]
    before = lax.optimization_barrier(jnp.sum(jnp.where(same & earlier, 1, 0).astype(jnp.int32), axis=1))
    onehot = pair_expert[:, None] == jnp.arange(expert_count, dtype=jnp.int32)[None, :]
    first_slot = lax.optimization_barrier(jnp.sum(jnp.where(onehot, offsets[None, :], 0).astype(jnp.int32), axis=1))
    keep = before + first_slot < capacity
    picked = jnp.where(onehot & keep[:, None], 1.0, 0.0).astype(jnp.float32)
    return lax.optimization_barrier(jnp.sum(picked.reshape(-1, 2, expert_count), axis=1))

def forward(params, tokens_block, noise_block, chosen):
    gain_one, bias_one, weight_qkv, bias_query, bias_value, weight_proj, bias_proj, gain_two, bias_two, weight_route, weight_in, bias_in, weight_out, bias_out = params
    normed_one = low(layer_norm(tokens_block, gain_one, bias_one))
    qkv_bias = jnp.concatenate([bias_query, jnp.zeros_like(bias_query), bias_value])
    mixed = low(low_back(jnp.dot(normed_one, weight_qkv, precision=HIGH) + qkv_bias))
    shaped = mixed.reshape(IMG_DEV, PATCHES, 3, HEADS, HEAD_DIM)
    query, keys, values = (shaped[:, :, 0], shaped[:, :, 1], shaped[:, :, 2])
    scores = low_back(jnp.einsum('bqhd,bkhd->bhqk', query, keys, precision=HIGH) * HEAD_DIM ** (-0.5))
    attn_probs = low(jax.nn.softmax(scores, axis=-1))
    context = jnp.einsum('bhqk,bkhd->bqhd', attn_probs, values, precision=HIGH).reshape(TOK_DEV, D)
    context = low(low_back(context))
    branch = low_back(jnp.dot(context, weight_proj, precision=HIGH) + bias_proj)
    middle = tokens_block + branch
    normed_two = low(layer_norm(middle, gain_two, bias_two))
    logits = low_back(jnp.dot(normed_two, weight_route, precision=HIGH)) + noise_block
    gate_weights = jax.nn.softmax(logits, axis=-1) * chosen
    running = middle
    for expert_index in range(E):
        pre_act = low_back(jnp.dot(normed_two, weight_in[expert_index], precision=HIGH) + bias_in[expert_index])
        hidden = low(jax.nn.gelu(pre_act))
        result = low_back(jnp.dot(hidden, weight_out[expert_index], precision=HIGH) + bias_out[expert_index])
        running = running + gate_weights[:, expert_index:expert_index + 1] * result
    return running

def device_gates(record):
    return kept_gates(record[0], record[1], record[2], CAP, E)

def reference(inputs, norm1_gain, norm1_bias, qkv_weight, query_bias, value_bias, out_weight, out_bias, norm2_gain, norm2_bias, router_weight, noise, expert_in, expert_in_bias, expert_out, expert_out_bias, routes, priority, cotangent):
    pair_expert = routes.reshape(DEVICES, 2 * TOK_DEV)
    onehot = (pair_expert[..., None] == jnp.arange(E, dtype=jnp.int32)).astype(jnp.int32)
    expert_load = lax.optimization_barrier(jnp.sum(onehot, axis=1))
    offsets = (jnp.cumsum(expert_load, axis=0) - expert_load).astype(jnp.int32)
    chosen = lax.map(device_gates, (pair_expert, priority, offsets))
    params = tuple((weight.astype(jnp.float32) for weight in (norm1_gain, norm1_bias, qkv_weight, query_bias, value_bias, out_weight, out_bias, norm2_gain, norm2_bias, router_weight, expert_in, expert_in_bias, expert_out, expert_out_bias)))
    blocks = inputs.astype(jnp.float32).reshape(DEVICES, TOK_DEV, D)
    noises = noise.astype(jnp.float32).reshape(DEVICES, TOK_DEV, E)
    cotangents = cotangent.astype(jnp.float32).reshape(DEVICES, TOK_DEV, D)

    def advance(running, portion):
        tokens_block, noise_block, chosen_block, cot_block = portion

        def local_forward(params_now, block_now):
            return forward(params_now, block_now, noise_block, chosen_block)
        result_rows, pullback = jax.vjp(local_forward, params, tokens_block)
        grad_params, grad_block = pullback(cot_block)
        running = jax.tree.map(jnp.add, running, grad_params)
        return (running, (result_rows.astype(jnp.bfloat16), grad_block))
    initial = jax.tree.map(jnp.zeros_like, params)
    grads, (outputs, grad_blocks) = lax.scan(advance, initial, (blocks, noises, chosen, cotangents))
    return (outputs.reshape(TOKENS, D), grad_blocks.reshape(TOKENS, D), grads[0], grads[1], grads[2], grads[3], grads[4], grads[5], grads[6], grads[7], grads[8], grads[9], grads[10], grads[11], grads[12], grads[13])
```

```python
import functools

import jax
import jax.numpy as jnp
from jax import lax
from jax.experimental import pallas as pl
from jax.experimental.pallas import tpu as pltpu
from jax.sharding import PartitionSpec as P

HEAD_DIM = 64
PATCHES = 197
LN_EPS = 1e-06
MESH = pl.DeviceIdType.MESH
NT = (((1,), (1,)), ((), ()))
GELU_K = 0.7978845608028654
GELU_A = 0.044715


def half(values):
    return values.astype(jnp.bfloat16)


def dot(a, b):
    return jnp.dot(a, b, preferred_element_type=jnp.float32)


def dot_nt(a, b):
    return lax.dot_general(a, b, NT, preferred_element_type=jnp.float32)


def gelu_parts(x):
    x2 = x * x
    q = 0.5 + 0.5 * jnp.tanh(x * (GELU_K + (GELU_K * GELU_A) * x2))
    h = x * q
    return h, q + (h * (1.0 - q)) * (2 * GELU_K + (6 * GELU_K * GELU_A) * x2)


def layer_norm(values, gain_vector, bias_vector):
    centered = values - jnp.mean(values, axis=-1, keepdims=True)
    spread = lax.rsqrt(jnp.mean(centered * centered, axis=-1, keepdims=True) + LN_EPS)
    return centered * spread * gain_vector + bias_vector


def kept_gates(pair_expert, ranks, offsets, capacity, expert_count):
    same = pair_expert[:, None] == pair_expert[None, :]
    earlier = ranks[None, :] < ranks[:, None]
    before = jnp.sum(jnp.where(same & earlier, 1, 0).astype(jnp.int32), axis=1)
    onehot = pair_expert[:, None] == jnp.arange(expert_count, dtype=jnp.int32)[None, :]
    first_slot = jnp.sum(jnp.where(onehot, offsets[None, :], 0).astype(jnp.int32), axis=1)
    keep = before + first_slot < capacity
    picked = jnp.where(onehot & keep[:, None], 1.0, 0.0).astype(jnp.float32)
    return jnp.sum(picked.reshape(-1, 2, expert_count), axis=1)


def place():
    r = lax.axis_index("replica")
    return r // 4, (r // 2) % 2, r % 2, lax.axis_index("shard")


def rep(z, y, x):
    return (z * 2 + y) * 2 + x


def gather_kernel(zs, a_ref, b_ref, a_all, b_all, own_sem, send_sem, recv_sem, core_send, core_recv):
    z, y, x, c = place()
    me = rep(z, y, x)
    up, down, xn, yn = rep(z + 1, y, x), rep(z - 1, y, x), rep(z, y, 1 - x), rep(z, 1 - y, x)
    bar = pltpu.get_barrier_semaphore()

    @pl.when(z < zs - 1)
    def _():
        pl.semaphore_signal(bar, inc=1, device_id=(up, c), device_id_type=MESH)

    @pl.when(z > 0)
    def _():
        pl.semaphore_signal(bar, inc=1, device_id=(down, c), device_id_type=MESH)

    for t in ((xn, c), (yn, c), (me, 1 - c)):
        pl.semaphore_signal(bar, inc=1, device_id=t, device_id_type=MESH)
    pl.semaphore_wait(bar, 3 + (z < zs - 1).astype(jnp.int32) + (z > 0).astype(jnp.int32))

    src = (a_ref, b_ref)
    dst = (a_all, b_all)

    def link(m, kind, block, target):
        ref = dst[m].at[block * 2 + c]
        return pltpu.make_async_remote_copy(
            src_ref=ref, dst_ref=ref, send_sem=send_sem.at[m, kind, block], recv_sem=recv_sem.at[m, block],
            device_id=(target, c), device_id_type=MESH)

    def across(m, block):
        ref = dst[m].at[block * 2 + c]
        return pltpu.make_async_remote_copy(
            src_ref=ref, dst_ref=ref, send_sem=core_send.at[m, block], recv_sem=core_recv.at[m, block],
            device_id=(me, 1 - c), device_id_type=MESH)

    def from_core(m, block):
        ref = dst[m].at[block * 2 + 1 - c]
        return pltpu.make_async_remote_copy(
            src_ref=ref, dst_ref=ref, send_sem=core_send.at[m, block], recv_sem=core_recv.at[m, block],
            device_id=(me, 1 - c), device_id_type=MESH)

    first = (xn, yn)
    second = (yn, xn)

    def column(m, zz):
        block = rep(zz, y, x)
        link(m, 2, block, first[m]).start()
        link(m, 3, block, second[m]).start()
        across(m, block).start()

    own = [pltpu.make_async_copy(src[m], dst[m].at[me * 2 + c], own_sem.at[m]) for m in range(2)]
    for m in range(2):
        own[m].start()
    for m in range(2):
        own[m].wait()
    for m in range(2):
        pl.when(z < zs - 1)(lambda m=m: link(m, 0, me, up).start())
        pl.when(z > 0)(lambda m=m: link(m, 1, me, down).start())
    for m in range(2):
        column(m, z)

    def arrived(m, block):
        link(m, 0, block, up).wait_recv()

    def side_column(m, zz):
        block = rep(zz, y, 1 - x) if m == 0 else rep(zz, 1 - y, x)
        arrived(m, block)
        link(m, 3, block, second[m]).start()
        across(m, block).start()

    def far(m, zz):
        blocks = (rep(zz, 1 - y, x), rep(zz, 1 - y, 1 - x)) if m == 0 else (rep(zz, y, 1 - x), rep(zz, 1 - y, 1 - x))
        for block in blocks:
            arrived(m, block)
            across(m, block).start()

    for k in range(1, zs):
        for m in range(2):
            @pl.when(z - k >= 0)
            def _(m=m, k=k):
                arrived(m, rep(z - k, y, x))
                pl.when(z < zs - 1)(lambda: link(m, 0, rep(z - k, y, x), up).start())
                column(m, z - k)

            @pl.when(z + k < zs)
            def _(m=m, k=k):
                arrived(m, rep(z + k, y, x))
                pl.when(z > 0)(lambda: link(m, 1, rep(z + k, y, x), down).start())
                column(m, z + k)

        for m in range(2):
            for s in (-1, 1):
                if k == 1 and s == 1:
                    continue
                d = s * (k - 1)
                pl.when((z + d >= 0) & (z + d < zs))(lambda m=m, d=d: side_column(m, z + d))
    for m in range(2):
        for d in (1 - zs, zs - 1):
            pl.when((z + d >= 0) & (z + d < zs))(lambda m=m, d=d: side_column(m, z + d))
    for zz in range(zs):
        for m in range(2):
            far(m, zz)
    for block in range(4 * zs):
        for m in range(2):
            from_core(m, block).wait_recv()
            across(m, block).wait_send()
    for zz in range(zs):
        for m in range(2):
            pl.when((z >= zz) & (z < zs - 1))(lambda m=m, zz=zz: link(m, 0, rep(zz, y, x), up).wait_send())
            pl.when((z <= zz) & (z > 0))(lambda m=m, zz=zz: link(m, 1, rep(zz, y, x), down).wait_send())
            link(m, 2, rep(zz, y, x), xn).wait_send()
            link(m, 3, rep(zz, y, x), xn).wait_send()
            side = rep(zz, y, 1 - x) if m == 0 else rep(zz, 1 - y, x)
            link(m, 3, side, xn).wait_send()


def gather_blocks(a, b, zs):
    rows, width = a.shape
    hbm = pl.BlockSpec(memory_space=pl.ANY)
    n = 4 * zs
    return pl.pallas_call(
        functools.partial(gather_kernel, zs),
        out_shape=(jax.ShapeDtypeStruct((2 * n, rows, width), a.dtype), jax.ShapeDtypeStruct((2 * n, rows, width), a.dtype)),
        in_specs=[hbm, hbm],
        out_specs=(hbm, hbm),
        scratch_shapes=[
            pltpu.SemaphoreType.DMA((2,)),
            pltpu.SemaphoreType.DMA((2, 4, n)),
            pltpu.SemaphoreType.DMA((2, n)),
            pltpu.SemaphoreType.DMA((2, n)),
            pltpu.SemaphoreType.DMA((2, n)),
        ],
        compiler_params=pltpu.CompilerParams(collective_id=0, has_side_effects=True),
        name="token_gather",
    )(a, b)


def slice_kernel(block, n_ref, c_ref, g_ref, wi_ref, wo_ref, b_ref, gin_ref, gout_ref,
                 acc_in, acc_out, st_in, st_out, own_sem, send_sem, recv_sem):
    z, y, x, c = place()
    zn = z + 1 - 2 * (z % 2)
    targets = (rep(z, y, 1 - x), rep(z, 1 - y, x), rep(zn, y, x))
    bar = pltpu.get_barrier_semaphore()
    for t in targets:
        pl.semaphore_signal(bar, inc=1, device_id=(t, c), device_id_type=MESH)
    pl.semaphore_wait(bar, 3)
    qx, qy = (x + z) % 2, (y + z) % 2
    mine = qx * 2 + qy
    quarters = ((1 - qx) * 2 + qy, qx * 2 + 1 - qy, (1 - qx) * 2 + 1 - qy)
    experts, hq, _ = wi_ref.shape
    total = n_ref.shape[0]

    def sends(e, kind):
        src = st_in.at[e] if kind == 0 else st_out.at[e]
        cols = pl.ds(pl.multiple_of(mine * hq, 128), hq)
        dst = gin_ref.at[e, :, cols] if kind == 0 else gout_ref.at[e, cols, :]
        out = [pltpu.make_async_remote_copy(
            src_ref=src, dst_ref=dst, send_sem=send_sem.at[e, kind, i], recv_sem=recv_sem.at[e, kind, i],
            device_id=(t, c), device_id_type=MESH) for i, t in enumerate(targets)]
        return out, pltpu.make_async_copy(src, dst, own_sem.at[e, kind])

    def receives(e, kind):
        src = st_in.at[e] if kind == 0 else st_out.at[e]
        out = []
        for i, t in enumerate(targets):
            cols = pl.ds(pl.multiple_of(quarters[i] * hq, 128), hq)
            dst = gin_ref.at[e, :, cols] if kind == 0 else gout_ref.at[e, cols, :]
            out.append(pltpu.make_async_remote_copy(
                src_ref=src, dst_ref=dst, send_sem=send_sem.at[e, kind, i], recv_sem=recv_sem.at[e, kind, i],
                device_id=(t, c), device_id_type=MESH))
        return out

    for e in range(experts):
        acc_in[...] = jnp.zeros_like(acc_in)
        acc_out[...] = jnp.zeros_like(acc_out)
        wi, wo, bias = wi_ref[e], wo_ref[e], b_ref[e]

        def body(i, _):
            ts = pl.ds(pl.multiple_of(i * block, block), block)
            n, co, g = n_ref[ts, :], c_ref[ts, :], g_ref[e:e + 1, ts]
            pre = dot_nt(wi, n) + bias
            dh = dot_nt(wo, co)
            h, slope = gelu_parts(pre)
            acc_out[...] += dot(half(h * g), co)
            acc_in[...] += dot(half(slope * (dh * g)), n)
            return 0

        lax.fori_loop(0, total // block, body, 0)
        st_in[e] = half(acc_in[...].T)
        st_out[e] = half(acc_out[...])
        for kind in range(2):
            out, own = sends(e, kind)
            for copy in out:
                copy.start()
            own.start()
    for e in range(experts):
        for kind in range(2):
            out, own = sends(e, kind)
            own.wait()
            for copy in out:
                copy.wait_send()
            for copy in receives(e, kind):
                copy.wait_recv()


def slice_grads(n_all, c_all, gates_t, wi, wo, bias, block):
    experts, hq, width = wi.shape
    vm = pl.BlockSpec(memory_space=pltpu.VMEM)
    hbm = pl.BlockSpec(memory_space=pl.ANY)
    return pl.pallas_call(
        functools.partial(slice_kernel, block),
        out_shape=(jax.ShapeDtypeStruct((experts, width, 4 * hq), jnp.bfloat16), jax.ShapeDtypeStruct((experts, 4 * hq, width), jnp.bfloat16)),
        in_specs=[vm] * 6,
        out_specs=(hbm, hbm),
        scratch_shapes=[
            pltpu.VMEM((hq, width), jnp.float32),
            pltpu.VMEM((hq, width), jnp.float32),
            pltpu.VMEM((experts, width, hq), jnp.bfloat16),
            pltpu.VMEM((experts, hq, width), jnp.bfloat16),
            pltpu.SemaphoreType.DMA((experts, 2)),
            pltpu.SemaphoreType.DMA((experts, 2, 3)),
            pltpu.SemaphoreType.DMA((experts, 2, 3)),
        ],
        compiler_params=pltpu.CompilerParams(collective_id=1, has_side_effects=True, vmem_limit_bytes=56 << 20),
        name="slice_grads",
    )(n_all, c_all, gates_t, wi, wo, bias)


def swap(v):
    return lax.ppermute(v, "shard", [(0, 1), (1, 0)])


def on_device(
    inputs, norm1_gain, norm1_bias, qkv_weight, query_bias, value_bias, out_weight, out_bias, norm2_gain, norm2_bias,
    router_weight, noise, expert_in, expert_in_bias, expert_out, expert_out_bias, routes, priority, cotangent,
):
    tok_count, width = inputs.shape
    replicas, cores = lax.axis_size("replica"), lax.axis_size("shard")
    shard = lax.axis_index("shard")
    images = tok_count // PATCHES
    heads = width // HEAD_DIM
    owned, _, hidden_count = expert_in.shape
    expert_count = owned * cores
    score_scale = HEAD_DIM ** (-0.5)
    f32 = jnp.float32

    vectors = (norm1_gain, norm1_bias, query_bias, value_bias, out_bias, norm2_gain, norm2_bias)
    packed = jnp.concatenate(
        [qkv_weight, out_weight, jnp.stack(vectors, axis=1), router_weight], axis=1)
    packed = lax.all_gather(packed, "shard", axis=0, tiled=True)
    weight_qkv = packed[:, :3 * width]
    weight_proj = packed[:, 3 * width:4 * width]
    small = packed[:, 4 * width:]
    gain_one, bias_one, bias_query, bias_value, bias_proj, gain_two, bias_two = [
        small[:, i].astype(f32) for i in range(len(vectors))]
    weight_route = small[:, len(vectors):]

    pair_expert = routes.reshape(-1)
    onehot_pairs = (pair_expert[:, None] == jnp.arange(expert_count, dtype=jnp.int32)[None, :]).astype(jnp.int32)
    load = jnp.sum(onehot_pairs, axis=0)
    loads = lax.all_gather(load, ("replica", "shard"))
    position = lax.axis_index("replica") * cores + shard
    ahead = jnp.arange(replicas * cores)[:, None] < position
    offsets = jnp.sum(jnp.where(ahead, loads, 0), axis=0)
    capacity = 2 * tok_count * replicas * cores // expert_count
    chosen = kept_gates(pair_expert, priority.reshape(-1), offsets, capacity, expert_count)

    residual_in = inputs.astype(f32)
    normed_one, norm_one_back = jax.vjp(layer_norm, residual_in, gain_one, bias_one)
    normed_one_half = half(normed_one)
    qkv_bias = jnp.concatenate([bias_query, jnp.zeros_like(bias_query), bias_value])
    mixed = half(dot(normed_one_half, weight_qkv) + qkv_bias)
    shaped = mixed.reshape(images, PATCHES, 3, heads, HEAD_DIM)
    query, keys, values = (shaped[:, :, 0], shaped[:, :, 1], shaped[:, :, 2])
    scores = jnp.einsum("bqhd,bkhd->bhqk", query, keys, preferred_element_type=f32) * score_scale
    row_max = jnp.max(scores, axis=-1, keepdims=True)
    log_total = row_max + jnp.log(jnp.sum(jnp.exp(scores - row_max), axis=-1, keepdims=True))
    context = jnp.einsum(
        "bhqk,bkhd->bqhd", half(jnp.exp(scores - log_total)), values, preferred_element_type=f32)
    context_half = half(context.reshape(tok_count, width))
    middle = residual_in + (dot(context_half, weight_proj) + bias_proj)
    normed_two, norm_two_back = jax.vjp(layer_norm, middle, gain_two, bias_two)
    normed_two_half = half(normed_two)
    logits = dot(normed_two_half, weight_route) + noise
    route_probs = jax.nn.softmax(logits, axis=-1)
    gate_weights = route_probs * chosen
    upstream = cotangent.astype(f32)

    rows = -(-tok_count // 16) * 16
    pad = ((0, rows - tok_count), (0, 0))
    special = replicas == 16 and cores == 2 and images == 1 and hidden_count % 512 == 0
    if special:
        gates_pad = jnp.pad(gate_weights, pad).T
        gates_all = lax.all_gather(gates_pad, ("replica", "shard"), axis=0)
        n_all, c_all = gather_blocks(jnp.pad(normed_two_half, pad), jnp.pad(cotangent, pad), 4)

    pair_n = jnp.concatenate([normed_two_half, swap(normed_two_half)], axis=0)
    pair_c = jnp.concatenate([cotangent, swap(cotangent)], axis=0)
    own_gates = lax.dynamic_slice_in_dim(gate_weights, shard * owned, owned, 1)
    other_gates = swap(lax.dynamic_slice_in_dim(gate_weights, (1 - shard) * owned, owned, 1))
    pair_g = jnp.concatenate([own_gates, other_gates], axis=0)
    pair_up = pair_c.astype(f32)
    running = jnp.zeros((2 * tok_count, width), f32)
    d_rows = jnp.zeros((2 * tok_count, width), f32)
    gate_columns, bias_in_grads, bias_out_grads, in_grads, out_grads = [], [], [], [], []
    for e in range(owned):
        gate = pair_g[:, e:e + 1]
        pre = dot(pair_n, expert_in[e]) + expert_in_bias[e].astype(f32)
        act, slope = gelu_parts(pre)
        hid = half(act)
        result = dot(hid, expert_out[e]) + expert_out_bias[e].astype(f32)
        running = running + gate * result
        gate_columns.append(jnp.sum(pair_up * result, axis=1))
        d_result = half(gate * pair_up)
        d_pre = half(slope * dot_nt(d_result, expert_out[e]))
        d_rows = d_rows + dot_nt(d_pre, expert_in[e])
        bias_in_grads.append(jnp.sum(d_pre.astype(f32), axis=0))
        bias_out_grads.append(jnp.sum(d_result.astype(f32), axis=0))
        if not special:
            in_grads.append(jnp.einsum("td,th->dh", pair_n, d_pre, preferred_element_type=f32))
            out_grads.append(jnp.einsum("th,td->hd", hid, d_result, preferred_element_type=f32))
    d_gate_part = jnp.stack(gate_columns, axis=1)
    running = running[:tok_count] + swap(running[tok_count:])
    d_normed = d_rows[:tok_count] + swap(d_rows[tok_count:])
    d_gate_other = swap(d_gate_part[tok_count:])
    d_gate_own = d_gate_part[:tok_count]
    d_gates = jnp.where(shard == 0, jnp.concatenate([d_gate_own, d_gate_other], axis=1),
                        jnp.concatenate([d_gate_other, d_gate_own], axis=1))

    if special:
        z, y, x, _ = place()
        quarter = hidden_count // 4
        start = (((x + z) % 2) * 2 + (y + z) % 2) * quarter
        wi = lax.dynamic_slice_in_dim(expert_in, start, quarter, 2).swapaxes(1, 2)
        wo = lax.dynamic_slice_in_dim(expert_out, start, quarter, 1)
        bias = lax.dynamic_slice_in_dim(expert_in_bias, start, quarter, 1).astype(f32)[:, :, None]
        gates_t = lax.dynamic_slice_in_dim(gates_all, shard * owned, owned, 1)
        gates_t = gates_t.transpose(1, 0, 2).reshape(owned, -1)
        grad_in, grad_out = slice_grads(
            n_all.reshape(-1, width), c_all.reshape(-1, width), gates_t, wi, wo, bias, 512)
    else:
        grad_in = lax.psum(half(jnp.stack(in_grads, axis=0)), "replica")
        grad_out = lax.psum(half(jnp.stack(out_grads, axis=0)), "replica")

    output = half(middle + running)
    d_probs = d_gates * chosen
    d_logits = half(route_probs * (d_probs - jnp.sum(route_probs * d_probs, axis=-1, keepdims=True)))
    grad_route = jnp.einsum("td,te->de", normed_two_half, d_logits, preferred_element_type=f32)
    d_normed = d_normed + dot_nt(d_logits, weight_route)
    d_middle, grad_gain_two, grad_bias_two = norm_two_back(d_normed)
    d_middle = d_middle + upstream
    d_branch = half(d_middle)
    grad_proj = jnp.einsum("tc,td->cd", context_half, d_branch, preferred_element_type=f32)
    grad_proj_bias = jnp.sum(d_branch.astype(f32), axis=0)
    d_context = half(dot_nt(d_branch, weight_proj)).reshape(images, PATCHES, heads, HEAD_DIM)
    attn_probs = jnp.exp(scores - log_total)
    d_attn = jnp.einsum("bqhd,bkhd->bhqk", d_context, values, preferred_element_type=f32)
    d_values = jnp.einsum("bhqk,bqhd->bkhd", half(attn_probs), d_context, preferred_element_type=f32)
    d_scores = half(attn_probs * (d_attn - jnp.sum(attn_probs * d_attn, axis=-1, keepdims=True)))
    d_query = jnp.einsum("bhqk,bkhd->bqhd", d_scores, keys, preferred_element_type=f32) * score_scale
    d_keys = jnp.einsum("bhqk,bqhd->bkhd", d_scores, query, preferred_element_type=f32) * score_scale
    d_mixed = half(jnp.stack([d_query, d_keys, d_values], axis=2).reshape(tok_count, 3 * width))
    grad_qkv = jnp.einsum("td,tf->df", normed_one_half, d_mixed, preferred_element_type=f32)
    mixed_sums = jnp.sum(d_mixed.astype(f32), axis=0)
    d_normed_one = dot_nt(d_mixed, weight_qkv)
    d_input, grad_gain_one, grad_bias_one = norm_one_back(d_normed_one)
    input_grad = d_input + d_middle

    columns = jnp.stack((grad_gain_one, grad_bias_one, mixed_sums[:width], mixed_sums[2 * width:], grad_proj_bias,
                         grad_gain_two, grad_bias_two), axis=1)
    dense = half(jnp.concatenate([grad_qkv, grad_proj, columns, grad_route], axis=1))
    mine = width // 2
    keep = lax.dynamic_slice_in_dim(dense, shard * mine, mine, 0)
    give = lax.dynamic_slice_in_dim(dense, (1 - shard) * mine, mine, 0)
    dense = keep.astype(f32) + swap(give).astype(f32)
    bias_row = jnp.concatenate(bias_in_grads + bias_out_grads)
    summed, bias_row = lax.psum((half(dense), bias_row), "replica")
    summed = summed.astype(f32)
    columns = [summed[:, 4 * width + i] for i in range(len(vectors))]
    grad_in_bias = bias_row[:owned * hidden_count].reshape(owned, hidden_count)
    grad_out_bias = bias_row[owned * hidden_count:].reshape(owned, width)
    return (
        output, input_grad, columns[0], columns[1], summed[:, :3 * width], columns[2], columns[3],
        summed[:, 3 * width:4 * width], columns[4], columns[5], columns[6], summed[:, 4 * width + len(vectors):],
        grad_in.astype(f32), grad_in_bias, grad_out.astype(f32), grad_out_bias,
    )


def solution(mesh):
    both, split = ("replica", "shard"), "shard"
    return jax.shard_map(
        on_device,
        mesh=mesh,
        in_specs=(
            P(both, None), P(split), P(split), P(split, None), P(split), P(split), P(split, None), P(split), P(split),
            P(split), P(split, None), P(both, None), P(split, None, None), P(split, None), P(split, None, None),
            P(split, None), P(both, None), P(both, None), P(both, None),
        ),
        out_specs=(
            P(both, None), P(both, None), P(split), P(split), P(split, None), P(split), P(split), P(split, None),
            P(split), P(split), P(split), P(split, None), P(split, None, None), P(split, None), P(split, None, None),
            P(split, None),
        ),
        check_vma=False,
    )
```

```python
import functools
from types import SimpleNamespace

import jax
import jax.numpy as jnp
from jax import lax
from jax.experimental import pallas as pl
from jax.experimental.pallas import tpu as pltpu
from jax.sharding import PartitionSpec as P

HEAD_DIM = 64
PATCHES = 197
LN_EPS = 1e-06
MESH = pl.DeviceIdType.MESH
NT = (((1,), (1,)), ((), ()))
GELU_K = 0.7978845608028654
GELU_A = 0.044715
F32 = jnp.float32
BF16 = jnp.bfloat16
ROWS = 256
BLOCK = 208
STEP = 512


def half(values):
    return values.astype(BF16)


def dot(a, b):
    return jnp.dot(a, b, preferred_element_type=F32)


def dot_nt(a, b):
    return lax.dot_general(a, b, NT, preferred_element_type=F32)


def gelu_parts(x):
    x2 = x * x
    q = 0.5 + 0.5 * jnp.tanh(x * (GELU_K + (GELU_K * GELU_A) * x2))
    h = x * q
    return h, q + (h * (1.0 - q)) * (2 * GELU_K + (6 * GELU_K * GELU_A) * x2)


def iota(shape, dim):
    return lax.broadcasted_iota(jnp.int32, shape, dim)


def many(start, size, unit):
    return pl.ds(pl.multiple_of(start, unit), size)


def normalize(v):
    centered = v - jnp.mean(v, axis=-1, keepdims=True)
    spread = lax.rsqrt(jnp.mean(centered * centered, axis=-1, keepdims=True) + LN_EPS)
    return centered * spread, spread


def norm_back(d, xhat, spread, gain):
    dx = d * gain
    return spread * (dx - jnp.mean(dx, axis=-1, keepdims=True) - xhat * jnp.mean(dx * xhat, axis=-1, keepdims=True))


def column_sum(v):
    return jnp.sum(v, axis=0, keepdims=True)


def place():
    r = lax.axis_index("replica")
    return r // 4, (r // 2) % 2, r % 2, lax.axis_index("shard")


def rep(z, y, x):
    return (z * 2 + y) * 2 + x


def as_int(flag):
    return flag.astype(jnp.int32)


class Gather:
    def __init__(self, zs, x_first, rows, sems):
        self.zs, self.x_first, self.rows = zs, x_first, rows
        self.send, self.recv, self.core_send, self.core_recv = sems
        self.z, self.y, self.x, self.c = place()
        z, y, x = self.z, self.y, self.x
        self.me, self.up, self.down = rep(z, y, x), rep(z + 1, y, x), rep(z - 1, y, x)
        near = (rep(z, y, 1 - x), rep(z, 1 - y, x))
        self.first, self.second = near if x_first else near[::-1]

    def side(self, zz):
        return rep(zz, self.y, 1 - self.x) if self.x_first else rep(zz, 1 - self.y, self.x)

    def opposite(self, zz):
        return rep(zz, 1 - self.y, self.x) if self.x_first else rep(zz, self.y, 1 - self.x)

    def ref(self, block, core):
        return self.rows.at[many((block * 2 + core) * BLOCK, BLOCK, 16), :]

    def link(self, kind, block, target):
        ref = self.ref(block, self.c)
        return pltpu.make_async_remote_copy(
            src_ref=ref, dst_ref=ref, send_sem=self.send.at[kind, block], recv_sem=self.recv.at[block],
            device_id=(target, self.c), device_id_type=MESH)

    def across(self, block, core=None):
        ref = self.ref(block, self.c if core is None else core)
        return pltpu.make_async_remote_copy(
            src_ref=ref, dst_ref=ref, send_sem=self.core_send.at[block], recv_sem=self.core_recv.at[block],
            device_id=(self.me, 1 - self.c), device_id_type=MESH)

    def column(self, block):
        self.link(2, block, self.first).start()
        self.link(3, block, self.second).start()
        self.across(block).start()

    def arrived(self, block):
        self.link(0, block, self.up).wait_recv()

    def begin(self):
        pl.when(self.z < self.zs - 1)(lambda: self.link(0, self.me, self.up).start())
        pl.when(self.z > 0)(lambda: self.link(1, self.me, self.down).start())
        self.column(self.me)

    def turn(self, k):
        z, y, x = self.z, self.y, self.x

        @pl.when(z - k >= 0)
        def _():
            block = rep(z - k, y, x)
            self.arrived(block)
            pl.when(z < self.zs - 1)(lambda: self.link(0, block, self.up).start())
            self.column(block)

        @pl.when(z + k < self.zs)
        def _():
            block = rep(z + k, y, x)
            self.arrived(block)
            pl.when(z > 0)(lambda: self.link(1, block, self.down).start())
            self.column(block)

    def side_turn(self, k):
        for d in ((0,) if k == 0 else (-k, k)):
            @pl.when((self.z + d >= 0) & (self.z + d < self.zs))
            def _():
                block = self.side(self.z + d)
                self.arrived(block)
                self.link(3, block, self.second).start()
                self.across(block).start()

    def far(self, zz):
        for block in (self.opposite(zz), rep(zz, 1 - self.y, 1 - self.x)):
            self.arrived(block)
            self.across(block).start()

    def finish_partner(self):
        self.across(self.me, 1 - self.c).wait_recv()

    def finish(self):
        for block in range(4 * self.zs):
            pl.when(block != self.me)(lambda block=block: self.across(block, 1 - self.c).wait_recv())

    def drain(self):
        z, y, x = self.z, self.y, self.x
        for block in range(4 * self.zs):
            self.across(block).wait_send()
        for zz in range(self.zs):
            block = rep(zz, y, x)
            pl.when((z >= zz) & (z < self.zs - 1))(lambda block=block: self.link(0, block, self.up).wait_send())
            pl.when((z <= zz) & (z > 0))(lambda block=block: self.link(1, block, self.down).wait_send())
            self.link(2, block, self.first).wait_send()
            self.link(3, block, self.second).wait_send()
            self.link(3, self.side(zz), self.second).wait_send()


SCRATCH = (
    ("n_all", (None, 512), BF16), ("c_all", (None, 512), BF16), ("g_all", (8, None), F32),
    ("wqkv", (512, 1536), BF16), ("wproj", (512, 512), BF16), ("wroute", (512, 128), BF16), ("vec", (2, 8, 256), F32),
    ("win", (2, 512, 2048), BF16), ("wout", (2, 2048, 512), BF16),
    ("count_out", (6, 8, 128), F32), ("count_in", (4, 8, 128), F32),
    ("xs", (ROWS, 512), F32), ("noise", (ROWS, 128), F32), ("routes", (ROWS, 128), F32),
    ("xhat1", (ROWS, 512), F32), ("n1", (ROWS, 512), BF16), ("mixed", (ROWS, 1536), BF16),
    ("probs", (8, ROWS, ROWS), F32), ("ctx", (ROWS, 512), BF16), ("mid", (ROWS, 512), F32), ("xhat2", (ROWS, 512), F32),
    ("chosen", (ROWS, 128), F32), ("rprobs", (ROWS, 128), F32),
    ("res", (2 * BLOCK, 512), F32), ("running", (2 * BLOCK, 512), F32), ("drows", (2 * BLOCK, 512), F32),
    ("dgate", (2 * BLOCK, 128), F32), ("dres", (2 * BLOCK, 512), BF16), ("gcol", (2 * BLOCK, 128), F32),
    ("got_running", (BLOCK, 512), F32), ("got_drows", (BLOCK, 512), F32), ("got_dgate", (BLOCK, 128), F32),
    ("db", (ROWS, 512), BF16), ("dctx", (ROWS, 512), BF16), ("dmixed", (ROWS, 1536), BF16), ("dn", (ROWS, 512), F32),
    ("dense", (512, 2048), BF16), ("dense_in", (256, 2048), BF16), ("extra", (3, 16, 2048), F32),
    ("total", (272, 2048), BF16), ("final", (272, 2048), BF16), ("part_in", (4, 272, 512), BF16), ("z_out", (4, 272, 256), BF16), ("z_in", (4, 272, 256), BF16),
    ("acc_in", (512, 512), F32), ("acc_out", (512, 512), F32),
    ("st_in", (2, 512, 512), BF16), ("st_out", (2, 512, 512), BF16),
)
SEMS = (
    ("g_send", (2, 4, None)), ("g_recv", (2, None)), ("g_csend", (2, None)), ("g_crecv", (2, None)),
    ("load", (2,)), ("w_send", (4,)), ("w_recv", (4,)), ("count_send", (6,)), ("count_recv", (4,)),
    ("p_send", (3,)), ("p_recv", (3,)), ("d_send", (2,)), ("d_recv", (2,)),
    ("ar_send", (12,)), ("ar_recv", (12,)), ("s_own", (2, 2)), ("s_send", (2, 2, 3)), ("s_recv", (2, 2, 3)),
)
INPUTS = ("x", "cot", "noise_in", "routes_in", "prio", "vec_in", "wqkv_in", "wproj_in", "wroute_in", "win_in", "wout_in",
          "bin", "bout")
OUTPUTS = ("out", "igrad", "gin", "gout", "summed")


def remote(src, dst, send, recv, target):
    return pltpu.make_async_remote_copy(
        src_ref=src, dst_ref=dst, send_sem=send, recv_sem=recv, device_id=target, device_id_type=MESH)


def block_kernel(zs, *refs):
    names = INPUTS + OUTPUTS + tuple(n for n, _, _ in SCRATCH) + tuple(n for n, _ in SEMS)
    r = SimpleNamespace(**dict(zip(names, refs, strict=True)))
    z, y, x, c = place()
    me = rep(z, y, x)
    partner = (me, 1 - c)
    xn, yn = (rep(z, y, 1 - x), c), (rep(z, 1 - y, x), c)
    up, down = (rep(z + 1, y, x), c), (rep(z - 1, y, x), c)
    low_z, high_z = z > 0, z < zs - 1
    tokens = r.x.shape[0]
    devices = 8 * zs
    capacity = 2 * tokens * devices // 4

    bar = pltpu.get_barrier_semaphore()
    pl.when(high_z)(lambda: pl.semaphore_signal(bar, inc=1, device_id=up, device_id_type=MESH))
    pl.when(low_z)(lambda: pl.semaphore_signal(bar, inc=1, device_id=down, device_id_type=MESH))
    for t in (xn, yn, partner):
        pl.semaphore_signal(bar, inc=1, device_id=t, device_id_type=MESH)

    loads = [pltpu.make_async_copy(r.win_in, r.win, r.load.at[0]), pltpu.make_async_copy(r.wout_in, r.wout, r.load.at[1])]
    for copy in loads:
        copy.start()

    r.xs[...] = jnp.zeros_like(r.xs)
    r.xs[0:tokens, :] = r.cot[...].astype(F32)
    own_rows = many((me * 2 + c) * BLOCK, BLOCK, 16)
    r.c_all[own_rows, :] = half(r.xs[0:BLOCK, :])
    mine, other = many(c * 256, 256, 16), many((1 - c) * 256, 256, 16)
    r.wqkv[mine, :] = r.wqkv_in[...]
    r.wproj[mine, :] = r.wproj_in[...]
    r.wroute[mine, :] = r.wroute_in[...]
    r.vec[c] = r.vec_in[...]

    pl.semaphore_wait(bar, 3 + as_int(low_z) + as_int(high_z))

    weights = [remote(ref, ref, r.w_send.at[i], r.w_recv.at[i], partner) for i, ref in enumerate(
        (r.vec.at[c], r.wqkv.at[mine, :], r.wproj.at[mine, :], r.wroute.at[mine, :]))]
    for copy in weights:
        copy.start()
    gathers = [Gather(zs, m == 0, (r.n_all, r.c_all)[m],
                      (r.g_send.at[m], r.g_recv.at[m], r.g_csend.at[m], r.g_crecv.at[m])) for m in range(2)]
    ga, gb = gathers
    gb.begin()

    lane, row = iota((ROWS, 128), 1), iota((ROWS, 128), 0)
    r.routes[...] = jnp.full_like(r.routes, -1.0)
    r.routes[0:tokens, 0:2] = r.routes_in[...].astype(F32)
    experts = [r.routes[:, k:k + 1] for k in range(2)]
    onehot = [jnp.where(lane.astype(F32) == experts[k], 1.0, 0.0) for k in range(2)]
    count = jnp.broadcast_to(column_sum(onehot[0] + onehot[1]), (8, 128))

    def count_copy(i, slot, target):
        return remote(r.count_out.at[i], r.count_in.at[slot], r.count_send.at[i], r.count_recv.at[slot], target)

    r.count_out[0] = count
    count_copy(0, 0, partner).start()

    places = iota((ROWS, r.prio.shape[1]), 1) - 2 * iota((ROWS, r.prio.shape[1]), 0)
    ranks = r.prio[...].astype(F32)
    codes = [experts[k] * 1024.0 + jnp.sum(jnp.where(places == k, ranks, 0.0), axis=1, keepdims=True) for k in range(2)]
    codes = [jnp.where(row[:, 0:1] < tokens, code, -1.0) for code in codes]
    code_rows = jnp.where(lane == 0, codes[0], jnp.where(lane == 1, codes[1], 0.0)).T
    before = []
    for k in range(2):
        floor = experts[k] * 1024.0
        seen = 0.0
        for j in range(2):
            others = code_rows[j:j + 1, :]
            seen = seen + jnp.where((others < codes[k]) & (others >= floor), 1.0, 0.0)
        before.append(jnp.sum(seen, axis=1, keepdims=True))

    count_copy(0, 0, partner).wait_recv()
    ahead = jnp.where(c == 1, 1.0, 0.0) * r.count_in[0]
    count = count + r.count_in[0]
    r.count_out[1] = count
    count_copy(1, 1, xn).start()

    weights[0].wait_send()
    remote(r.vec.at[1 - c], r.vec.at[1 - c], r.w_send.at[0], r.w_recv.at[0], partner).wait_recv()
    vec = jnp.concatenate([r.vec[0], r.vec[1]], axis=1)
    gain1, bias1, bias_q, bias_v, bias_p, gain2, bias2 = [vec[i:i + 1, :] for i in range(7)]
    r.xs[0:tokens, :] = r.x[...].astype(F32)
    xhat, spread1 = normalize(r.xs[...])
    r.xhat1[...] = xhat
    r.n1[...] = half(xhat * gain1 + bias1)

    count_copy(1, 1, xn).wait_recv()
    ahead = ahead + jnp.where(x == 1, 1.0, 0.0) * r.count_in[1]
    count = count + r.count_in[1]
    r.count_out[2] = count
    count_copy(2, 2, yn).start()

    for i, ref in ((1, r.wqkv), (2, r.wproj), (3, r.wroute)):
        weights[i].wait_send()
        ref = ref.at[other, :]
        remote(ref, ref, r.w_send.at[i], r.w_recv.at[i], partner).wait_recv()
    for i, bias in enumerate((bias_q, None, bias_v)):
        part = dot(r.n1[...], r.wqkv[:, 512 * i:512 * (i + 1)])
        r.mixed[:, 512 * i:512 * (i + 1)] = half(part if bias is None else part + bias)

    gb.turn(1)
    gb.side_turn(0)
    count_copy(2, 2, yn).wait_recv()
    ahead = ahead + jnp.where(y == 1, 1.0, 0.0) * r.count_in[2]
    count = count + r.count_in[2]

    low_lane = lane < HEAD_DIM
    key_kept = iota((ROWS, ROWS), 1) < tokens

    def heads_forward(i, _):
        q, k, v = [r.mixed[:, many(base + 128 * i, 128, 128)] for base in (0, 512, 1024)]
        q = q * BF16(HEAD_DIM ** -0.5)
        parts = []
        for h in range(2):
            s = dot_nt(jnp.where(low_lane == (h == 0), q, jnp.zeros_like(q)), k)
            s = jnp.where(key_kept, s, -1e30)
            e = jnp.exp(s - jnp.max(s, axis=-1, keepdims=True))
            p = e / jnp.sum(e, axis=-1, keepdims=True)
            r.probs[2 * i + h] = p
            parts.append(dot(half(p), v))
        r.ctx[:, many(128 * i, 128, 128)] = half(jnp.where(low_lane, parts[0], parts[1]))
        return 0

    lax.fori_loop(0, 4, heads_forward, 0)

    gb.turn(2)
    gb.side_turn(1)

    def pass_up(extra):
        r.count_out[3] = count + extra
        pl.when(high_z)(lambda: count_copy(3, 3, up).start())

    pl.when(z == 0)(lambda: pass_up(0.0))

    @pl.when(low_z)
    def _():
        count_copy(3, 3, up).wait_recv()
        pass_up(r.count_in[3])

    below = jnp.where(low_z, r.count_in[3], 0.0)
    offsets = (ahead + below)[0:1, :]
    chosen = 0.0
    for k in range(2):
        slot = before[k] + jnp.sum(onehot[k] * offsets, axis=1, keepdims=True)
        chosen = chosen + onehot[k] * jnp.where(slot < float(capacity), 1.0, 0.0)
    r.chosen[...] = chosen

    middle = r.xs[...] + (dot(r.ctx[...], r.wproj[...]) + bias_p)
    r.mid[...] = middle
    xhat, spread2 = normalize(middle)
    r.xhat2[...] = xhat
    n2 = half(xhat * gain2 + bias2)
    r.noise[...] = jnp.zeros_like(r.noise)
    r.noise[0:tokens, 0:4] = r.noise_in[...]
    logits = jnp.where(lane < 4, dot(n2, r.wroute[...]) + r.noise[...], -1e30)
    e = jnp.exp(logits - jnp.max(logits, axis=-1, keepdims=True))
    rprobs = e / jnp.sum(e, axis=-1, keepdims=True)
    r.rprobs[...] = rprobs
    gates = rprobs * chosen
    gates_high = half(gates).astype(F32)
    packed = jnp.where(lane < 4, gates_high, pltpu.roll(gates - gates_high, 4, 1)).T
    packed = jnp.concatenate([packed[0:8, :], jnp.zeros((8, 256), F32)], axis=1)
    r.n_all[own_rows, :] = jnp.concatenate([n2[0:192, :], half(jnp.concatenate(
        [n2[192:200, :].astype(F32), packed], axis=0))], axis=0)
    ga.begin()

    gb.turn(3)
    gb.side_turn(2)

    pair = many(me * 2 * BLOCK, 2 * BLOCK, 16)
    gb.finish_partner()
    ga.finish_partner()
    own_gate = [rowwise for rowwise in range(2)]
    for j in range(2):
        g8 = r.n_all[many((me * 2 + j) * BLOCK + 192, 16, 16), 0:256].astype(F32)[8:16, :]
        g8 = g8 + pltpu.roll(g8, 4, 0)
        g8 = jnp.where(c == 0, g8, pltpu.roll(g8, 6, 0))
        r.gcol[j * BLOCK:(j + 1) * BLOCK, :] = jnp.concatenate([g8, jnp.zeros((120, 256), F32)], axis=0).T[0:BLOCK, :]
    for copy in loads:
        copy.wait()
    r.running[...] = jnp.zeros_like(r.running)
    r.drows[...] = jnp.zeros_like(r.drows)
    r.dgate[...] = jnp.zeros_like(r.dgate)
    r.extra[...] = jnp.zeros_like(r.extra)
    pair_lane = iota((2 * BLOCK, 128), 1)
    for e in range(2):
        gate = r.gcol[:, e:e + 1]
        r.res[...] = jnp.zeros_like(r.res)
        d_result = gate * r.c_all[pair, :].astype(F32)
        r.dres[...] = half(d_result)
        r.extra[0, 2 + e:3 + e, 0:512] = column_sum(r.dres[...].astype(F32))

        def hidden_step(j, _, e=e):
            hs = many(j * STEP, STEP, STEP)
            n = r.n_all[pair, :]
            pre = dot(n, r.win[e, :, hs]) + r.bin[e:e + 1, hs].astype(F32)
            hid, slope = gelu_parts(pre)
            r.res[...] += dot(half(hid), r.wout[e, hs, :])
            d_pre = half(slope * dot_nt(r.dres[...], r.wout[e, hs, :]))
            r.extra[0, e:e + 1, hs] = column_sum(d_pre.astype(F32))
            r.drows[...] += dot_nt(d_pre, r.win[e, :, hs])
            return 0

        lax.fori_loop(0, 2, hidden_step, 0)
        if e == 0:
            ga.turn(1)
            ga.side_turn(0)
        else:
            ga.turn(3)
            ga.side_turn(2)
        lax.fori_loop(2, 4, hidden_step, 0)
        if e == 0:
            gb.side_turn(3)
            ga.turn(2)
            ga.side_turn(1)
        else:
            ga.side_turn(3)
        result = r.res[...] + r.bout[e:e + 1, :].astype(F32)
        r.running[...] += gate * result
        d_gate = jnp.sum(r.c_all[pair, :].astype(F32) * result, axis=1, keepdims=True)
        r.dgate[...] = jnp.where(pair_lane == 2 * c + e, d_gate, r.dgate[...])

    theirs, ours = many((1 - c) * BLOCK, BLOCK, 8), many(c * BLOCK, BLOCK, 8)
    partials = [remote(src.at[theirs, :], dst, r.p_send.at[i], r.p_recv.at[i], partner) for i, (src, dst) in enumerate(
        ((r.running, r.got_running), (r.drows, r.got_drows), (r.dgate, r.got_dgate)))]
    for copy in partials:
        copy.start()
    for zz in range(zs):
        gb.far(zz)
    for copy in partials:
        copy.wait()

    r.out[...] = half(r.mid[0:BLOCK, :] + (r.running[ours, :] + r.got_running[...]))[0:tokens, :]
    zeros = jnp.zeros((ROWS - BLOCK, 128), F32)
    d_gates = jnp.concatenate([r.dgate[ours, :] + r.got_dgate[...], zeros], axis=0)
    rprobs, chosen = r.rprobs[...], r.chosen[...]
    d_probs = d_gates * chosen
    d_logits = half(rprobs * (d_probs - jnp.sum(rprobs * d_probs, axis=-1, keepdims=True)))
    r.dn[0:BLOCK, :] = r.drows[ours, :] + r.got_drows[...]
    r.dn[BLOCK:ROWS, :] = jnp.zeros((ROWS - BLOCK, 512), F32)
    dn = r.dn[...] + dot_nt(d_logits, r.wroute[...])
    xhat = r.xhat2[...]
    n2 = half(xhat * gain2 + bias2)
    route_rows = dot(half(d_logits.astype(F32).T), n2)
    vector_rows = {5: column_sum(dn * xhat), 6: column_sum(dn)}
    r.xs[...] = jnp.zeros_like(r.xs)
    r.xs[0:tokens, :] = r.cot[...].astype(F32)
    d_middle = r.xs[...] + norm_back(dn, xhat, spread2, gain2)
    r.mid[...] = d_middle
    r.db[...] = half(d_middle)
    db = r.db[...]
    vector_rows[4] = column_sum(db.astype(F32))
    r.dense[:, 1536:2048] = half(dot(half(r.ctx[...].astype(F32).T), db))
    r.dctx[...] = half(dot_nt(db, r.wproj[...]))

    def heads_back(i, _):
        q, k, v = [r.mixed[:, many(base + 128 * i, 128, 128)] for base in (0, 512, 1024)]
        q = q * BF16(HEAD_DIM ** -0.5)
        do = r.dctx[:, many(128 * i, 128, 128)]
        parts = []
        for h in range(2):
            p = r.probs[2 * i + h]
            dp = dot_nt(jnp.where(low_lane == (h == 0), do, jnp.zeros_like(do)), v)
            ds = p * (dp - jnp.sum(p * dp, axis=-1, keepdims=True))
            parts.append((dot(half(ds), k) * HEAD_DIM ** -0.5, dot(half(ds.T), q), dot(half(p.T), do)))
        for j, base in enumerate((0, 512, 1024)):
            r.dmixed[:, many(base + 128 * i, 128, 128)] = half(jnp.where(low_lane, parts[0][j], parts[1][j]))
        return 0

    lax.fori_loop(0, 4, heads_back, 0)
    n1_t = half(r.n1[...].astype(F32).T)
    dn = 0.0
    for i in range(3):
        part = r.dmixed[:, 512 * i:512 * (i + 1)]
        if i != 1:
            vector_rows[2 + i // 2] = column_sum(part.astype(F32))
        r.dense[:, 512 * i:512 * (i + 1)] = half(dot(n1_t, part))
        dn = dn + dot_nt(part, r.wqkv[:, 512 * i:512 * (i + 1)])
    xhat = r.xhat1[...]
    vector_rows[0] = column_sum(dn * xhat)
    vector_rows[1] = column_sum(dn)
    r.igrad[...] = (r.mid[...] + norm_back(dn, xhat, spread1, gain1))[0:tokens, :]

    vectors = jnp.concatenate([route_rows[0:4, :]] + [vector_rows[i] for i in range(7)] + [jnp.zeros((5, 512), F32)], axis=0)
    r.dn[0:16, :] = vectors
    low_half, high_half = r.dn[0:16, 0:256], r.dn[0:16, 256:512]
    r.extra[1, :, 0:256] = jnp.where(c == 0, high_half, low_half)
    own_half = jnp.where(c == 0, low_half, high_half)
    swaps = [remote(r.dense.at[other, :], r.dense_in, r.d_send.at[0], r.d_recv.at[0], partner),
             remote(r.extra.at[1], r.extra.at[2], r.d_send.at[1], r.d_recv.at[1], partner)]
    for copy in swaps:
        copy.start()
    for zz in range(zs):
        ga.far(zz)
    for copy in swaps:
        copy.wait()
    r.total[0:256, :] = half(r.dense[mine, :].astype(F32) + r.dense_in[...].astype(F32))
    sums = own_half + r.extra[2, :, 0:256]
    small = jnp.concatenate([r.extra[0, 0:4, :], jnp.zeros((12, 2048), F32)], axis=0)
    shifted = jnp.concatenate([jnp.zeros((4, 256), F32), sums[0:12, :]], axis=0)
    r.total[256:272, :] = half(small + jnp.concatenate([shifted, jnp.zeros((16, 1792), F32)], axis=1))

    far_half = (1 - x, 1 - y)
    near_half = (x, y)
    quarter = (x * 2 + y, 4 + y * 2 + x)
    near, next_near = (xn, yn), (yn, xn)

    def cols(j, n):
        return many(j * 256, 256 * n, 256)

    def ar(i, src, dst, target):
        return remote(src, dst, r.ar_send.at[i], r.ar_recv.at[i], target)

    def ar_one(s):
        return ar(s, r.total.at[:, cols(4 * s + 2 * far_half[s], 2)], r.part_in.at[s], near[s])

    def ar_two(s):
        give = 4 * s + 2 * near_half[s] + (1 - near_half[1 - s])
        return ar(2 + s, r.total.at[:, cols(give, 1)], r.part_in.at[2 + s, :, 0:256], next_near[s])

    def ar_up(s):
        return ar(4 + s, r.z_out.at[s], r.z_in.at[s], up)

    def ar_down(s):
        return ar(6 + s, r.z_out.at[2 + s], r.z_in.at[2 + s], down)

    def ar_four(s):
        piece = r.final.at[:, cols(quarter[s], 1)]
        return ar(8 + s, piece, piece, next_near[s])

    def ar_four_got(s):
        piece = r.final.at[:, cols(4 * s + 2 * near_half[s] + (1 - near_half[1 - s]), 1)]
        return ar(8 + s, piece, piece, next_near[s])

    def ar_five(s):
        piece = r.final.at[:, cols(4 * s + 2 * near_half[s], 2)]
        return ar(10 + s, piece, piece, near[s])

    def ar_five_got(s):
        piece = r.final.at[:, cols(4 * s + 2 * far_half[s], 2)]
        return ar(10 + s, piece, piece, near[s])

    def add_into(ref, other_part):
        ref[...] = half(ref[...].astype(F32) + other_part.astype(F32))

    def ar_stage1():
        for s in range(2):
            ar_one(s).start()

    def ar_stage2():
        for s in range(2):
            ar_one(s).wait()
            add_into(r.total.at[:, cols(4 * s + 2 * near_half[s], 2)], r.part_in[s])
            ar_two(s).start()

    def ar_stage3():
        for s in range(2):
            ar_two(s).wait()
            add_into(r.total.at[:, cols(quarter[s], 1)], r.part_in[2 + s, :, 0:256])

            @pl.when(z == 0)
            def _():
                r.z_out[s] = r.total[:, cols(quarter[s], 1)]
                ar_up(s).start()

            @pl.when(z == zs - 1)
            def _():
                r.z_out[2 + s] = r.total[:, cols(quarter[s], 1)]
                ar_down(s).start()

    def ar_stage_z(k):
        for s in range(2):
            @pl.when(z == k)
            def _():
                ar_up(s).wait_recv()
                if k < zs - 1:
                    r.z_out[s] = half(r.total[:, cols(quarter[s], 1)].astype(F32) + r.z_in[s].astype(F32))
                    ar_up(s).start()

            @pl.when(z == zs - 1 - k)
            def _():
                ar_down(s).wait_recv()
                if k < zs - 1:
                    r.z_out[2 + s] = half(r.total[:, cols(quarter[s], 1)].astype(F32) + r.z_in[2 + s].astype(F32))
                    ar_down(s).start()

    def ar_stage4():
        for s in range(2):
            lower = jnp.where(low_z, r.z_in[s].astype(F32), 0.0)
            upper = jnp.where(high_z, r.z_in[2 + s].astype(F32), 0.0)
            own = r.total[:, cols(quarter[s], 1)].astype(F32)
            r.final[:, cols(quarter[s], 1)] = half(own + lower + upper)
            ar_four(s).start()

    def ar_stage5():
        for s in range(2):
            ar_four_got(s).wait_recv()
            ar_five(s).start()

    def ar_stage6():
        for s in range(2):
            ar_five_got(s).wait_recv()
            ar_four(s).wait_send()
            ar_five(s).wait_send()
            pl.when(high_z)(lambda s=s: ar_up(s).wait_send())
            pl.when(low_z)(lambda s=s: ar_down(s).wait_send())

    ar_stage1()
    for g in (gb, ga):
        g.finish()

    r.g_all[...] = jnp.zeros_like(r.g_all)
    for d in range(devices):
        g8 = r.n_all[d * BLOCK + 192:(d + 1) * BLOCK, 0:256].astype(F32)[8:16, :]
        g8 = g8 + pltpu.roll(g8, 4, 0)
        g8 = jnp.where(c == 0, g8, pltpu.roll(g8, 6, 0))
        start, shift = d * BLOCK // 128 * 128, d * BLOCK % 128
        width = min(384, devices * BLOCK - start)
        g8 = jnp.concatenate([g8, jnp.zeros((8, 128), F32)], axis=1)
        if shift:
            g8 = pltpu.roll(g8, shift, 1)
        r.g_all[:, start:start + width] += g8[:, 0:width]

    zn = (jnp.where(z % 2 == 0, rep(z + 1, y, x), rep(z - 1, y, x)), c)
    targets = (xn, yn, zn)
    qx, qy = (x + z) % 2, (y + z) % 2
    quarters = ((1 - qx) * 2 + qy, qx * 2 + 1 - qy, (1 - qx) * 2 + 1 - qy)
    own_quarter = qx * 2 + qy

    def piece(e, kind, q):
        where = many(q * STEP, STEP, STEP)
        return r.gin.at[e, :, where] if kind == 0 else r.gout.at[e, where, :]

    def source(e, kind):
        return (r.st_in if kind == 0 else r.st_out).at[e]

    def give(e, kind, i, q):
        return remote(source(e, kind), piece(e, kind, q), r.s_send.at[e, kind, i], r.s_recv.at[e, kind, i], targets[i])

    ar_stage2()
    hs = many(own_quarter * STEP, STEP, STEP)
    blocks = devices * BLOCK // STEP
    for e in range(2):
        r.acc_in[...] = jnp.zeros_like(r.acc_in)
        r.acc_out[...] = jnp.zeros_like(r.acc_out)
        wi = half(r.win[e, :, hs].astype(F32).T)
        wo = r.wout[e, hs, :]
        bias = jnp.broadcast_to(r.bin[e:e + 1, hs].astype(F32), (128, STEP)).T[:, 0:1]

        def token_step(i, _, e=e, wi=wi, wo=wo, bias=bias):
            ts = many(i * STEP, STEP, STEP)
            n, co, g = r.n_all[ts, :], r.c_all[ts, :], r.g_all[e:e + 1, ts]
            hid, slope = gelu_parts(dot_nt(wi, n) + bias)
            dh = dot_nt(wo, co)
            r.acc_out[...] += dot(half(hid * g), co)
            r.acc_in[...] += dot(half(slope * (dh * g)), n)
            return 0

        lax.fori_loop(0, blocks // 2, token_step, 0)
        if e == 0:
            ar_stage3()
        else:
            ar_stage_z(2)
            ar_stage_z(3)
            ar_stage4()
        lax.fori_loop(blocks // 2, blocks, token_step, 0)
        if e == 0:
            ar_stage_z(1)
        else:
            ar_stage5()
        r.st_in[e] = half(r.acc_in[...].T)
        r.st_out[e] = half(r.acc_out[...])
        for kind in range(2):
            for i in range(3):
                give(e, kind, i, own_quarter).start()
            pltpu.make_async_copy(source(e, kind), piece(e, kind, own_quarter), r.s_own.at[e, kind]).start()

    ar_stage6()
    r.summed[...] = r.final[...].astype(F32)
    for g in (gb, ga):
        g.drain()
    for i in range(3):
        count_copy(i, i, partner).wait_send()
    pl.when(high_z)(lambda: count_copy(3, 3, up).wait_send())
    for e in range(2):
        for kind in range(2):
            pltpu.make_async_copy(source(e, kind), piece(e, kind, own_quarter), r.s_own.at[e, kind]).wait()
            for i in range(3):
                give(e, kind, i, own_quarter).wait_send()
                give(e, kind, i, quarters[i]).wait_recv()


def block_call(zs, *args):
    devices = 8 * zs
    tokens, width = args[0].shape
    flat = devices * BLOCK
    vm, hbm = pl.BlockSpec(memory_space=pltpu.VMEM), pl.BlockSpec(memory_space=pl.ANY)
    shape = jax.ShapeDtypeStruct
    in_specs = [hbm if name in ("win_in", "wout_in") else vm for name in INPUTS]
    scratch = [pltpu.VMEM(tuple(flat if d is None else d for d in dims), dtype) for _, dims, dtype in SCRATCH]
    scratch += [pltpu.SemaphoreType.DMA(tuple(4 * zs if d is None else d for d in dims)) for _, dims in SEMS]
    return pl.pallas_call(
        functools.partial(block_kernel, zs),
        out_shape=(shape((tokens, width), BF16), shape((tokens, width), F32), shape((2, 512, 2048), BF16),
                   shape((2, 2048, 512), BF16), shape((272, 2048), F32)),
        in_specs=in_specs,
        out_specs=(vm, vm, hbm, hbm, vm),
        scratch_shapes=scratch,
        compiler_params=pltpu.CompilerParams(collective_id=0, has_side_effects=True, vmem_limit_bytes=60 << 20),
        name="encoder_block",
    )(*args)


def swap(v):
    return lax.ppermute(v, "shard", [(0, 1), (1, 0)])


def fused(inputs, norm1_gain, norm1_bias, qkv_weight, query_bias, value_bias, out_weight, out_bias, norm2_gain, norm2_bias,
          router_weight, noise, expert_in, expert_in_bias, expert_out, expert_out_bias, routes, priority, cotangent):
    vectors = (norm1_gain, norm1_bias, query_bias, value_bias, out_bias, norm2_gain, norm2_bias)
    vec = jnp.concatenate(vectors + (jnp.zeros_like(norm1_gain),)).astype(F32).reshape(8, -1)
    out, igrad, gin, gout, summed = block_call(
        lax.axis_size("replica") // 4, inputs, cotangent, noise, routes, priority, vec, qkv_weight, out_weight,
        jnp.pad(router_weight, ((0, 0), (0, 124))), expert_in, expert_out, expert_in_bias, expert_out_bias)
    rows = summed[256:272]
    columns = [rows[8 + i, 0:256] for i in range(7)]
    return (
        out, igrad, columns[0], columns[1], summed[0:256, 0:1536], columns[2], columns[3], summed[0:256, 1536:2048],
        columns[4], columns[5], columns[6], rows[4:8, 0:256].T, gin.astype(F32), rows[0:2], gout.astype(F32),
        rows[2:4, 0:512],
    )


def layer_norm(values, gain_vector, bias_vector):
    centered = values - jnp.mean(values, axis=-1, keepdims=True)
    spread = lax.rsqrt(jnp.mean(centered * centered, axis=-1, keepdims=True) + LN_EPS)
    return centered * spread * gain_vector + bias_vector


def kept_gates(pair_expert, ranks, offsets, capacity, expert_count):
    same = pair_expert[:, None] == pair_expert[None, :]
    earlier = ranks[None, :] < ranks[:, None]
    before = jnp.sum(jnp.where(same & earlier, 1, 0).astype(jnp.int32), axis=1)
    onehot = pair_expert[:, None] == jnp.arange(expert_count, dtype=jnp.int32)[None, :]
    first_slot = jnp.sum(jnp.where(onehot, offsets[None, :], 0).astype(jnp.int32), axis=1)
    keep = before + first_slot < capacity
    picked = jnp.where(onehot & keep[:, None], 1.0, 0.0).astype(jnp.float32)
    return jnp.sum(picked.reshape(-1, 2, expert_count), axis=1)


def general(
    inputs, norm1_gain, norm1_bias, qkv_weight, query_bias, value_bias, out_weight, out_bias, norm2_gain, norm2_bias,
    router_weight, noise, expert_in, expert_in_bias, expert_out, expert_out_bias, routes, priority, cotangent,
):
    tok_count, width = inputs.shape
    replicas, cores = lax.axis_size("replica"), lax.axis_size("shard")
    shard = lax.axis_index("shard")
    images = tok_count // PATCHES
    heads = width // HEAD_DIM
    owned, _, hidden_count = expert_in.shape
    expert_count = owned * cores
    score_scale = HEAD_DIM ** (-0.5)
    f32 = jnp.float32

    vectors = (norm1_gain, norm1_bias, query_bias, value_bias, out_bias, norm2_gain, norm2_bias)
    packed = jnp.concatenate(
        [qkv_weight, out_weight, jnp.stack(vectors, axis=1), router_weight], axis=1)
    packed = lax.all_gather(packed, "shard", axis=0, tiled=True)
    weight_qkv = packed[:, :3 * width]
    weight_proj = packed[:, 3 * width:4 * width]
    small = packed[:, 4 * width:]
    gain_one, bias_one, bias_query, bias_value, bias_proj, gain_two, bias_two = [
        small[:, i].astype(f32) for i in range(len(vectors))]
    weight_route = small[:, len(vectors):]

    pair_expert = routes.reshape(-1)
    onehot_pairs = (pair_expert[:, None] == jnp.arange(expert_count, dtype=jnp.int32)[None, :]).astype(jnp.int32)
    load = jnp.sum(onehot_pairs, axis=0)
    loads = lax.all_gather(load, ("replica", "shard"))
    position = lax.axis_index("replica") * cores + shard
    ahead = jnp.arange(replicas * cores)[:, None] < position
    offsets = jnp.sum(jnp.where(ahead, loads, 0), axis=0)
    capacity = 2 * tok_count * replicas * cores // expert_count
    chosen = kept_gates(pair_expert, priority.reshape(-1), offsets, capacity, expert_count)

    residual_in = inputs.astype(f32)
    normed_one, norm_one_back = jax.vjp(layer_norm, residual_in, gain_one, bias_one)
    normed_one_half = half(normed_one)
    qkv_bias = jnp.concatenate([bias_query, jnp.zeros_like(bias_query), bias_value])
    mixed = half(dot(normed_one_half, weight_qkv) + qkv_bias)
    shaped = mixed.reshape(images, PATCHES, 3, heads, HEAD_DIM)
    query, keys, values = (shaped[:, :, 0], shaped[:, :, 1], shaped[:, :, 2])
    scores = jnp.einsum("bqhd,bkhd->bhqk", query, keys, preferred_element_type=f32) * score_scale
    row_max = jnp.max(scores, axis=-1, keepdims=True)
    log_total = row_max + jnp.log(jnp.sum(jnp.exp(scores - row_max), axis=-1, keepdims=True))
    context = jnp.einsum(
        "bhqk,bkhd->bqhd", half(jnp.exp(scores - log_total)), values, preferred_element_type=f32)
    context_half = half(context.reshape(tok_count, width))
    middle = residual_in + (dot(context_half, weight_proj) + bias_proj)
    normed_two, norm_two_back = jax.vjp(layer_norm, middle, gain_two, bias_two)
    normed_two_half = half(normed_two)
    logits = dot(normed_two_half, weight_route) + noise
    route_probs = jax.nn.softmax(logits, axis=-1)
    gate_weights = route_probs * chosen
    upstream = cotangent.astype(f32)

    pair_n = jnp.concatenate([normed_two_half, swap(normed_two_half)], axis=0)
    pair_c = jnp.concatenate([cotangent, swap(cotangent)], axis=0)
    own_gates = lax.dynamic_slice_in_dim(gate_weights, shard * owned, owned, 1)
    other_gates = swap(lax.dynamic_slice_in_dim(gate_weights, (1 - shard) * owned, owned, 1))
    pair_g = jnp.concatenate([own_gates, other_gates], axis=0)
    pair_up = pair_c.astype(f32)
    running = jnp.zeros((2 * tok_count, width), f32)
    d_rows = jnp.zeros((2 * tok_count, width), f32)
    gate_columns, bias_in_grads, bias_out_grads, in_grads, out_grads = [], [], [], [], []
    for e in range(owned):
        gate = pair_g[:, e:e + 1]
        pre = dot(pair_n, expert_in[e]) + expert_in_bias[e].astype(f32)
        act, slope = gelu_parts(pre)
        hid = half(act)
        result = dot(hid, expert_out[e]) + expert_out_bias[e].astype(f32)
        running = running + gate * result
        gate_columns.append(jnp.sum(pair_up * result, axis=1))
        d_result = half(gate * pair_up)
        d_pre = half(slope * dot_nt(d_result, expert_out[e]))
        d_rows = d_rows + dot_nt(d_pre, expert_in[e])
        bias_in_grads.append(jnp.sum(d_pre.astype(f32), axis=0))
        bias_out_grads.append(jnp.sum(d_result.astype(f32), axis=0))
        in_grads.append(jnp.einsum("td,th->dh", pair_n, d_pre, preferred_element_type=f32))
        out_grads.append(jnp.einsum("th,td->hd", hid, d_result, preferred_element_type=f32))
    d_gate_part = jnp.stack(gate_columns, axis=1)
    running = running[:tok_count] + swap(running[tok_count:])
    d_normed = d_rows[:tok_count] + swap(d_rows[tok_count:])
    d_gate_other = swap(d_gate_part[tok_count:])
    d_gate_own = d_gate_part[:tok_count]
    d_gates = jnp.where(shard == 0, jnp.concatenate([d_gate_own, d_gate_other], axis=1),
                        jnp.concatenate([d_gate_other, d_gate_own], axis=1))

    grad_in = lax.psum(half(jnp.stack(in_grads, axis=0)), "replica")
    grad_out = lax.psum(half(jnp.stack(out_grads, axis=0)), "replica")

    output = half(middle + running)
    d_probs = d_gates * chosen
    d_logits = half(route_probs * (d_probs - jnp.sum(route_probs * d_probs, axis=-1, keepdims=True)))
    grad_route = jnp.einsum("td,te->de", normed_two_half, d_logits, preferred_element_type=f32)
    d_normed = d_normed + dot_nt(d_logits, weight_route)
    d_middle, grad_gain_two, grad_bias_two = norm_two_back(d_normed)
    d_middle = d_middle + upstream
    d_branch = half(d_middle)
    grad_proj = jnp.einsum("tc,td->cd", context_half, d_branch, preferred_element_type=f32)
    grad_proj_bias = jnp.sum(d_branch.astype(f32), axis=0)
    d_context = half(dot_nt(d_branch, weight_proj)).reshape(images, PATCHES, heads, HEAD_DIM)
    attn_probs = jnp.exp(scores - log_total)
    d_attn = jnp.einsum("bqhd,bkhd->bhqk", d_context, values, preferred_element_type=f32)
    d_values = jnp.einsum("bhqk,bqhd->bkhd", half(attn_probs), d_context, preferred_element_type=f32)
    d_scores = half(attn_probs * (d_attn - jnp.sum(attn_probs * d_attn, axis=-1, keepdims=True)))
    d_query = jnp.einsum("bhqk,bkhd->bqhd", d_scores, keys, preferred_element_type=f32) * score_scale
    d_keys = jnp.einsum("bhqk,bqhd->bkhd", d_scores, query, preferred_element_type=f32) * score_scale
    d_mixed = half(jnp.stack([d_query, d_keys, d_values], axis=2).reshape(tok_count, 3 * width))
    grad_qkv = jnp.einsum("td,tf->df", normed_one_half, d_mixed, preferred_element_type=f32)
    mixed_sums = jnp.sum(d_mixed.astype(f32), axis=0)
    d_normed_one = dot_nt(d_mixed, weight_qkv)
    d_input, grad_gain_one, grad_bias_one = norm_one_back(d_normed_one)
    input_grad = d_input + d_middle

    columns = jnp.stack((grad_gain_one, grad_bias_one, mixed_sums[:width], mixed_sums[2 * width:], grad_proj_bias,
                         grad_gain_two, grad_bias_two), axis=1)
    dense = half(jnp.concatenate([grad_qkv, grad_proj, columns, grad_route], axis=1))
    mine = width // 2
    keep = lax.dynamic_slice_in_dim(dense, shard * mine, mine, 0)
    give = lax.dynamic_slice_in_dim(dense, (1 - shard) * mine, mine, 0)
    dense = keep.astype(f32) + swap(give).astype(f32)
    bias_row = jnp.concatenate(bias_in_grads + bias_out_grads)
    summed, bias_row = lax.psum((half(dense), bias_row), "replica")
    summed = summed.astype(f32)
    columns = [summed[:, 4 * width + i] for i in range(len(vectors))]
    grad_in_bias = bias_row[:owned * hidden_count].reshape(owned, hidden_count)
    grad_out_bias = bias_row[owned * hidden_count:].reshape(owned, width)
    return (
        output, input_grad, columns[0], columns[1], summed[:, :3 * width], columns[2], columns[3],
        summed[:, 3 * width:4 * width], columns[4], columns[5], columns[6], summed[:, 4 * width + len(vectors):],
        grad_in.astype(f32), grad_in_bias, grad_out.astype(f32), grad_out_bias,
    )


def on_device(*args):
    expert_in, inputs = args[12], args[0]
    planes = lax.axis_size("replica") == 16 and lax.axis_size("shard") == 2
    if planes and inputs.shape == (PATCHES, 512) and expert_in.shape == (2, 512, 2048):
        return fused(*args)
    return general(*args)


def solution(mesh):
    both, split = ("replica", "shard"), "shard"
    return jax.shard_map(
        on_device,
        mesh=mesh,
        in_specs=(
            P(both, None), P(split), P(split), P(split, None), P(split), P(split), P(split, None), P(split), P(split),
            P(split), P(split, None), P(both, None), P(split, None, None), P(split, None), P(split, None, None),
            P(split, None), P(both, None), P(both, None), P(both, None),
        ),
        out_specs=(
            P(both, None), P(both, None), P(split), P(split), P(split, None), P(split), P(split), P(split, None),
            P(split), P(split), P(split), P(split, None), P(split, None, None), P(split, None), P(split, None, None),
            P(split, None),
        ),
        check_vma=False,
    )
```

```python
import functools
from types import SimpleNamespace

import jax
import jax.numpy as jnp
from jax import lax
from jax.experimental import pallas as pl
from jax.experimental.pallas import tpu as pltpu
from jax.sharding import PartitionSpec as P

HEAD_DIM = 64
PATCHES = 197
LN_EPS = 1e-06
MESH = pl.DeviceIdType.MESH
NT = (((1,), (1,)), ((), ()))
GELU_K = 0.7978845608028654
GELU_A = 0.044715
F32 = jnp.float32
BF16 = jnp.bfloat16
ROWS = 256
BLOCK = 208
STEP = 512
SLICE = 256
PIECE = 64
STEPS = 6
PIECES = STEPS * 2 * SLICE // PIECE
SETS = 2 * 2 * SLICE // PIECE
HOP = 3
TICKS = 3
PASS = 8


def half(values):
    return values.astype(BF16)


def dot(a, b):
    return jnp.dot(a, b, preferred_element_type=F32)


def dot_nt(a, b):
    return lax.dot_general(a, b, NT, preferred_element_type=F32)


def gelu_parts(x):
    x2 = x * x
    q = 0.5 + 0.5 * jnp.tanh(x * (GELU_K + (GELU_K * GELU_A) * x2))
    h = x * q
    return h, q + (h * (1.0 - q)) * (2 * GELU_K + (6 * GELU_K * GELU_A) * x2)


def iota(shape, dim):
    return lax.broadcasted_iota(jnp.int32, shape, dim)


def many(start, size, unit):
    return pl.ds(pl.multiple_of(start, unit), size)


def normalize(v):
    centered = v - jnp.mean(v, axis=-1, keepdims=True)
    spread = lax.rsqrt(jnp.mean(centered * centered, axis=-1, keepdims=True) + LN_EPS)
    return centered * spread, spread


def norm_back(d, xhat, spread, gain):
    dx = d * gain
    return spread * (dx - jnp.mean(dx, axis=-1, keepdims=True) - xhat * jnp.mean(dx * xhat, axis=-1, keepdims=True))


def column_sum(v):
    return jnp.sum(v, axis=0, keepdims=True)


def place():
    r = lax.axis_index("replica")
    return r // 4, (r // 2) % 2, r % 2, lax.axis_index("shard")


def rep(z, y, x):
    return (z * 2 + y) * 2 + x


class PlaneGather:
    def __init__(self, x_first, rows, sems):
        self.rows = rows
        self.send, self.recv, self.core_send, self.core_recv = sems
        z, y, x, c = place()
        near = ((rep(z, y, 1 - x), c), (rep(z, 1 - y, x), c))
        spots = (y * 2 + 1 - x, (1 - y) * 2 + x)
        self.targets = near if x_first else near[::-1]
        self.first, self.second = spots if x_first else spots[::-1]
        self.me, self.diagonal = y * 2 + x, (1 - y) * 2 + 1 - x
        self.core, self.partner = c, (rep(z, y, x), 1 - c)

    def ref(self, spot, core):
        return self.rows.at[many((spot * 2 + core) * BLOCK, BLOCK, 16), :]

    def link(self, kind, spot):
        ref = self.ref(spot, self.core)
        return remote(ref, ref, self.send.at[kind, spot], self.recv.at[spot], self.targets[kind])

    def across(self, spot, core=None):
        ref = self.ref(spot, self.core if core is None else core)
        return remote(ref, ref, self.core_send.at[spot], self.core_recv.at[spot], self.partner)

    def begin(self):
        self.link(0, self.me).start()
        self.link(1, self.me).start()
        self.across(self.me).start()

    def turn(self):
        self.link(0, self.first).wait_recv()
        self.link(1, self.first).start()
        self.across(self.first).start()

    def far(self):
        for spot in (self.second, self.diagonal):
            self.link(0, spot).wait_recv()
            self.across(spot).start()

    def from_core(self, spot):
        self.across(spot, 1 - self.core).wait_recv()

    def drain(self):
        for kind, spot in ((0, self.me), (1, self.me), (1, self.first)):
            self.link(kind, spot).wait_send()
        for spot in range(4):
            self.across(spot).wait_send()


SCRATCH = (
    ("n_all", (8 * BLOCK, 512), BF16), ("c_all", (8 * BLOCK, 512), BF16), ("g_all", (8, 8 * BLOCK), F32),
    ("wqkv", (512, 1536), BF16), ("wproj", (512, 512), BF16), ("vec", (2, 16, 256), F32), ("binf", (2, 2048), F32),
    ("win", (2, 512, 2048), BF16), ("wout", (2, 2048, 512), BF16),
    ("count_out", (3, 8, 128), F32), ("count_in", (9, 8, 128), F32),
    ("xs", (ROWS, 512), F32), ("pairs", (16, ROWS), F32),
    ("xhat1", (ROWS, 512), F32), ("n1", (ROWS, 512), BF16), ("mixed", (ROWS, 1536), BF16),
    ("probs", (8, ROWS, ROWS), F32), ("ctx", (ROWS, 512), BF16), ("mid", (ROWS, 512), F32), ("xhat2", (ROWS, 512), F32),
    ("chosen", (ROWS, 128), F32), ("rprobs", (ROWS, 128), F32),
    ("res", (2 * BLOCK, 512), F32), ("running", (2 * BLOCK, 512), F32), ("drows", (2 * BLOCK, 512), F32),
    ("dgate", (2 * BLOCK, 128), F32), ("dres", (2 * BLOCK, 512), BF16), ("gcol", (2 * BLOCK, 128), F32),
    ("got_running", (BLOCK, 512), F32), ("got_drows", (BLOCK, 512), F32), ("got_dgate", (BLOCK, 128), F32),
    ("db", (ROWS, 512), BF16), ("dctx", (ROWS, 512), BF16), ("dmixed", (ROWS, 1536), BF16), ("dn", (ROWS, 512), F32),
    ("dense", (512, 2048), BF16), ("dense_in", (256, 2048), BF16), ("extra", (3, 16, 2048), F32),
    ("total", (272, 2048), BF16), ("part_in", (4, 272, 512), BF16), ("z_out", (4, 272, 256), BF16), ("z_in", (4, 272, 256), BF16),
    ("own", (PIECES, PIECE, 512), BF16), ("up_in", (PIECES, PIECE, 512), BF16), ("up_out", (PIECES, PIECE, 512), BF16),
    ("down_in", (PIECES, PIECE, 512), BF16), ("down_out", (PIECES, PIECE, 512), BF16), ("fin", (PIECES, PIECE, 512), BF16),
)
SEMS = (
    ("g_send", (2, 2, 4)), ("g_recv", (2, 4)), ("g_csend", (2, 4)), ("g_crecv", (2, 4)),
    ("load", (2,)), ("w_send", (3,)), ("w_recv", (3,)), ("count_send", (7,)), ("count_recv", (9,)),
    ("p_send", (3,)), ("p_recv", (3,)), ("d_send", (2,)), ("d_recv", (2,)),
    ("ar_send", (12,)), ("ar_recv", (12,)), ("up_recv", (PIECES,)), ("down_recv", (PIECES,)), ("bulk", (9,)),
    ("x_recv", (SETS,)), ("y_recv", (SETS,)),
)
INPUTS = ("x", "cot", "noise_in", "routes_in", "prio", "v0", "v1", "v2", "v3", "v4", "v5", "v6", "route_in", "wqkv_in",
          "wproj_in", "win_in", "wout_in", "bin", "bout")
OUTPUTS = ("out", "igrad", "grads", "final")


def remote(src, dst, send, recv, target):
    return pltpu.make_async_remote_copy(
        src_ref=src, dst_ref=dst, send_sem=send, recv_sem=recv, device_id=target, device_id_type=MESH)


def block_kernel(zs, *refs):
    names = INPUTS + OUTPUTS + tuple(n for n, _, _ in SCRATCH) + tuple(n for n, _ in SEMS)
    r = SimpleNamespace(**dict(zip(names, refs, strict=True)))
    z, y, x, c = place()
    me = rep(z, y, x)
    partner = (me, 1 - c)
    xn, yn = (rep(z, y, 1 - x), c), (rep(z, 1 - y, x), c)
    up, down = (rep(z + 1, y, x), c), (rep(z - 1, y, x), c)
    low_z, high_z = z > 0, z < zs - 1
    tokens = r.x.shape[0]
    devices = 8 * zs
    capacity = 2 * tokens * devices // 4

    bar = pltpu.get_barrier_semaphore()
    for d in range(1, zs):
        peer = (rep(lax.rem(z + d, zs), y, x), c)
        pl.semaphore_signal(bar, inc=1, device_id=peer, device_id_type=MESH)
    for peer in (xn, yn, (rep(z, 1 - y, 1 - x), c), partner):
        pl.semaphore_signal(bar, inc=1, device_id=peer, device_id_type=MESH)

    loads = [pltpu.make_async_copy(r.win_in, r.win, r.load.at[0]), pltpu.make_async_copy(r.wout_in, r.wout, r.load.at[1])]
    for copy in loads:
        copy.start()

    r.xs[...] = jnp.zeros_like(r.xs)
    r.xs[0:tokens, :] = r.cot[...].astype(F32)
    own_rows = many(((y * 2 + x) * 2 + c) * BLOCK, BLOCK, 16)
    r.c_all[own_rows, :] = half(r.xs[0:BLOCK, :])
    mine, other = many(c * 256, 256, 16), many((1 - c) * 256, 256, 16)
    r.wqkv[mine, :] = r.wqkv_in[...]
    r.wproj[mine, :] = r.wproj_in[...]
    rows = [ref[...].astype(F32).reshape(1, 256) for ref in (r.v0, r.v1, r.v2, r.v3, r.v4, r.v5, r.v6)]
    rows += [jnp.zeros((1, 256), F32), r.route_in[...].astype(F32), jnp.zeros((4, 256), F32)]
    r.vec[c] = jnp.concatenate(rows, axis=0)
    r.binf[...] = r.bin[...].astype(F32)

    pl.semaphore_wait(bar, zs + 3)

    weights = [remote(ref, ref, r.w_send.at[i], r.w_recv.at[i], partner) for i, ref in enumerate(
        (r.vec.at[c], r.wqkv.at[mine, :], r.wproj.at[mine, :]))]
    for copy in weights:
        copy.start()
    gathers = [PlaneGather(m == 0, (r.n_all, r.c_all)[m],
                           (r.g_send.at[m], r.g_recv.at[m], r.g_csend.at[m], r.g_crecv.at[m])) for m in range(2)]
    ga, gb = gathers
    gb.begin()

    lane, row = iota((ROWS, 128), 1), iota((ROWS, 128), 0)
    r.pairs[0:8, :] = jnp.full((8, ROWS), -1.0, F32)
    r.pairs[8:16, :] = jnp.zeros((8, ROWS), F32)
    r.pairs[0:2, 0:tokens] = r.routes_in[...].astype(F32)
    r.pairs[8:12, 0:tokens] = r.noise_in[...]
    by_token = jnp.concatenate([r.pairs[...], jnp.zeros((112, ROWS), F32)], axis=0).T
    experts = [by_token[:, k:k + 1] for k in range(2)]
    noise = pltpu.roll(by_token, 120, 1)
    onehot = [jnp.where(lane.astype(F32) == experts[k], 1.0, 0.0) for k in range(2)]
    count = jnp.broadcast_to(column_sum(onehot[0] + onehot[1]), (8, 128))

    def count_copy(stage, i, slot, target):
        return remote(r.count_out.at[stage], r.count_in.at[slot], r.count_send.at[i], r.count_recv.at[slot], target)

    spot = y * 2 + x
    column = [(rep(k, y, x), c) for k in range(zs)]

    def counts_to_plane():
        for d in range(1, 4):
            q = lax.rem(spot + d, 4)
            count_copy(1, d, 1 + spot, (rep(z, q // 2, lax.rem(q, 2)), c)).start()

    def counts_up():
        for k in range(1, zs):
            pl.when(z < k)(lambda k=k: count_copy(2, 3 + k, 5 + z, column[k]).start())

    r.count_out[0] = count
    count_copy(0, 0, 0, partner).start()

    places = iota((ROWS, r.prio.shape[1]), 1) - 2 * iota((ROWS, r.prio.shape[1]), 0)
    ranks = r.prio[...].astype(F32)
    codes = [experts[k] * 1024.0 + jnp.sum(jnp.where(places == k, ranks, 0.0), axis=1, keepdims=True) for k in range(2)]
    codes = [jnp.where(row[:, 0:1] < tokens, code, -1.0) for code in codes]
    code_rows = jnp.where(lane == 0, codes[0], jnp.where(lane == 1, codes[1], 0.0)).T
    before = []
    for k in range(2):
        floor = experts[k] * 1024.0
        seen = 0.0
        for j in range(2):
            others = code_rows[j:j + 1, :]
            seen = seen + jnp.where((others < codes[k]) & (others >= floor), 1.0, 0.0)
        before.append(jnp.sum(seen, axis=1, keepdims=True))

    count_copy(0, 0, 0, partner).wait_recv()
    ahead = jnp.where(c == 1, 1.0, 0.0) * r.count_in[0]
    count = count + r.count_in[0]
    r.count_out[1] = count
    counts_to_plane()

    weights[0].wait_send()
    remote(r.vec.at[1 - c], r.vec.at[1 - c], r.w_send.at[0], r.w_recv.at[0], partner).wait_recv()
    vec = jnp.concatenate([r.vec[0], r.vec[1]], axis=1)
    gain1, bias1, bias_q, bias_v, bias_p, gain2, bias2 = [vec[i:i + 1, :] for i in range(7)]
    route_rows = jnp.concatenate([vec[8:16, :], jnp.zeros((120, 512), F32)], axis=0)
    route_t, route = half(route_rows), half(route_rows.T)
    r.xs[0:tokens, :] = r.x[...].astype(F32)
    xhat, spread1 = normalize(r.xs[...])
    r.xhat1[...] = xhat
    r.n1[...] = half(xhat * gain1 + bias1)

    for q in range(4):
        pl.when(spot != q)(lambda q=q: count_copy(1, 1, 1 + q, partner).wait_recv())
    for q in range(4):
        ahead = ahead + jnp.where(spot > q, r.count_in[1 + q], 0.0)
        count = count + jnp.where(spot != q, r.count_in[1 + q], 0.0)
    r.count_out[2] = count
    counts_up()

    for i, ref in ((1, r.wqkv), (2, r.wproj)):
        weights[i].wait_send()
        ref = ref.at[other, :]
        remote(ref, ref, r.w_send.at[i], r.w_recv.at[i], partner).wait_recv()
    for i, bias in enumerate((bias_q, None, bias_v)):
        part = dot(r.n1[...], r.wqkv[:, 512 * i:512 * (i + 1)])
        r.mixed[:, 512 * i:512 * (i + 1)] = half(part if bias is None else part + bias)

    low_lane = lane < HEAD_DIM
    key_kept = iota((ROWS, ROWS), 1) < tokens

    def heads_forward(i, _):
        q, k, v = [r.mixed[:, many(base + 128 * i, 128, 128)] for base in (0, 512, 1024)]
        q = q * BF16(HEAD_DIM ** -0.5)
        parts = []
        for h in range(2):
            s = dot_nt(jnp.where(low_lane == (h == 0), q, jnp.zeros_like(q)), k)
            s = jnp.where(key_kept, s, -1e30)
            e = jnp.exp(s - jnp.max(s, axis=-1, keepdims=True))
            p = e / jnp.sum(e, axis=-1, keepdims=True)
            r.probs[2 * i + h] = p
            parts.append(dot(half(p), v))
        r.ctx[:, many(128 * i, 128, 128)] = half(jnp.where(low_lane, parts[0], parts[1]))
        return 0

    lax.fori_loop(0, 4, heads_forward, 0)

    gb.turn()

    for k in range(zs - 1):
        pl.when(z > k)(lambda k=k: count_copy(2, 4, 5 + k, partner).wait_recv())
    for k in range(zs - 1):
        ahead = ahead + jnp.where(z > k, r.count_in[5 + k], 0.0)
    offsets = ahead[0:1, :]
    chosen = 0.0
    for k in range(2):
        slot = before[k] + jnp.sum(onehot[k] * offsets, axis=1, keepdims=True)
        chosen = chosen + onehot[k] * jnp.where(slot < float(capacity), 1.0, 0.0)
    r.chosen[...] = chosen

    middle = r.xs[...] + (dot(r.ctx[...], r.wproj[...]) + bias_p)
    r.mid[...] = middle
    xhat, spread2 = normalize(middle)
    r.xhat2[...] = xhat
    n2 = half(xhat * gain2 + bias2)
    logits = jnp.where(lane < 4, dot(n2, route) + noise, -1e30)
    e = jnp.exp(logits - jnp.max(logits, axis=-1, keepdims=True))
    rprobs = e / jnp.sum(e, axis=-1, keepdims=True)
    r.rprobs[...] = rprobs
    gates = rprobs * chosen
    gates_high = half(gates).astype(F32)
    packed = jnp.where(lane < 4, gates_high, pltpu.roll(gates - gates_high, 4, 1)).T
    packed = jnp.concatenate([packed[0:8, :], jnp.zeros((8, 256), F32)], axis=1)
    r.n_all[own_rows, :] = jnp.concatenate([n2[0:192, :], half(jnp.concatenate(
        [n2[192:200, :].astype(F32), packed], axis=0))], axis=0)
    ga.begin()
    gb.far()

    pair = many(spot * 2 * BLOCK, 2 * BLOCK, 16)
    for g in gathers:
        g.from_core(spot)
    for j in range(2):
        g8 = r.n_all[many((spot * 2 + j) * BLOCK + 192, 16, 16), 0:256].astype(F32)[8:16, :]
        g8 = g8 + pltpu.roll(g8, 4, 0)
        g8 = jnp.where(c == 0, g8, pltpu.roll(g8, 6, 0))
        r.gcol[j * BLOCK:(j + 1) * BLOCK, :] = jnp.concatenate([g8, jnp.zeros((120, 256), F32)], axis=0).T[0:BLOCK, :]
    for copy in loads:
        copy.wait()
    r.running[...] = jnp.zeros_like(r.running)
    r.drows[...] = jnp.zeros_like(r.drows)
    r.dgate[...] = jnp.zeros_like(r.dgate)
    r.extra[...] = jnp.zeros_like(r.extra)
    pair_lane = iota((2 * BLOCK, 128), 1)
    for e in range(2):
        gate = r.gcol[:, e:e + 1]
        r.res[...] = jnp.zeros_like(r.res)
        d_result = gate * r.c_all[pair, :].astype(F32)
        r.dres[...] = half(d_result)
        r.extra[0, 2 + e:3 + e, 0:512] = column_sum(r.dres[...].astype(F32))

        def hidden_step(j, _, e=e):
            hs = many(j * STEP, STEP, STEP)
            n = r.n_all[pair, :]
            pre = dot(n, r.win[e, :, hs]) + r.bin[e:e + 1, hs].astype(F32)
            hid, slope = gelu_parts(pre)
            r.res[...] += dot(half(hid), r.wout[e, hs, :])
            d_pre = half(slope * dot_nt(r.dres[...], r.wout[e, hs, :]))
            r.extra[0, e:e + 1, hs] = column_sum(d_pre.astype(F32))
            r.drows[...] += dot_nt(d_pre, r.win[e, :, hs])
            return 0

        lax.fori_loop(0, 2, hidden_step, 0)
        if e == 0:
            ga.turn()
        lax.fori_loop(2, 4, hidden_step, 0)
        if e == 0:
            ga.far()
        result = r.res[...] + r.bout[e:e + 1, :].astype(F32)
        r.running[...] += gate * result
        d_gate = jnp.sum(r.c_all[pair, :].astype(F32) * result, axis=1, keepdims=True)
        r.dgate[...] = jnp.where(pair_lane == 2 * c + e, d_gate, r.dgate[...])

    theirs, ours = many((1 - c) * BLOCK, BLOCK, 8), many(c * BLOCK, BLOCK, 8)
    partials = [remote(src.at[theirs, :], dst, r.p_send.at[i], r.p_recv.at[i], partner) for i, (src, dst) in enumerate(
        ((r.running, r.got_running), (r.drows, r.got_drows), (r.dgate, r.got_dgate)))]
    for copy in partials:
        copy.start()

    for g in gathers:
        for other_spot in (g.first, g.second, g.diagonal):
            g.from_core(other_spot)
    span = 8 * BLOCK
    row = jnp.zeros((8, span), F32)
    for d in range(8):
        g8 = r.n_all[d * BLOCK + 192:(d + 1) * BLOCK, 0:256].astype(F32)[8:16, :]
        g8 = g8 + pltpu.roll(g8, 4, 0)
        g8 = jnp.where(c == 0, g8, pltpu.roll(g8, 6, 0))
        at, shift = d * BLOCK // 128 * 128, d * BLOCK % 128
        width = min(384, span - at)
        g8 = jnp.concatenate([g8, jnp.zeros((8, 128), F32)], axis=1)
        g8 = pltpu.roll(g8, shift, 1) if shift else g8
        pieces = [jnp.zeros((8, at), F32)] if at else []
        pieces += [g8[:, 0:width]] + ([jnp.zeros((8, span - at - width), F32)] if span > at + width else [])
        row = row + jnp.concatenate(pieces, axis=1)
    r.g_all[...] = row

    slot = lax.rem(x + y, 2)

    def where_from(f, slice_of, x_of):
        s, i, kind = f // 8, lax.rem(f, 8) // 2, lax.rem(f, 2)
        t = jnp.maximum(s - 2, 0)
        e = jnp.where(s < 2, s, t // 2)
        start = slice_of * 1024 + jnp.where(s < 2, 512 + x_of * SLICE, lax.rem(t, 2) * SLICE)
        return e, start, i, kind

    def landing(f, slice_of=slot, x_of=x):
        e, start, i, kind = where_from(f, slice_of, x_of)
        return r.grads.at[kind * 2 + e, many(start + i * PIECE, PIECE, PIECE), :]

    def up_copy(src, f):
        return remote(src, r.up_in.at[f], r.bulk.at[0], r.up_recv.at[f], up)

    def down_copy(src, f):
        return remote(src, r.down_in.at[f], r.bulk.at[1], r.down_recv.at[f], down)

    def keep_copy(f):
        return pltpu.make_async_copy(r.fin.at[f], landing(f), r.bulk.at[2])

    def give_x(f, recv, ref=None):
        return remote(r.fin.at[f], landing(f) if ref is None else ref, r.bulk.at[3], recv, xn)

    def give_y(f, recv, ref=None):
        return remote(r.fin.at[f], landing(f) if ref is None else ref, r.bulk.at[4], recv, yn)

    def pass_x(f):
        ref = landing(f, 1 - slot, x)
        return remote(ref, ref, r.bulk.at[5], r.bulk.at[7], xn)

    def pass_y(f):
        ref = landing(f, 1 - slot, 1 - x)
        return remote(ref, ref, r.bulk.at[6], r.bulk.at[8], yn)

    def goes(f):
        late = lax.rem(f // 8, 2)
        return (f < SETS) | (late == 0), (f < SETS) | (late == 1), lax.rem(f, 8) < 4

    def inside(f, count=PIECES):
        return (f >= 0) & (f < count)

    def tick(t):
        u, d, f, w = t - HOP * z, t - HOP * (zs - 1 - z), t - HOP * (zs - 1), t - HOP * (zs - 1) - PASS

        @pl.when(inside(u))
        def _():
            pl.when(z == 0)(lambda: up_copy(r.own.at[u], u).start())

            @pl.when(low_z)
            def _():
                up_copy(r.up_out.at[u], u).wait_recv()

                @pl.when(high_z)
                def _():
                    r.up_out[u] = half(r.own[u].astype(F32) + r.up_in[u].astype(F32))
                    up_copy(r.up_out.at[u], u).start()

        @pl.when(inside(d))
        def _():
            pl.when(z == zs - 1)(lambda: down_copy(r.own.at[d], d).start())

            @pl.when(high_z)
            def _():
                down_copy(r.down_out.at[d], d).wait_recv()

                @pl.when(low_z)
                def _():
                    r.down_out[d] = half(r.own[d].astype(F32) + r.down_in[d].astype(F32))
                    down_copy(r.down_out.at[d], d).start()

        @pl.when(inside(f))
        def _():
            lower = jnp.where(low_z, r.up_in[f].astype(F32), 0.0)
            upper = jnp.where(high_z, r.down_in[f].astype(F32), 0.0)
            r.fin[f] = half(r.own[f].astype(F32) + lower + upper)
            keep_copy(f).start()
            to_x, to_y, by_x = goes(f)
            single = f < SETS
            pl.when(to_x & single & jnp.logical_not(by_x))(lambda: give_x(f, r.x_recv.at[jnp.minimum(f, SETS - 1)]).start())
            pl.when(to_x & jnp.logical_not(single & jnp.logical_not(by_x)))(lambda: give_x(f, r.bulk.at[7]).start())
            pl.when(to_y & single & by_x)(lambda: give_y(f, r.y_recv.at[jnp.minimum(f, SETS - 1)]).start())
            pl.when(to_y & jnp.logical_not(single & by_x))(lambda: give_y(f, r.bulk.at[8]).start())

        @pl.when(inside(w, SETS))
        def _():
            _, _, by_x = goes(w)

            @pl.when(by_x)
            def _():
                give_y(w, r.y_recv.at[w], landing(w, 1 - slot, x)).wait_recv()
                pass_x(w).start()

            @pl.when(jnp.logical_not(by_x))
            def _():
                give_x(w, r.x_recv.at[w], landing(w, 1 - slot, 1 - x)).wait_recv()
                pass_y(w).start()

    def finish_pieces():
        both = PIECES - SETS
        some = SETS + both // 2
        got = both // 2 + SETS
        pl.when(high_z)(lambda: remote(r.own, r.up_in, r.bulk.at[0], r.bulk.at[0], up).wait_send())
        pl.when(low_z)(lambda: remote(r.own, r.down_in, r.bulk.at[1], r.bulk.at[1], down).wait_send())
        pltpu.make_async_copy(r.fin, r.own, r.bulk.at[2]).wait()
        for i, count in ((3, some), (4, some), (5, SETS // 2), (6, SETS // 2)):
            remote(r.fin.at[0:count], r.own.at[0:count], r.bulk.at[i], r.bulk.at[i], xn).wait_send()
        for i in (7, 8):
            remote(r.fin.at[0:got], r.own.at[0:got], r.bulk.at[i], r.bulk.at[i], xn).wait_recv()

    far_half = (1 - x, 1 - y)
    near_half = (x, y)
    quarter = (x * 2 + y, 4 + y * 2 + x)
    near, next_near = (xn, yn), (yn, xn)

    def cols(j, n):
        return many(j * 256, 256 * n, 256)

    def ar(i, src, dst, target):
        return remote(src, dst, r.ar_send.at[i], r.ar_recv.at[i], target)

    def ar_one(s):
        return ar(s, r.total.at[:, cols(4 * s + 2 * far_half[s], 2)], r.part_in.at[s], near[s])

    def ar_two(s):
        give = 4 * s + 2 * near_half[s] + (1 - near_half[1 - s])
        return ar(2 + s, r.total.at[:, cols(give, 1)], r.part_in.at[2 + s, :, 0:256], next_near[s])

    def ar_up(s):
        return ar(4 + s, r.z_out.at[s], r.z_in.at[s], up)

    def ar_down(s):
        return ar(6 + s, r.z_out.at[2 + s], r.z_in.at[2 + s], down)

    def ar_four(s):
        piece = r.final.at[:, cols(quarter[s], 1)]
        return ar(8 + s, piece, piece, next_near[s])

    def ar_four_got(s):
        piece = r.final.at[:, cols(4 * s + 2 * near_half[s] + (1 - near_half[1 - s]), 1)]
        return ar(8 + s, piece, piece, next_near[s])

    def ar_five(s):
        piece = r.final.at[:, cols(4 * s + 2 * near_half[s], 2)]
        return ar(10 + s, piece, piece, near[s])

    def ar_five_got(s):
        piece = r.final.at[:, cols(4 * s + 2 * far_half[s], 2)]
        return ar(10 + s, piece, piece, near[s])

    def add_into(ref, other_part):
        ref[...] = half(ref[...].astype(F32) + other_part.astype(F32))

    def ar_stage1():
        for s in range(2):
            ar_one(s).start()

    def ar_stage2():
        for s in range(2):
            ar_one(s).wait()
            add_into(r.total.at[:, cols(4 * s + 2 * near_half[s], 2)], r.part_in[s])
            ar_two(s).start()

    def ar_stage3():
        for s in range(2):
            ar_two(s).wait()
            add_into(r.total.at[:, cols(quarter[s], 1)], r.part_in[2 + s, :, 0:256])

            @pl.when(z == 0)
            def _():
                r.z_out[s] = r.total[:, cols(quarter[s], 1)]
                ar_up(s).start()

            @pl.when(z == zs - 1)
            def _():
                r.z_out[2 + s] = r.total[:, cols(quarter[s], 1)]
                ar_down(s).start()

    def ar_stage_z(k):
        for s in range(2):
            @pl.when(z == k)
            def _():
                ar_up(s).wait_recv()
                if k < zs - 1:
                    r.z_out[s] = half(r.total[:, cols(quarter[s], 1)].astype(F32) + r.z_in[s].astype(F32))
                    ar_up(s).start()

            @pl.when(z == zs - 1 - k)
            def _():
                ar_down(s).wait_recv()
                if k < zs - 1:
                    r.z_out[2 + s] = half(r.total[:, cols(quarter[s], 1)].astype(F32) + r.z_in[2 + s].astype(F32))
                    ar_down(s).start()

    def ar_stage4():
        for s in range(2):
            lower = jnp.where(low_z, r.z_in[s].astype(F32), 0.0)
            upper = jnp.where(high_z, r.z_in[2 + s].astype(F32), 0.0)
            own = r.total[:, cols(quarter[s], 1)].astype(F32)
            r.final[:, cols(quarter[s], 1)] = half(own + lower + upper)
            ar_four(s).start()

    def ar_stage5():
        for s in range(2):
            ar_four_got(s).wait_recv()
            ar_five(s).start()

    def ar_stage6():
        for s in range(2):
            ar_five_got(s).wait_recv()
            ar_four(s).wait_send()
            ar_five(s).wait_send()
            pl.when(high_z)(lambda s=s: ar_up(s).wait_send())
            pl.when(low_z)(lambda s=s: ar_down(s).wait_send())

    stages_at = {3: ar_stage2, 4: ar_stage3, 5: lambda: ar_stage_z(1)}

    def slice_step(s, _):
        e, start, _, _ = where_from(s * 8, slot, x)
        hs = many(start, SLICE, SLICE)
        wi = half(r.win[e, :, hs].astype(F32).T)
        wo = r.wout[e, hs, :]
        bias = jnp.broadcast_to(r.binf[pl.ds(e, 1), hs], (128, SLICE)).T[:, 0:1]
        n, co, g = r.n_all[...], r.c_all[...], r.g_all[pl.ds(e, 1), :]
        hid, slope = gelu_parts(dot_nt(wi, n) + bias)
        dh = dot_nt(wo, co)
        for kind, grad in ((0, dot(half(slope * (dh * g)), n)), (1, dot(half(hid * g), co))):
            for i in range(SLICE // PIECE):
                r.own[s * 8 + i * 2 + kind] = half(grad[i * PIECE:(i + 1) * PIECE, :])
        for at, todo in stages_at.items():
            pl.when(s == at)(todo)
        first = jnp.where(s < 2, s * TICKS, SETS + (s - 2) * TICKS)
        for k in range(TICKS):
            tick(first + k)
        return 0

    lax.fori_loop(0, 2, slice_step, 0)
    clock = iter(range(2 * TICKS, SETS))

    for copy in partials:
        copy.wait()

    r.out[...] = half(r.mid[0:BLOCK, :] + (r.running[ours, :] + r.got_running[...]))[0:tokens, :]
    zeros = jnp.zeros((ROWS - BLOCK, 128), F32)
    d_gates = jnp.concatenate([r.dgate[ours, :] + r.got_dgate[...], zeros], axis=0)
    rprobs, chosen = r.rprobs[...], r.chosen[...]
    d_probs = d_gates * chosen
    d_logits = half(rprobs * (d_probs - jnp.sum(rprobs * d_probs, axis=-1, keepdims=True)))
    r.dn[0:BLOCK, :] = r.drows[ours, :] + r.got_drows[...]
    r.dn[BLOCK:ROWS, :] = jnp.zeros((ROWS - BLOCK, 512), F32)
    tick(next(clock))
    dn = r.dn[...] + dot(d_logits, route_t)
    xhat = r.xhat2[...]
    n2 = half(xhat * gain2 + bias2)
    grad_route = dot(half(d_logits.astype(F32).T), n2)
    vector_rows = {5: column_sum(dn * xhat), 6: column_sum(dn)}
    r.xs[...] = jnp.zeros_like(r.xs)
    r.xs[0:tokens, :] = r.cot[...].astype(F32)
    d_middle = r.xs[...] + norm_back(dn, xhat, spread2, gain2)
    r.mid[...] = d_middle
    r.db[...] = half(d_middle)
    db = r.db[...]
    vector_rows[4] = column_sum(db.astype(F32))
    r.dense[:, 1536:2048] = half(dot(half(r.ctx[...].astype(F32).T), db))
    r.dctx[...] = half(dot_nt(db, r.wproj[...]))
    tick(next(clock))

    def heads_back(i, _):
        q, k, v = [r.mixed[:, many(base + 128 * i, 128, 128)] for base in (0, 512, 1024)]
        q = q * BF16(HEAD_DIM ** -0.5)
        do = r.dctx[:, many(128 * i, 128, 128)]
        parts = []
        for h in range(2):
            p = r.probs[2 * i + h]
            dp = dot_nt(jnp.where(low_lane == (h == 0), do, jnp.zeros_like(do)), v)
            ds = p * (dp - jnp.sum(p * dp, axis=-1, keepdims=True))
            parts.append((dot(half(ds), k) * HEAD_DIM ** -0.5, dot(half(ds.T), q), dot(half(p.T), do)))
        for j, base in enumerate((0, 512, 1024)):
            r.dmixed[:, many(base + 128 * i, 128, 128)] = half(jnp.where(low_lane, parts[0][j], parts[1][j]))
        return 0

    tick(next(clock))
    tick(next(clock))
    lax.fori_loop(0, 4, heads_back, 0)
    tick(next(clock))
    tick(next(clock))
    tick(next(clock))
    n1_t = half(r.n1[...].astype(F32).T)
    dn = 0.0
    for i in range(3):
        part = r.dmixed[:, 512 * i:512 * (i + 1)]
        if i != 1:
            vector_rows[2 + i // 2] = column_sum(part.astype(F32))
        r.dense[:, 512 * i:512 * (i + 1)] = half(dot(n1_t, part))
        dn = dn + dot_nt(part, r.wqkv[:, 512 * i:512 * (i + 1)])
        tick(next(clock))
    xhat = r.xhat1[...]
    vector_rows[0] = column_sum(dn * xhat)
    vector_rows[1] = column_sum(dn)
    r.igrad[...] = (r.mid[...] + norm_back(dn, xhat, spread1, gain1))[0:tokens, :]

    vectors = jnp.concatenate([grad_route[0:4, :]] + [vector_rows[i] for i in range(7)] + [jnp.zeros((5, 512), F32)], axis=0)
    r.dn[0:16, :] = vectors
    low_half, high_half = r.dn[0:16, 0:256], r.dn[0:16, 256:512]
    r.extra[1, :, 0:256] = jnp.where(c == 0, high_half, low_half)
    own_half = jnp.where(c == 0, low_half, high_half)
    swaps = [remote(r.dense.at[other, :], r.dense_in, r.d_send.at[0], r.d_recv.at[0], partner),
             remote(r.extra.at[1], r.extra.at[2], r.d_send.at[1], r.d_recv.at[1], partner)]
    for copy in swaps:
        copy.start()
    for copy in swaps:
        copy.wait()
    r.total[0:256, :] = half(r.dense[mine, :].astype(F32) + r.dense_in[...].astype(F32))
    sums = own_half + r.extra[2, :, 0:256]
    small = jnp.concatenate([r.extra[0, 0:4, :], jnp.zeros((12, 2048), F32)], axis=0)
    shifted = jnp.concatenate([jnp.zeros((4, 256), F32), sums[0:12, :]], axis=0)
    r.total[256:272, :] = half(small + jnp.concatenate([shifted, jnp.zeros((16, 1792), F32)], axis=1))

    ar_stage1()

    for t in clock:
        tick(t)
    lax.fori_loop(2, STEPS, slice_step, 0)
    start, ends = SETS + (STEPS - 2) * TICKS, PIECES + HOP * (zs - 1)
    stages = {2: lambda: ar_stage_z(2), 5: lambda: ar_stage_z(3), 8: ar_stage4, 13: ar_stage5}

    def last_ticks(t, _):
        for at, stage in stages.items():
            pl.when(t == start + at)(stage)
        tick(t)
        return 0

    lax.fori_loop(start, ends, last_ticks, 0)
    ar_stage6()
    finish_pieces()
    for g in gathers:
        g.drain()
    for i in range(4):
        count_copy(min(i, 1), i, 0, partner).wait_send()
    for k in range(1, zs):
        pl.when(z < k)(lambda k=k: count_copy(2, 3 + k, 0, partner).wait_send())


def block_call(zs, *args):
    tokens, width = args[0].shape
    vm, hbm = pl.BlockSpec(memory_space=pltpu.VMEM), pl.BlockSpec(memory_space=pl.ANY)
    shape = jax.ShapeDtypeStruct
    in_specs = [hbm if name in ("win_in", "wout_in") else vm for name in INPUTS]
    scratch = [pltpu.VMEM(dims, dtype) for _, dims, dtype in SCRATCH]
    scratch += [pltpu.SemaphoreType.DMA(dims) for _, dims in SEMS]
    return pl.pallas_call(
        functools.partial(block_kernel, zs),
        out_shape=(shape((tokens, width), BF16), shape((tokens, width), F32), shape((4, 2048, 512), BF16), shape((272, 2048), BF16)),
        in_specs=in_specs,
        out_specs=(vm, vm, hbm, vm),
        scratch_shapes=scratch,
        compiler_params=pltpu.CompilerParams(collective_id=0, has_side_effects=True, vmem_limit_bytes=63 << 20),
        name="encoder_block",
    )(*args)


def finish_kernel(grads_in, grads_out, summed, out_in, igrad_in, grad_in, grad_out, qkv, proj, route, bias_in, bias_out, out, igrad,
                  *vectors):
    grad_in[0] = grads_in[0].astype(F32).T
    grad_out[...] = grads_out[...].astype(F32)

    @pl.when(pl.program_id(0) == 0)
    def _():
        qkv[...] = summed[0:256, 0:1536].astype(F32)
        proj[...] = summed[0:256, 1536:2048].astype(F32)
        rows = summed[256:272, :].astype(F32)
        bias_in[...] = rows[0:2, :]
        bias_out[...] = rows[2:4, 0:512]
        route[...] = rows[4:8, 0:256]
        for i, ref in enumerate(vectors):
            ref[...] = rows[8 + i, 0:256]
        out[...] = out_in[...]
        igrad[...] = igrad_in[...]


def finish(grads, summed, out, igrad):
    shape = jax.ShapeDtypeStruct
    steps = 8

    def whole(ref):
        return pl.BlockSpec(ref.shape, lambda i: (0,) * len(ref.shape))

    got_in = pl.BlockSpec((1, 512, 512), lambda i: (i // 4, i % 4, 0))
    got_out = pl.BlockSpec((1, 512, 512), lambda i: (2 + i // 4, i % 4, 0))
    block_in = pl.BlockSpec((1, 512, 512), lambda i: (i // 4, 0, i % 4))
    block_out = pl.BlockSpec((1, 512, 512), lambda i: (i // 4, i % 4, 0))
    small = [shape((256, 1536), F32), shape((256, 512), F32), shape((4, 256), F32), shape((2, 2048), F32), shape((2, 512), F32),
             shape(out.shape, out.dtype), shape(igrad.shape, igrad.dtype)] + [shape((256,), F32)] * 7
    return pl.pallas_call(
        finish_kernel,
        grid=(steps,),
        out_shape=[shape((2, 512, 2048), F32), shape((2, 2048, 512), F32)] + small,
        in_specs=[got_in, got_out, whole(summed), whole(out), whole(igrad)],
        out_specs=[block_in, block_out] + [whole(v) for v in small],
        compiler_params=pltpu.CompilerParams(vmem_limit_bytes=60 << 20),
        name="finish",
    )(grads, grads, summed, out, igrad)


def swap(v):
    return lax.ppermute(v, "shard", [(0, 1), (1, 0)])


def fused(inputs, norm1_gain, norm1_bias, qkv_weight, query_bias, value_bias, out_weight, out_bias, norm2_gain, norm2_bias,
          router_weight, noise, expert_in, expert_in_bias, expert_out, expert_out_bias, routes, priority, cotangent):
    out, igrad, grads, summed = block_call(
        lax.axis_size("replica") // 4, inputs, cotangent, noise.T, routes.T, priority, norm1_gain, norm1_bias, query_bias,
        value_bias, out_bias, norm2_gain, norm2_bias, router_weight.T, qkv_weight, out_weight, expert_in, expert_out,
        expert_in_bias, expert_out_bias)
    grad_in, grad_out, qkv, proj, route, bias_in, bias_out, out, igrad, *cols = finish(grads, summed, out, igrad)
    return (out, igrad, cols[0], cols[1], qkv, cols[2], cols[3], proj, cols[4], cols[5], cols[6], route.T,
            grad_in, bias_in, grad_out, bias_out)


def layer_norm(values, gain_vector, bias_vector):
    centered = values - jnp.mean(values, axis=-1, keepdims=True)
    spread = lax.rsqrt(jnp.mean(centered * centered, axis=-1, keepdims=True) + LN_EPS)
    return centered * spread * gain_vector + bias_vector


def kept_gates(pair_expert, ranks, offsets, capacity, expert_count):
    same = pair_expert[:, None] == pair_expert[None, :]
    earlier = ranks[None, :] < ranks[:, None]
    before = jnp.sum(jnp.where(same & earlier, 1, 0).astype(jnp.int32), axis=1)
    onehot = pair_expert[:, None] == jnp.arange(expert_count, dtype=jnp.int32)[None, :]
    first_slot = jnp.sum(jnp.where(onehot, offsets[None, :], 0).astype(jnp.int32), axis=1)
    keep = before + first_slot < capacity
    picked = jnp.where(onehot & keep[:, None], 1.0, 0.0).astype(jnp.float32)
    return jnp.sum(picked.reshape(-1, 2, expert_count), axis=1)


def general(
    inputs, norm1_gain, norm1_bias, qkv_weight, query_bias, value_bias, out_weight, out_bias, norm2_gain, norm2_bias,
    router_weight, noise, expert_in, expert_in_bias, expert_out, expert_out_bias, routes, priority, cotangent,
):
    tok_count, width = inputs.shape
    replicas, cores = lax.axis_size("replica"), lax.axis_size("shard")
    shard = lax.axis_index("shard")
    images = tok_count // PATCHES
    heads = width // HEAD_DIM
    owned, _, hidden_count = expert_in.shape
    expert_count = owned * cores
    score_scale = HEAD_DIM ** (-0.5)
    f32 = jnp.float32

    vectors = (norm1_gain, norm1_bias, query_bias, value_bias, out_bias, norm2_gain, norm2_bias)
    packed = jnp.concatenate(
        [qkv_weight, out_weight, jnp.stack(vectors, axis=1), router_weight], axis=1)
    packed = lax.all_gather(packed, "shard", axis=0, tiled=True)
    weight_qkv = packed[:, :3 * width]
    weight_proj = packed[:, 3 * width:4 * width]
    small = packed[:, 4 * width:]
    gain_one, bias_one, bias_query, bias_value, bias_proj, gain_two, bias_two = [
        small[:, i].astype(f32) for i in range(len(vectors))]
    weight_route = small[:, len(vectors):]

    pair_expert = routes.reshape(-1)
    onehot_pairs = (pair_expert[:, None] == jnp.arange(expert_count, dtype=jnp.int32)[None, :]).astype(jnp.int32)
    load = jnp.sum(onehot_pairs, axis=0)
    loads = lax.all_gather(load, ("replica", "shard"))
    position = lax.axis_index("replica") * cores + shard
    ahead = jnp.arange(replicas * cores)[:, None] < position
    offsets = jnp.sum(jnp.where(ahead, loads, 0), axis=0)
    capacity = 2 * tok_count * replicas * cores // expert_count
    chosen = kept_gates(pair_expert, priority.reshape(-1), offsets, capacity, expert_count)

    residual_in = inputs.astype(f32)
    normed_one, norm_one_back = jax.vjp(layer_norm, residual_in, gain_one, bias_one)
    normed_one_half = half(normed_one)
    qkv_bias = jnp.concatenate([bias_query, jnp.zeros_like(bias_query), bias_value])
    mixed = half(dot(normed_one_half, weight_qkv) + qkv_bias)
    shaped = mixed.reshape(images, PATCHES, 3, heads, HEAD_DIM)
    query, keys, values = (shaped[:, :, 0], shaped[:, :, 1], shaped[:, :, 2])
    scores = jnp.einsum("bqhd,bkhd->bhqk", query, keys, preferred_element_type=f32) * score_scale
    row_max = jnp.max(scores, axis=-1, keepdims=True)
    log_total = row_max + jnp.log(jnp.sum(jnp.exp(scores - row_max), axis=-1, keepdims=True))
    context = jnp.einsum(
        "bhqk,bkhd->bqhd", half(jnp.exp(scores - log_total)), values, preferred_element_type=f32)
    context_half = half(context.reshape(tok_count, width))
    middle = residual_in + (dot(context_half, weight_proj) + bias_proj)
    normed_two, norm_two_back = jax.vjp(layer_norm, middle, gain_two, bias_two)
    normed_two_half = half(normed_two)
    logits = dot(normed_two_half, weight_route) + noise
    route_probs = jax.nn.softmax(logits, axis=-1)
    gate_weights = route_probs * chosen
    upstream = cotangent.astype(f32)

    pair_n = jnp.concatenate([normed_two_half, swap(normed_two_half)], axis=0)
    pair_c = jnp.concatenate([cotangent, swap(cotangent)], axis=0)
    own_gates = lax.dynamic_slice_in_dim(gate_weights, shard * owned, owned, 1)
    other_gates = swap(lax.dynamic_slice_in_dim(gate_weights, (1 - shard) * owned, owned, 1))
    pair_g = jnp.concatenate([own_gates, other_gates], axis=0)
    pair_up = pair_c.astype(f32)
    running = jnp.zeros((2 * tok_count, width), f32)
    d_rows = jnp.zeros((2 * tok_count, width), f32)
    gate_columns, bias_in_grads, bias_out_grads, in_grads, out_grads = [], [], [], [], []
    for e in range(owned):
        gate = pair_g[:, e:e + 1]
        pre = dot(pair_n, expert_in[e]) + expert_in_bias[e].astype(f32)
        act, slope = gelu_parts(pre)
        hid = half(act)
        result = dot(hid, expert_out[e]) + expert_out_bias[e].astype(f32)
        running = running + gate * result
        gate_columns.append(jnp.sum(pair_up * result, axis=1))
        d_result = half(gate * pair_up)
        d_pre = half(slope * dot_nt(d_result, expert_out[e]))
        d_rows = d_rows + dot_nt(d_pre, expert_in[e])
        bias_in_grads.append(jnp.sum(d_pre.astype(f32), axis=0))
        bias_out_grads.append(jnp.sum(d_result.astype(f32), axis=0))
        in_grads.append(jnp.einsum("td,th->dh", pair_n, d_pre, preferred_element_type=f32))
        out_grads.append(jnp.einsum("th,td->hd", hid, d_result, preferred_element_type=f32))
    d_gate_part = jnp.stack(gate_columns, axis=1)
    running = running[:tok_count] + swap(running[tok_count:])
    d_normed = d_rows[:tok_count] + swap(d_rows[tok_count:])
    d_gate_other = swap(d_gate_part[tok_count:])
    d_gate_own = d_gate_part[:tok_count]
    d_gates = jnp.where(shard == 0, jnp.concatenate([d_gate_own, d_gate_other], axis=1),
                        jnp.concatenate([d_gate_other, d_gate_own], axis=1))

    grad_in = lax.psum(half(jnp.stack(in_grads, axis=0)), "replica")
    grad_out = lax.psum(half(jnp.stack(out_grads, axis=0)), "replica")

    output = half(middle + running)
    d_probs = d_gates * chosen
    d_logits = half(route_probs * (d_probs - jnp.sum(route_probs * d_probs, axis=-1, keepdims=True)))
    grad_route = jnp.einsum("td,te->de", normed_two_half, d_logits, preferred_element_type=f32)
    d_normed = d_normed + dot_nt(d_logits, weight_route)
    d_middle, grad_gain_two, grad_bias_two = norm_two_back(d_normed)
    d_middle = d_middle + upstream
    d_branch = half(d_middle)
    grad_proj = jnp.einsum("tc,td->cd", context_half, d_branch, preferred_element_type=f32)
    grad_proj_bias = jnp.sum(d_branch.astype(f32), axis=0)
    d_context = half(dot_nt(d_branch, weight_proj)).reshape(images, PATCHES, heads, HEAD_DIM)
    attn_probs = jnp.exp(scores - log_total)
    d_attn = jnp.einsum("bqhd,bkhd->bhqk", d_context, values, preferred_element_type=f32)
    d_values = jnp.einsum("bhqk,bqhd->bkhd", half(attn_probs), d_context, preferred_element_type=f32)
    d_scores = half(attn_probs * (d_attn - jnp.sum(attn_probs * d_attn, axis=-1, keepdims=True)))
    d_query = jnp.einsum("bhqk,bkhd->bqhd", d_scores, keys, preferred_element_type=f32) * score_scale
    d_keys = jnp.einsum("bhqk,bqhd->bkhd", d_scores, query, preferred_element_type=f32) * score_scale
    d_mixed = half(jnp.stack([d_query, d_keys, d_values], axis=2).reshape(tok_count, 3 * width))
    grad_qkv = jnp.einsum("td,tf->df", normed_one_half, d_mixed, preferred_element_type=f32)
    mixed_sums = jnp.sum(d_mixed.astype(f32), axis=0)
    d_normed_one = dot_nt(d_mixed, weight_qkv)
    d_input, grad_gain_one, grad_bias_one = norm_one_back(d_normed_one)
    input_grad = d_input + d_middle

    columns = jnp.stack((grad_gain_one, grad_bias_one, mixed_sums[:width], mixed_sums[2 * width:], grad_proj_bias,
                         grad_gain_two, grad_bias_two), axis=1)
    dense = half(jnp.concatenate([grad_qkv, grad_proj, columns, grad_route], axis=1))
    mine = width // 2
    keep = lax.dynamic_slice_in_dim(dense, shard * mine, mine, 0)
    give = lax.dynamic_slice_in_dim(dense, (1 - shard) * mine, mine, 0)
    dense = keep.astype(f32) + swap(give).astype(f32)
    bias_row = jnp.concatenate(bias_in_grads + bias_out_grads)
    summed, bias_row = lax.psum((half(dense), bias_row), "replica")
    summed = summed.astype(f32)
    columns = [summed[:, 4 * width + i] for i in range(len(vectors))]
    grad_in_bias = bias_row[:owned * hidden_count].reshape(owned, hidden_count)
    grad_out_bias = bias_row[owned * hidden_count:].reshape(owned, width)
    return (
        output, input_grad, columns[0], columns[1], summed[:, :3 * width], columns[2], columns[3],
        summed[:, 3 * width:4 * width], columns[4], columns[5], columns[6], summed[:, 4 * width + len(vectors):],
        grad_in.astype(f32), grad_in_bias, grad_out.astype(f32), grad_out_bias,
    )


def on_device(*args):
    expert_in, inputs = args[12], args[0]
    planes = lax.axis_size("replica") == 16 and lax.axis_size("shard") == 2
    if planes and inputs.shape == (PATCHES, 512) and expert_in.shape == (2, 512, 2048):
        return fused(*args)
    return general(*args)


def solution(mesh):
    both, split = ("replica", "shard"), "shard"
    return jax.shard_map(
        on_device,
        mesh=mesh,
        in_specs=(
            P(both, None), P(split), P(split), P(split, None), P(split), P(split), P(split, None), P(split), P(split),
            P(split), P(split, None), P(both, None), P(split, None, None), P(split, None), P(split, None, None),
            P(split, None), P(both, None), P(both, None), P(both, None),
        ),
        out_specs=(
            P(both, None), P(both, None), P(split), P(split), P(split, None), P(split), P(split), P(split, None),
            P(split), P(split), P(split), P(split, None), P(split, None, None), P(split, None), P(split, None, None),
            P(split, None),
        ),
        check_vma=False,
    )
```

```python
import functools
from types import SimpleNamespace

import jax
import jax.numpy as jnp
from jax import lax
from jax.experimental import pallas as pl
from jax.experimental.pallas import tpu as pltpu
from jax.sharding import PartitionSpec as P

HEAD_DIM = 64
PATCHES = 197
LN_EPS = 1e-06
MESH = pl.DeviceIdType.MESH
NT = (((1,), (1,)), ((), ()))
GELU_K = 0.7978845608028654
GELU_A = 0.044715
F32 = jnp.float32
BF16 = jnp.bfloat16
ROWS = 256
BLOCK = 208
STEP = 512
SLICE = 256
PIECE = 128
STEPS = 6
PER = 2 * SLICE // PIECE
PIECES = STEPS * PER
SETS = 2 * PER
HOP = 3
TICKS, LATER = 1, 2
EARLY = 3
BEATS = (1, 1, 1, 1, 1, 0, 1, 1, 0, 1)
PASS = 4


def half(values):
    return values.astype(BF16)


def dot(a, b):
    return jnp.dot(a, b, preferred_element_type=F32)


def dot_nt(a, b):
    return lax.dot_general(a, b, NT, preferred_element_type=F32)


def gelu_parts(x):
    x2 = x * x
    q = 0.5 + 0.5 * jnp.tanh(x * (GELU_K + (GELU_K * GELU_A) * x2))
    h = x * q
    return h, q + (h * (1.0 - q)) * (2 * GELU_K + (6 * GELU_K * GELU_A) * x2)


def iota(shape, dim):
    return lax.broadcasted_iota(jnp.int32, shape, dim)


def many(start, size, unit):
    return pl.ds(pl.multiple_of(start, unit), size)


def normalize(v):
    centered = v - jnp.mean(v, axis=-1, keepdims=True)
    spread = lax.rsqrt(jnp.mean(centered * centered, axis=-1, keepdims=True) + LN_EPS)
    return centered * spread, spread


def norm_back(d, xhat, spread, gain):
    dx = d * gain
    return spread * (dx - jnp.mean(dx, axis=-1, keepdims=True) - xhat * jnp.mean(dx * xhat, axis=-1, keepdims=True))


def column_sum(v):
    return jnp.sum(v, axis=0, keepdims=True)


def place():
    r = lax.axis_index("replica")
    return r // 4, (r // 2) % 2, r % 2, lax.axis_index("shard")


def rep(z, y, x):
    return (z * 2 + y) * 2 + x


class PlaneGather:
    def __init__(self, x_first, rows, at, sems):
        self.rows, self.at = rows, at
        self.send, self.recv, self.core_send, self.core_recv = sems
        z, y, x, c = place()
        near = ((rep(z, y, 1 - x), c), (rep(z, 1 - y, x), c))
        spots = (y * 2 + 1 - x, (1 - y) * 2 + x)
        self.targets = near if x_first else near[::-1]
        self.first, self.second = spots if x_first else spots[::-1]
        self.me, self.diagonal = y * 2 + x, (1 - y) * 2 + 1 - x
        self.core, self.partner = c, (rep(z, y, x), 1 - c)

    def ref(self, spot, core):
        first, size = self.at
        return self.rows.at[many((spot * 2 + core) * BLOCK + first, size, 16), :]

    def link(self, kind, spot):
        ref = self.ref(spot, self.core)
        return remote(ref, ref, self.send.at[kind, spot], self.recv.at[spot], self.targets[kind])

    def across(self, spot, core=None):
        ref = self.ref(spot, self.core if core is None else core)
        return remote(ref, ref, self.core_send.at[spot], self.core_recv.at[spot], self.partner)

    def begin(self, kind):
        self.link(kind, self.me).start()

    def hand(self):
        self.across(self.me).start()

    def turn(self):
        self.link(0, self.first).wait_recv()
        self.link(1, self.first).start()
        self.across(self.first).start()

    def far(self):
        for spot in (self.second, self.diagonal):
            self.link(0, spot).wait_recv()
            self.across(spot).start()

    def from_core(self, spot):
        self.across(spot, 1 - self.core).wait_recv()

    def drain(self):
        for kind, spot in ((0, self.me), (1, self.me), (1, self.first)):
            self.link(kind, spot).wait_send()
        for spot in range(4):
            self.across(spot).wait_send()


class Halves:
    def __init__(self, rows, sems):
        cuts = ((0, 112), (112, BLOCK - 112))
        self.parts = [PlaneGather(m == 0, rows, cuts[m], [ref.at[m] for ref in sems]) for m in range(2)]

    def begin(self):
        for part in self.parts:
            part.begin(0)
        for part in self.parts:
            part.hand()
        for part in self.parts:
            part.begin(1)

    def turn(self):
        for part in self.parts:
            part.turn()

    def far(self):
        for part in self.parts:
            part.far()

    def from_core(self, spot):
        for part in self.parts:
            part.from_core(spot)

    def others(self):
        part = self.parts[0]
        return part.first, part.second, part.diagonal

    def drain(self):
        for part in self.parts:
            part.drain()


SCRATCH = (
    ("n_all", (8 * BLOCK, 512), BF16), ("c_all", (8 * BLOCK, 512), BF16), ("g_all", (8, 8 * BLOCK), F32),
    ("wqkv", (512, 1536), BF16), ("wproj", (512, 512), BF16), ("vec", (2, 16, 256), F32), ("binf", (2, 2048), F32),
    ("win", (2, 512, 2048), BF16), ("wout", (2, 2048, 512), BF16),
    ("count_out", (3, 8, 128), F32), ("count_in", (9, 8, 128), F32),
    ("xs", (ROWS, 512), F32), ("pairs", (16, ROWS), F32),
    ("xhat1", (ROWS, 512), F32), ("n1", (ROWS, 512), BF16), ("mixed", (ROWS, 1536), BF16),
    ("probs", (8, ROWS, ROWS), F32), ("ctx", (ROWS, 512), BF16), ("mid", (ROWS, 512), F32), ("xhat2", (ROWS, 512), F32),
    ("chosen", (ROWS, 128), F32), ("rprobs", (ROWS, 128), F32),
    ("res", (2 * BLOCK, 512), F32), ("running", (2 * BLOCK, 512), F32), ("drows", (2 * BLOCK, 512), F32),
    ("dgate", (2 * BLOCK, 128), F32), ("dres", (2 * BLOCK, 512), BF16), ("gcol", (2 * BLOCK, 128), F32),
    ("got_running", (BLOCK, 512), F32), ("got_drows", (BLOCK, 512), F32), ("got_dgate", (BLOCK, 128), F32),
    ("db", (ROWS, 512), BF16), ("dctx", (ROWS, 512), BF16), ("dmixed", (ROWS, 1536), BF16), ("dn", (ROWS, 512), F32),
    ("dense", (512, 2048), BF16), ("dense_in", (256, 2048), BF16), ("extra", (3, 16, 2048), F32),
    ("total", (272, 2048), BF16), ("part_in", (4, 272, 512), BF16), ("z_out", (4, 272, 256), BF16), ("z_in", (4, 272, 256), BF16),
    ("own", (PIECES, PIECE, 512), BF16), ("up_in", (PIECES, PIECE, 512), BF16), ("up_out", (PIECES, PIECE, 512), BF16),
    ("down_in", (PIECES, PIECE, 512), BF16), ("down_out", (PIECES, PIECE, 512), BF16), ("fin", (PIECES, PIECE, 512), BF16),
)
SEMS = (
    ("g_send", (2, 2, 2, 4)), ("g_recv", (2, 2, 4)), ("g_csend", (2, 2, 4)), ("g_crecv", (2, 2, 4)),
    ("load", (2,)), ("w_send", (3,)), ("w_recv", (3,)), ("count_send", (7,)), ("count_recv", (9,)),
    ("p_send", (3,)), ("p_recv", (3,)), ("d_send", (2,)), ("d_recv", (2,)),
    ("ar_send", (12,)), ("ar_recv", (12,)), ("up_recv", (PIECES,)), ("down_recv", (PIECES,)), ("bulk", (9,)),
    ("x_recv", (SETS,)), ("y_recv", (SETS,)),
)
INPUTS = ("x", "cot", "noise_in", "routes_in", "prio", "v0", "v1", "v2", "v3", "v4", "v5", "v6", "route_in", "wqkv_in",
          "wproj_in", "win_in", "wout_in", "bin", "bout")
OUTPUTS = ("out", "igrad", "grads", "final")


def remote(src, dst, send, recv, target):
    return pltpu.make_async_remote_copy(
        src_ref=src, dst_ref=dst, send_sem=send, recv_sem=recv, device_id=target, device_id_type=MESH)


def block_kernel(zs, *refs):
    names = INPUTS + OUTPUTS + tuple(n for n, _, _ in SCRATCH) + tuple(n for n, _ in SEMS)
    r = SimpleNamespace(**dict(zip(names, refs, strict=True)))
    z, y, x, c = place()
    me = rep(z, y, x)
    partner = (me, 1 - c)
    xn, yn = (rep(z, y, 1 - x), c), (rep(z, 1 - y, x), c)
    up, down = (rep(z + 1, y, x), c), (rep(z - 1, y, x), c)
    low_z, high_z = z > 0, z < zs - 1
    tokens = r.x.shape[0]
    devices = 8 * zs
    capacity = 2 * tokens * devices // 4

    bar = pltpu.get_barrier_semaphore()
    for d in range(1, zs):
        peer = (rep(lax.rem(z + d, zs), y, x), c)
        pl.semaphore_signal(bar, inc=1, device_id=peer, device_id_type=MESH)
    for peer in (xn, yn, (rep(z, 1 - y, 1 - x), c), partner):
        pl.semaphore_signal(bar, inc=1, device_id=peer, device_id_type=MESH)

    loads = [pltpu.make_async_copy(r.win_in, r.win, r.load.at[0]), pltpu.make_async_copy(r.wout_in, r.wout, r.load.at[1])]
    for copy in loads:
        copy.start()

    r.xs[...] = jnp.zeros_like(r.xs)
    r.xs[0:tokens, :] = r.cot[...].astype(F32)
    own_rows = many(((y * 2 + x) * 2 + c) * BLOCK, BLOCK, 16)
    r.c_all[own_rows, :] = half(r.xs[0:BLOCK, :])
    mine, other = many(c * 256, 256, 16), many((1 - c) * 256, 256, 16)
    r.wqkv[mine, :] = r.wqkv_in[...]
    r.wproj[mine, :] = r.wproj_in[...]
    rows = [ref[...].astype(F32).reshape(1, 256) for ref in (r.v0, r.v1, r.v2, r.v3, r.v4, r.v5, r.v6)]
    rows += [jnp.zeros((1, 256), F32), r.route_in[...].astype(F32), jnp.zeros((4, 256), F32)]
    r.vec[c] = jnp.concatenate(rows, axis=0)
    r.binf[...] = r.bin[...].astype(F32)

    lane, row = iota((ROWS, 128), 1), iota((ROWS, 128), 0)
    r.pairs[0:8, :] = jnp.full((8, ROWS), -1.0, F32)
    r.pairs[8:16, :] = jnp.zeros((8, ROWS), F32)
    r.pairs[0:2, 0:tokens] = r.routes_in[...].astype(F32)
    r.pairs[8:12, 0:tokens] = r.noise_in[...]
    by_token = jnp.concatenate([r.pairs[...], jnp.zeros((112, ROWS), F32)], axis=0).T
    experts = [by_token[:, k:k + 1] for k in range(2)]
    noise = pltpu.roll(by_token, 120, 1)
    onehot = [jnp.where(lane.astype(F32) == experts[k], 1.0, 0.0) for k in range(2)]
    count = jnp.broadcast_to(column_sum(onehot[0] + onehot[1]), (8, 128))

    r.count_out[0] = count

    places = iota((ROWS, r.prio.shape[1]), 1) - 2 * iota((ROWS, r.prio.shape[1]), 0)
    ranks = r.prio[...].astype(F32)
    codes = [experts[k] * 1024.0 + jnp.sum(jnp.where(places == k, ranks, 0.0), axis=1, keepdims=True) for k in range(2)]
    codes = [jnp.where(row[:, 0:1] < tokens, code, -1.0) for code in codes]
    code_rows = jnp.where(lane == 0, codes[0], jnp.where(lane == 1, codes[1], 0.0)).T
    before = []
    for k in range(2):
        floor = experts[k] * 1024.0
        seen = 0.0
        for j in range(2):
            others = code_rows[j:j + 1, :]
            seen = seen + jnp.where((others < codes[k]) & (others >= floor), 1.0, 0.0)
        before.append(jnp.sum(seen, axis=1, keepdims=True))

    def count_copy(stage, i, slot, target):
        return remote(r.count_out.at[stage], r.count_in.at[slot], r.count_send.at[i], r.count_recv.at[slot], target)

    spot = y * 2 + x
    column = [(rep(k, y, x), c) for k in range(zs)]

    def counts_to_plane():
        for d in range(1, 4):
            q = lax.rem(spot + d, 4)
            count_copy(1, d, 1 + spot, (rep(z, q // 2, lax.rem(q, 2)), c)).start()

    def counts_up():
        for k in range(1, zs):
            pl.when(z < k)(lambda k=k: count_copy(2, 3 + k, 5 + z, column[k]).start())

    pl.semaphore_wait(bar, zs + 3)

    weights = [remote(ref, ref, r.w_send.at[i], r.w_recv.at[i], partner) for i, ref in enumerate(
        (r.vec.at[c], r.wqkv.at[mine, :], r.wproj.at[mine, :]))]
    for copy in weights:
        copy.start()
    gathers = [Halves((r.n_all, r.c_all)[m], (r.g_send.at[m], r.g_recv.at[m], r.g_csend.at[m], r.g_crecv.at[m]))
               for m in range(2)]
    ga, gb = gathers
    gb.begin()
    count_copy(0, 0, 0, partner).start()

    r.xs[0:tokens, :] = r.x[...].astype(F32)
    xhat, spread1 = normalize(r.xs[...])
    r.xhat1[...] = xhat

    count_copy(0, 0, 0, partner).wait_recv()
    ahead = jnp.where(c == 1, 1.0, 0.0) * r.count_in[0]
    count = count + r.count_in[0]
    r.count_out[1] = count
    counts_to_plane()

    weights[0].wait_send()
    remote(r.vec.at[1 - c], r.vec.at[1 - c], r.w_send.at[0], r.w_recv.at[0], partner).wait_recv()
    vec = jnp.concatenate([r.vec[0], r.vec[1]], axis=1)
    gain1, bias1, bias_q, bias_v, bias_p, gain2, bias2 = [vec[i:i + 1, :] for i in range(7)]
    route_rows = jnp.concatenate([vec[8:16, :], jnp.zeros((120, 512), F32)], axis=0)
    route_t, route = half(route_rows), half(route_rows.T)
    r.n1[...] = half(xhat * gain1 + bias1)

    for i, ref in ((1, r.wqkv), (2, r.wproj)):
        weights[i].wait_send()
        ref = ref.at[other, :]
        remote(ref, ref, r.w_send.at[i], r.w_recv.at[i], partner).wait_recv()
    for i, bias in enumerate((bias_q, None, bias_v)):
        part = dot(r.n1[...], r.wqkv[:, 512 * i:512 * (i + 1)])
        r.mixed[:, 512 * i:512 * (i + 1)] = half(part if bias is None else part + bias)

    for q in range(4):
        pl.when(spot != q)(lambda q=q: count_copy(1, 1, 1 + q, partner).wait_recv())
    for q in range(4):
        ahead = ahead + jnp.where(spot > q, r.count_in[1 + q], 0.0)
        count = count + jnp.where(spot != q, r.count_in[1 + q], 0.0)
    r.count_out[2] = count
    counts_up()

    gb.turn()

    low_lane = lane < HEAD_DIM
    key_kept = iota((ROWS, ROWS), 1) < tokens

    def heads_forward(i, _):
        q, k, v = [r.mixed[:, many(base + 128 * i, 128, 128)] for base in (0, 512, 1024)]
        q = q * BF16(HEAD_DIM ** -0.5)
        parts = []
        for h in range(2):
            s = dot_nt(jnp.where(low_lane == (h == 0), q, jnp.zeros_like(q)), k)
            s = jnp.where(key_kept, s, -1e30)
            e = jnp.exp(s - jnp.max(s, axis=-1, keepdims=True))
            p = e / jnp.sum(e, axis=-1, keepdims=True)
            r.probs[2 * i + h] = p
            parts.append(dot(half(p), v))
        r.ctx[:, many(128 * i, 128, 128)] = half(jnp.where(low_lane, parts[0], parts[1]))
        return 0

    lax.fori_loop(0, 4, heads_forward, 0)

    gb.far()
    for k in range(zs - 1):
        pl.when(z > k)(lambda k=k: count_copy(2, 4, 5 + k, partner).wait_recv())
    for k in range(zs - 1):
        ahead = ahead + jnp.where(z > k, r.count_in[5 + k], 0.0)
    offsets = ahead[0:1, :]
    chosen = 0.0
    for k in range(2):
        slot = before[k] + jnp.sum(onehot[k] * offsets, axis=1, keepdims=True)
        chosen = chosen + onehot[k] * jnp.where(slot < float(capacity), 1.0, 0.0)
    r.chosen[...] = chosen

    middle = r.xs[...] + (dot(r.ctx[...], r.wproj[...]) + bias_p)
    r.mid[...] = middle
    xhat, spread2 = normalize(middle)
    r.xhat2[...] = xhat
    n2 = half(xhat * gain2 + bias2)
    logits = jnp.where(lane < 4, dot(n2, route) + noise, -1e30)
    e = jnp.exp(logits - jnp.max(logits, axis=-1, keepdims=True))
    rprobs = e / jnp.sum(e, axis=-1, keepdims=True)
    r.rprobs[...] = rprobs
    gates = rprobs * chosen
    gates_high = half(gates).astype(F32)
    packed = jnp.where(lane < 4, gates_high, pltpu.roll(gates - gates_high, 4, 1)).T
    packed = jnp.concatenate([packed[0:8, :], jnp.zeros((8, 256), F32)], axis=1)
    r.n_all[own_rows, :] = jnp.concatenate([n2[0:192, :], half(jnp.concatenate(
        [n2[192:200, :].astype(F32), packed], axis=0))], axis=0)
    ga.begin()

    pair = many(spot * 2 * BLOCK, 2 * BLOCK, 16)
    for g in gathers:
        g.from_core(spot)
    for j in range(2):
        g8 = r.n_all[many((spot * 2 + j) * BLOCK + 192, 16, 16), 0:256].astype(F32)[8:16, :]
        g8 = g8 + pltpu.roll(g8, 4, 0)
        g8 = jnp.where(c == 0, g8, pltpu.roll(g8, 6, 0))
        r.gcol[j * BLOCK:(j + 1) * BLOCK, :] = jnp.concatenate([g8, jnp.zeros((120, 256), F32)], axis=0).T[0:BLOCK, :]
    for copy in loads:
        copy.wait()
    r.running[...] = jnp.zeros_like(r.running)
    r.drows[...] = jnp.zeros_like(r.drows)
    r.dgate[...] = jnp.zeros_like(r.dgate)
    r.extra[...] = jnp.zeros_like(r.extra)
    pair_lane = iota((2 * BLOCK, 128), 1)
    def expert_pass(e, between):
        gate = r.gcol[:, e:e + 1]
        r.res[...] = jnp.zeros_like(r.res)
        d_result = gate * r.c_all[pair, :].astype(F32)
        r.dres[...] = half(d_result)
        r.extra[0, 2 + e:3 + e, 0:512] = column_sum(r.dres[...].astype(F32))

        def hidden_step(j, _):
            hs = many(j * STEP, STEP, STEP)
            n = r.n_all[pair, :]
            pre = dot(n, r.win[e, :, hs]) + r.bin[e:e + 1, hs].astype(F32)
            hid, slope = gelu_parts(pre)
            r.res[...] += dot(half(hid), r.wout[e, hs, :])
            d_pre = half(slope * dot_nt(r.dres[...], r.wout[e, hs, :]))
            r.extra[0, e:e + 1, hs] = column_sum(d_pre.astype(F32))
            r.drows[...] += dot_nt(d_pre, r.win[e, :, hs])
            return 0

        lax.fori_loop(0, 2, hidden_step, 0)
        between()
        lax.fori_loop(2, 4, hidden_step, 0)
        result = r.res[...] + r.bout[e:e + 1, :].astype(F32)
        r.running[...] += gate * result
        d_gate = jnp.sum(r.c_all[pair, :].astype(F32) * result, axis=1, keepdims=True)
        r.dgate[...] = jnp.where(pair_lane == 2 * c + e, d_gate, r.dgate[...])

    expert_pass(0, lambda: None)
    ga.turn()
    ga.far()

    for g in gathers:
        for other_spot in g.others():
            g.from_core(other_spot)
    span = 8 * BLOCK
    row = jnp.zeros((8, span), F32)
    for d in range(8):
        g8 = r.n_all[d * BLOCK + 192:(d + 1) * BLOCK, 0:256].astype(F32)[8:16, :]
        g8 = g8 + pltpu.roll(g8, 4, 0)
        g8 = jnp.where(c == 0, g8, pltpu.roll(g8, 6, 0))
        at, shift = d * BLOCK // 128 * 128, d * BLOCK % 128
        width = min(384, span - at)
        g8 = jnp.concatenate([g8, jnp.zeros((8, 128), F32)], axis=1)
        g8 = pltpu.roll(g8, shift, 1) if shift else g8
        pieces = [jnp.zeros((8, at), F32)] if at else []
        pieces += [g8[:, 0:width]] + ([jnp.zeros((8, span - at - width), F32)] if span > at + width else [])
        row = row + jnp.concatenate(pieces, axis=1)
    r.g_all[...] = row

    slot = lax.rem(x + y, 2)

    def where_from(f, slice_of, x_of):
        s, i, kind = f // PER, lax.rem(f, PER) // 2, lax.rem(f, 2)
        t = jnp.maximum(s - 2, 0)
        e = jnp.where(s < 2, s, t // 2)
        start = slice_of * 1024 + jnp.where(s < 2, 512 + x_of * SLICE, lax.rem(t, 2) * SLICE)
        return e, start, i, kind

    def landing(f, slice_of=slot, x_of=x):
        e, start, i, kind = where_from(f, slice_of, x_of)
        return r.grads.at[kind * 2 + e, many(start + i * PIECE, PIECE, PIECE), :]

    def up_copy(src, f):
        return remote(src, r.up_in.at[f], r.bulk.at[0], r.up_recv.at[f], up)

    def down_copy(src, f):
        return remote(src, r.down_in.at[f], r.bulk.at[1], r.down_recv.at[f], down)

    def keep_copy(f):
        return pltpu.make_async_copy(r.fin.at[f], landing(f), r.bulk.at[2])

    def give_x(f, recv, ref=None):
        return remote(r.fin.at[f], landing(f) if ref is None else ref, r.bulk.at[3], recv, xn)

    def give_y(f, recv, ref=None):
        return remote(r.fin.at[f], landing(f) if ref is None else ref, r.bulk.at[4], recv, yn)

    def pass_x(f):
        ref = landing(f, 1 - slot, x)
        return remote(ref, ref, r.bulk.at[5], r.bulk.at[7], xn)

    def pass_y(f):
        ref = landing(f, 1 - slot, 1 - x)
        return remote(ref, ref, r.bulk.at[6], r.bulk.at[8], yn)

    def goes(f):
        late = lax.rem(f // PER, 2)
        return (f < SETS) | (late == 0), (f < SETS) | (late == 1), lax.rem(f, PER) < PER // 2

    def inside(f, count=PIECES):
        return (f >= 0) & (f < count)

    def tick(t):
        u, d, f, w = t - HOP * z, t - HOP * (zs - 1 - z), t - HOP * (zs - 1), t - HOP * (zs - 1) - PASS

        @pl.when(inside(u))
        def _():
            pl.when(z == 0)(lambda: up_copy(r.own.at[u], u).start())

            @pl.when(low_z)
            def _():
                up_copy(r.up_out.at[u], u).wait_recv()

                @pl.when(high_z)
                def _():
                    r.up_out[u] = half(r.own[u].astype(F32) + r.up_in[u].astype(F32))
                    up_copy(r.up_out.at[u], u).start()

        @pl.when(inside(d))
        def _():
            pl.when(z == zs - 1)(lambda: down_copy(r.own.at[d], d).start())

            @pl.when(high_z)
            def _():
                down_copy(r.down_out.at[d], d).wait_recv()

                @pl.when(low_z)
                def _():
                    r.down_out[d] = half(r.own[d].astype(F32) + r.down_in[d].astype(F32))
                    down_copy(r.down_out.at[d], d).start()

        @pl.when(inside(f))
        def _():
            lower = jnp.where(low_z, r.up_in[f].astype(F32), 0.0)
            upper = jnp.where(high_z, r.down_in[f].astype(F32), 0.0)
            r.fin[f] = half(r.own[f].astype(F32) + lower + upper)
            keep_copy(f).start()
            to_x, to_y, by_x = goes(f)
            single = f < SETS
            pl.when(to_x & single & jnp.logical_not(by_x))(lambda: give_x(f, r.x_recv.at[jnp.minimum(f, SETS - 1)]).start())
            pl.when(to_x & jnp.logical_not(single & jnp.logical_not(by_x)))(lambda: give_x(f, r.bulk.at[7]).start())
            pl.when(to_y & single & by_x)(lambda: give_y(f, r.y_recv.at[jnp.minimum(f, SETS - 1)]).start())
            pl.when(to_y & jnp.logical_not(single & by_x))(lambda: give_y(f, r.bulk.at[8]).start())

        @pl.when(inside(w, SETS))
        def _():
            _, _, by_x = goes(w)

            @pl.when(by_x)
            def _():
                give_y(w, r.y_recv.at[w], landing(w, 1 - slot, x)).wait_recv()
                pass_x(w).start()

            @pl.when(jnp.logical_not(by_x))
            def _():
                give_x(w, r.x_recv.at[w], landing(w, 1 - slot, 1 - x)).wait_recv()
                pass_y(w).start()

    def finish_pieces():
        both = PIECES - SETS
        some = SETS + both // 2
        got = both // 2 + SETS
        pl.when(high_z)(lambda: remote(r.own, r.up_in, r.bulk.at[0], r.bulk.at[0], up).wait_send())
        pl.when(low_z)(lambda: remote(r.own, r.down_in, r.bulk.at[1], r.bulk.at[1], down).wait_send())
        pltpu.make_async_copy(r.fin, r.own, r.bulk.at[2]).wait()
        for i, count in ((3, some), (4, some), (5, SETS // 2), (6, SETS // 2)):
            remote(r.fin.at[0:count], r.own.at[0:count], r.bulk.at[i], r.bulk.at[i], xn).wait_send()
        for i in (7, 8):
            remote(r.fin.at[0:got], r.own.at[0:got], r.bulk.at[i], r.bulk.at[i], xn).wait_recv()

    far_half = (1 - x, 1 - y)
    near_half = (x, y)
    quarter = (x * 2 + y, 4 + y * 2 + x)
    near, next_near = (xn, yn), (yn, xn)

    def cols(j, n):
        return many(j * 256, 256 * n, 256)

    def ar(i, src, dst, target):
        return remote(src, dst, r.ar_send.at[i], r.ar_recv.at[i], target)

    def ar_one(s):
        return ar(s, r.total.at[:, cols(4 * s + 2 * far_half[s], 2)], r.part_in.at[s], near[s])

    def ar_two(s):
        give = 4 * s + 2 * near_half[s] + (1 - near_half[1 - s])
        return ar(2 + s, r.total.at[:, cols(give, 1)], r.part_in.at[2 + s, :, 0:256], next_near[s])

    def ar_up(s):
        return ar(4 + s, r.z_out.at[s], r.z_in.at[s], up)

    def ar_down(s):
        return ar(6 + s, r.z_out.at[2 + s], r.z_in.at[2 + s], down)

    def ar_four(s):
        piece = r.final.at[:, cols(quarter[s], 1)]
        return ar(8 + s, piece, piece, next_near[s])

    def ar_four_got(s):
        piece = r.final.at[:, cols(4 * s + 2 * near_half[s] + (1 - near_half[1 - s]), 1)]
        return ar(8 + s, piece, piece, next_near[s])

    def ar_five(s):
        piece = r.final.at[:, cols(4 * s + 2 * near_half[s], 2)]
        return ar(10 + s, piece, piece, near[s])

    def ar_five_got(s):
        piece = r.final.at[:, cols(4 * s + 2 * far_half[s], 2)]
        return ar(10 + s, piece, piece, near[s])

    def add_into(ref, other_part):
        ref[...] = half(ref[...].astype(F32) + other_part.astype(F32))

    def ar_stage1():
        for s in range(2):
            ar_one(s).start()

    def ar_stage2():
        for s in range(2):
            ar_one(s).wait()
            add_into(r.total.at[:, cols(4 * s + 2 * near_half[s], 2)], r.part_in[s])
            ar_two(s).start()

    def ar_stage3():
        for s in range(2):
            ar_two(s).wait()
            add_into(r.total.at[:, cols(quarter[s], 1)], r.part_in[2 + s, :, 0:256])

            @pl.when(z == 0)
            def _():
                r.z_out[s] = r.total[:, cols(quarter[s], 1)]
                ar_up(s).start()

            @pl.when(z == zs - 1)
            def _():
                r.z_out[2 + s] = r.total[:, cols(quarter[s], 1)]
                ar_down(s).start()

    def ar_stage_z(k):
        for s in range(2):
            @pl.when(z == k)
            def _():
                ar_up(s).wait_recv()
                if k < zs - 1:
                    r.z_out[s] = half(r.total[:, cols(quarter[s], 1)].astype(F32) + r.z_in[s].astype(F32))
                    ar_up(s).start()

            @pl.when(z == zs - 1 - k)
            def _():
                ar_down(s).wait_recv()
                if k < zs - 1:
                    r.z_out[2 + s] = half(r.total[:, cols(quarter[s], 1)].astype(F32) + r.z_in[2 + s].astype(F32))
                    ar_down(s).start()

    def ar_stage4():
        for s in range(2):
            lower = jnp.where(low_z, r.z_in[s].astype(F32), 0.0)
            upper = jnp.where(high_z, r.z_in[2 + s].astype(F32), 0.0)
            own = r.total[:, cols(quarter[s], 1)].astype(F32)
            r.final[:, cols(quarter[s], 1)] = half(own + lower + upper)
            ar_four(s).start()

    def ar_stage5():
        for s in range(2):
            ar_four_got(s).wait_recv()
            ar_five(s).start()

    def ar_stage6():
        for s in range(2):
            ar_five_got(s).wait_recv()
            ar_four(s).wait_send()
            ar_five(s).wait_send()
            pl.when(high_z)(lambda s=s: ar_up(s).wait_send())
            pl.when(low_z)(lambda s=s: ar_down(s).wait_send())

    stages_at = {4: ar_stage2, 5: ar_stage3}

    def slice_step(s, _):
        e, start, _, _ = where_from(s * PER, slot, x)
        hs = many(start, SLICE, SLICE)
        wi = half(r.win[e, :, hs].astype(F32).T)
        wo = r.wout[e, hs, :]
        bias = jnp.broadcast_to(r.binf[pl.ds(e, 1), hs], (128, SLICE)).T[:, 0:1]
        n, co, g = r.n_all[...], r.c_all[...], r.g_all[pl.ds(e, 1), :]
        hid, slope = gelu_parts(dot_nt(wi, n) + bias)
        dh = dot_nt(wo, co)
        for kind, grad in ((0, dot(half(slope * (dh * g)), n)), (1, dot(half(hid * g), co))):
            for i in range(SLICE // PIECE):
                r.own[s * PER + i * 2 + kind] = half(grad[i * PIECE:(i + 1) * PIECE, :])
        for at, todo in stages_at.items():
            pl.when(s == at)(todo)
        for k in range(TICKS):
            pl.when(s < EARLY)(lambda k=k: tick(s * TICKS + k))
        for k in range(LATER):
            pl.when(s >= EARLY)(lambda k=k: tick(middle + (s - EARLY) * LATER + k))
        return 0

    middle = EARLY * TICKS + sum(BEATS)
    assert middle <= EARLY * PER

    lax.fori_loop(0, EARLY, slice_step, 0)
    clock, beats = iter(range(EARLY * TICKS, middle)), iter(BEATS)

    def beat():
        for _ in range(next(beats)):
            tick(next(clock))


    expert_pass(1, beat)
    beat()
    theirs, ours = many((1 - c) * BLOCK, BLOCK, 8), many(c * BLOCK, BLOCK, 8)
    partials = [remote(src.at[theirs, :], dst, r.p_send.at[i], r.p_recv.at[i], partner) for i, (src, dst) in enumerate(
        ((r.running, r.got_running), (r.drows, r.got_drows), (r.dgate, r.got_dgate)))]
    for copy in partials:
        copy.start()
    beat()
    for copy in partials:
        copy.wait()

    r.out[...] = half(r.mid[0:BLOCK, :] + (r.running[ours, :] + r.got_running[...]))[0:tokens, :]
    zeros = jnp.zeros((ROWS - BLOCK, 128), F32)
    d_gates = jnp.concatenate([r.dgate[ours, :] + r.got_dgate[...], zeros], axis=0)
    rprobs, chosen = r.rprobs[...], r.chosen[...]
    d_probs = d_gates * chosen
    d_logits = half(rprobs * (d_probs - jnp.sum(rprobs * d_probs, axis=-1, keepdims=True)))
    r.dn[0:BLOCK, :] = r.drows[ours, :] + r.got_drows[...]
    r.dn[BLOCK:ROWS, :] = jnp.zeros((ROWS - BLOCK, 512), F32)
    beat()
    dn = r.dn[...] + dot(d_logits, route_t)
    xhat = r.xhat2[...]
    n2 = half(xhat * gain2 + bias2)
    grad_route = dot(half(d_logits.astype(F32).T), n2)
    vector_rows = {5: column_sum(dn * xhat), 6: column_sum(dn)}
    r.xs[...] = jnp.zeros_like(r.xs)
    r.xs[0:tokens, :] = r.cot[...].astype(F32)
    d_middle = r.xs[...] + norm_back(dn, xhat, spread2, gain2)
    r.mid[...] = d_middle
    r.db[...] = half(d_middle)
    db = r.db[...]
    vector_rows[4] = column_sum(db.astype(F32))
    r.dense[:, 1536:2048] = half(dot(half(r.ctx[...].astype(F32).T), db))
    r.dctx[...] = half(dot_nt(db, r.wproj[...]))
    beat()

    def heads_back(i, _):
        q, k, v = [r.mixed[:, many(base + 128 * i, 128, 128)] for base in (0, 512, 1024)]
        q = q * BF16(HEAD_DIM ** -0.5)
        do = r.dctx[:, many(128 * i, 128, 128)]
        parts = []
        for h in range(2):
            p = r.probs[2 * i + h]
            dp = dot_nt(jnp.where(low_lane == (h == 0), do, jnp.zeros_like(do)), v)
            ds = p * (dp - jnp.sum(p * dp, axis=-1, keepdims=True))
            parts.append((dot(half(ds), k) * HEAD_DIM ** -0.5, dot(half(ds.T), q), dot(half(p.T), do)))
        for j, base in enumerate((0, 512, 1024)):
            r.dmixed[:, many(base + 128 * i, 128, 128)] = half(jnp.where(low_lane, parts[0][j], parts[1][j]))
        return 0

    beat()
    lax.fori_loop(0, 4, heads_back, 0)
    beat()
    n1_t = half(r.n1[...].astype(F32).T)
    dn = 0.0
    for i in range(3):
        part = r.dmixed[:, 512 * i:512 * (i + 1)]
        if i != 1:
            vector_rows[2 + i // 2] = column_sum(part.astype(F32))
        r.dense[:, 512 * i:512 * (i + 1)] = half(dot(n1_t, part))
        dn = dn + dot_nt(part, r.wqkv[:, 512 * i:512 * (i + 1)])
        beat()
    xhat = r.xhat1[...]
    vector_rows[0] = column_sum(dn * xhat)
    vector_rows[1] = column_sum(dn)
    r.igrad[...] = (r.mid[...] + norm_back(dn, xhat, spread1, gain1))[0:tokens, :]

    vectors = jnp.concatenate([grad_route[0:4, :]] + [vector_rows[i] for i in range(7)] + [jnp.zeros((5, 512), F32)], axis=0)
    r.dn[0:16, :] = vectors
    low_half, high_half = r.dn[0:16, 0:256], r.dn[0:16, 256:512]
    r.extra[1, :, 0:256] = jnp.where(c == 0, high_half, low_half)
    own_half = jnp.where(c == 0, low_half, high_half)
    swaps = [remote(r.dense.at[other, :], r.dense_in, r.d_send.at[0], r.d_recv.at[0], partner),
             remote(r.extra.at[1], r.extra.at[2], r.d_send.at[1], r.d_recv.at[1], partner)]
    for copy in swaps:
        copy.start()
    for copy in swaps:
        copy.wait()
    r.total[0:256, :] = half(r.dense[mine, :].astype(F32) + r.dense_in[...].astype(F32))
    sums = own_half + r.extra[2, :, 0:256]
    small = jnp.concatenate([r.extra[0, 0:4, :], jnp.zeros((12, 2048), F32)], axis=0)
    shifted = jnp.concatenate([jnp.zeros((4, 256), F32), sums[0:12, :]], axis=0)
    r.total[256:272, :] = half(small + jnp.concatenate([shifted, jnp.zeros((16, 1792), F32)], axis=1))

    ar_stage1()

    lax.fori_loop(EARLY, STEPS, slice_step, 0)
    start, ends = middle + (STEPS - EARLY) * LATER, PIECES + HOP * (zs - 1)
    stages = {0: lambda: ar_stage_z(1), 3: lambda: ar_stage_z(2), 6: lambda: ar_stage_z(3), 8: ar_stage4, 11: ar_stage5}

    def last_ticks(t, _):
        for at, stage in stages.items():
            pl.when(t == start + at)(stage)
        tick(t)
        return 0

    lax.fori_loop(start, ends, last_ticks, 0)
    ar_stage6()
    finish_pieces()
    for g in gathers:
        g.drain()
    for i in range(4):
        count_copy(min(i, 1), i, 0, partner).wait_send()
    for k in range(1, zs):
        pl.when(z < k)(lambda k=k: count_copy(2, 3 + k, 0, partner).wait_send())


def block_call(zs, *args):
    tokens, width = args[0].shape
    vm, hbm = pl.BlockSpec(memory_space=pltpu.VMEM), pl.BlockSpec(memory_space=pl.ANY)
    shape = jax.ShapeDtypeStruct
    in_specs = [hbm if name in ("win_in", "wout_in") else vm for name in INPUTS]
    scratch = [pltpu.VMEM(dims, dtype) for _, dims, dtype in SCRATCH]
    scratch += [pltpu.SemaphoreType.DMA(dims) for _, dims in SEMS]
    return pl.pallas_call(
        functools.partial(block_kernel, zs),
        out_shape=(shape((tokens, width), BF16), shape((tokens, width), F32), shape((4, 2048, 512), BF16), shape((272, 2048), BF16)),
        in_specs=in_specs,
        out_specs=(vm, vm, hbm, vm),
        scratch_shapes=scratch,
        compiler_params=pltpu.CompilerParams(collective_id=0, has_side_effects=True, vmem_limit_bytes=63 << 20),
        name="encoder_block",
    )(*args)


def finish_kernel(grads, summed, out_in, igrad_in, grad_in, grad_out, qkv, proj, route, bias_in, bias_out, out, igrad, *rest):
    vectors, (got, done_in, done_out, got_sem, done_sem) = rest[:7], rest[7:]
    n = done_in.shape[0]

    def source(k, i):
        return pltpu.make_async_copy(
            grads.at[2 * k + i // 4, many(lax.rem(i, 4) * STEP, STEP, STEP), :], got.at[k * n + i], got_sem.at[k * n + i])

    def results(i):
        where = many(lax.rem(i, 4) * STEP, STEP, STEP)
        return (pltpu.make_async_copy(done_in.at[i], grad_in.at[i // 4, :, where], done_sem.at[i]),
                pltpu.make_async_copy(done_out.at[i], grad_out.at[i // 4, where, :], done_sem.at[n + i]))

    def fetch(i, _):
        source(1, i).start()
        source(0, i).start()
        return 0

    lax.fori_loop(0, n, fetch, 0)
    qkv[...] = summed[0:256, 0:1536].astype(F32)
    proj[...] = summed[0:256, 1536:2048].astype(F32)
    rows = summed[256:272, :].astype(F32)
    bias_in[...] = rows[0:2, :]
    bias_out[...] = rows[2:4, 0:512]
    route[...] = rows[4:8, 0:256]
    for i, ref in enumerate(vectors):
        ref[...] = rows[8 + i, 0:256]
    out[...] = out_in[...]
    igrad[...] = igrad_in[...]

    def convert(i, _):
        to_in, to_out = results(i)
        source(1, i).wait()
        done_out[i] = got[n + i].astype(F32)
        to_out.start()
        source(0, i).wait()
        done_in[i] = got[i].astype(F32).T
        to_in.start()
        return 0

    lax.fori_loop(0, n, convert, 0)

    def settle(i, _):
        for copy in results(i):
            copy.wait()
        return 0

    lax.fori_loop(0, n, settle, 0)


def finish(grads, summed, out, igrad):
    shape = jax.ShapeDtypeStruct
    vm, hbm = pl.BlockSpec(memory_space=pltpu.VMEM), pl.BlockSpec(memory_space=pl.ANY)
    small = [shape((256, 1536), F32), shape((256, 512), F32), shape((4, 256), F32), shape((2, 2048), F32), shape((2, 512), F32),
             shape(out.shape, out.dtype), shape(igrad.shape, igrad.dtype)] + [shape((256,), F32)] * 7
    n = 8
    return pl.pallas_call(
        finish_kernel,
        out_shape=[shape((2, 512, 2048), F32), shape((2, 2048, 512), F32)] + small,
        in_specs=[hbm, vm, vm, vm],
        out_specs=[hbm, hbm] + [vm] * len(small),
        scratch_shapes=[
            pltpu.VMEM((2 * n, STEP, 512), BF16), pltpu.VMEM((n, 512, STEP), F32), pltpu.VMEM((n, STEP, 512), F32),
            pltpu.SemaphoreType.DMA((2 * n,)), pltpu.SemaphoreType.DMA((2 * n,)),
        ],
        compiler_params=pltpu.CompilerParams(vmem_limit_bytes=60 << 20),
        name="finish",
    )(grads, summed, out, igrad)


def swap(v):
    return lax.ppermute(v, "shard", [(0, 1), (1, 0)])


def fused(inputs, norm1_gain, norm1_bias, qkv_weight, query_bias, value_bias, out_weight, out_bias, norm2_gain, norm2_bias,
          router_weight, noise, expert_in, expert_in_bias, expert_out, expert_out_bias, routes, priority, cotangent):
    out, igrad, grads, summed = block_call(
        lax.axis_size("replica") // 4, inputs, cotangent, noise.T, routes.T, priority, norm1_gain, norm1_bias, query_bias,
        value_bias, out_bias, norm2_gain, norm2_bias, router_weight.T, qkv_weight, out_weight, expert_in, expert_out,
        expert_in_bias, expert_out_bias)
    grad_in, grad_out, qkv, proj, route, bias_in, bias_out, out, igrad, *cols = finish(grads, summed, out, igrad)
    return (out, igrad, cols[0], cols[1], qkv, cols[2], cols[3], proj, cols[4], cols[5], cols[6], route.T,
            grad_in, bias_in, grad_out, bias_out)


def layer_norm(values, gain_vector, bias_vector):
    centered = values - jnp.mean(values, axis=-1, keepdims=True)
    spread = lax.rsqrt(jnp.mean(centered * centered, axis=-1, keepdims=True) + LN_EPS)
    return centered * spread * gain_vector + bias_vector


def kept_gates(pair_expert, ranks, offsets, capacity, expert_count):
    same = pair_expert[:, None] == pair_expert[None, :]
    earlier = ranks[None, :] < ranks[:, None]
    before = jnp.sum(jnp.where(same & earlier, 1, 0).astype(jnp.int32), axis=1)
    onehot = pair_expert[:, None] == jnp.arange(expert_count, dtype=jnp.int32)[None, :]
    first_slot = jnp.sum(jnp.where(onehot, offsets[None, :], 0).astype(jnp.int32), axis=1)
    keep = before + first_slot < capacity
    picked = jnp.where(onehot & keep[:, None], 1.0, 0.0).astype(jnp.float32)
    return jnp.sum(picked.reshape(-1, 2, expert_count), axis=1)


def general(
    inputs, norm1_gain, norm1_bias, qkv_weight, query_bias, value_bias, out_weight, out_bias, norm2_gain, norm2_bias,
    router_weight, noise, expert_in, expert_in_bias, expert_out, expert_out_bias, routes, priority, cotangent,
):
    tok_count, width = inputs.shape
    replicas, cores = lax.axis_size("replica"), lax.axis_size("shard")
    shard = lax.axis_index("shard")
    images = tok_count // PATCHES
    heads = width // HEAD_DIM
    owned, _, hidden_count = expert_in.shape
    expert_count = owned * cores
    score_scale = HEAD_DIM ** (-0.5)
    f32 = jnp.float32

    vectors = (norm1_gain, norm1_bias, query_bias, value_bias, out_bias, norm2_gain, norm2_bias)
    packed = jnp.concatenate(
        [qkv_weight, out_weight, jnp.stack(vectors, axis=1), router_weight], axis=1)
    packed = lax.all_gather(packed, "shard", axis=0, tiled=True)
    weight_qkv = packed[:, :3 * width]
    weight_proj = packed[:, 3 * width:4 * width]
    small = packed[:, 4 * width:]
    gain_one, bias_one, bias_query, bias_value, bias_proj, gain_two, bias_two = [
        small[:, i].astype(f32) for i in range(len(vectors))]
    weight_route = small[:, len(vectors):]

    pair_expert = routes.reshape(-1)
    onehot_pairs = (pair_expert[:, None] == jnp.arange(expert_count, dtype=jnp.int32)[None, :]).astype(jnp.int32)
    load = jnp.sum(onehot_pairs, axis=0)
    loads = lax.all_gather(load, ("replica", "shard"))
    position = lax.axis_index("replica") * cores + shard
    ahead = jnp.arange(replicas * cores)[:, None] < position
    offsets = jnp.sum(jnp.where(ahead, loads, 0), axis=0)
    capacity = 2 * tok_count * replicas * cores // expert_count
    chosen = kept_gates(pair_expert, priority.reshape(-1), offsets, capacity, expert_count)

    residual_in = inputs.astype(f32)
    normed_one, norm_one_back = jax.vjp(layer_norm, residual_in, gain_one, bias_one)
    normed_one_half = half(normed_one)
    qkv_bias = jnp.concatenate([bias_query, jnp.zeros_like(bias_query), bias_value])
    mixed = half(dot(normed_one_half, weight_qkv) + qkv_bias)
    shaped = mixed.reshape(images, PATCHES, 3, heads, HEAD_DIM)
    query, keys, values = (shaped[:, :, 0], shaped[:, :, 1], shaped[:, :, 2])
    scores = jnp.einsum("bqhd,bkhd->bhqk", query, keys, preferred_element_type=f32) * score_scale
    row_max = jnp.max(scores, axis=-1, keepdims=True)
    log_total = row_max + jnp.log(jnp.sum(jnp.exp(scores - row_max), axis=-1, keepdims=True))
    context = jnp.einsum(
        "bhqk,bkhd->bqhd", half(jnp.exp(scores - log_total)), values, preferred_element_type=f32)
    context_half = half(context.reshape(tok_count, width))
    middle = residual_in + (dot(context_half, weight_proj) + bias_proj)
    normed_two, norm_two_back = jax.vjp(layer_norm, middle, gain_two, bias_two)
    normed_two_half = half(normed_two)
    logits = dot(normed_two_half, weight_route) + noise
    route_probs = jax.nn.softmax(logits, axis=-1)
    gate_weights = route_probs * chosen
    upstream = cotangent.astype(f32)

    pair_n = jnp.concatenate([normed_two_half, swap(normed_two_half)], axis=0)
    pair_c = jnp.concatenate([cotangent, swap(cotangent)], axis=0)
    own_gates = lax.dynamic_slice_in_dim(gate_weights, shard * owned, owned, 1)
    other_gates = swap(lax.dynamic_slice_in_dim(gate_weights, (1 - shard) * owned, owned, 1))
    pair_g = jnp.concatenate([own_gates, other_gates], axis=0)
    pair_up = pair_c.astype(f32)
    running = jnp.zeros((2 * tok_count, width), f32)
    d_rows = jnp.zeros((2 * tok_count, width), f32)
    gate_columns, bias_in_grads, bias_out_grads, in_grads, out_grads = [], [], [], [], []
    for e in range(owned):
        gate = pair_g[:, e:e + 1]
        pre = dot(pair_n, expert_in[e]) + expert_in_bias[e].astype(f32)
        act, slope = gelu_parts(pre)
        hid = half(act)
        result = dot(hid, expert_out[e]) + expert_out_bias[e].astype(f32)
        running = running + gate * result
        gate_columns.append(jnp.sum(pair_up * result, axis=1))
        d_result = half(gate * pair_up)
        d_pre = half(slope * dot_nt(d_result, expert_out[e]))
        d_rows = d_rows + dot_nt(d_pre, expert_in[e])
        bias_in_grads.append(jnp.sum(d_pre.astype(f32), axis=0))
        bias_out_grads.append(jnp.sum(d_result.astype(f32), axis=0))
        in_grads.append(jnp.einsum("td,th->dh", pair_n, d_pre, preferred_element_type=f32))
        out_grads.append(jnp.einsum("th,td->hd", hid, d_result, preferred_element_type=f32))
    d_gate_part = jnp.stack(gate_columns, axis=1)
    running = running[:tok_count] + swap(running[tok_count:])
    d_normed = d_rows[:tok_count] + swap(d_rows[tok_count:])
    d_gate_other = swap(d_gate_part[tok_count:])
    d_gate_own = d_gate_part[:tok_count]
    d_gates = jnp.where(shard == 0, jnp.concatenate([d_gate_own, d_gate_other], axis=1),
                        jnp.concatenate([d_gate_other, d_gate_own], axis=1))

    grad_in = lax.psum(half(jnp.stack(in_grads, axis=0)), "replica")
    grad_out = lax.psum(half(jnp.stack(out_grads, axis=0)), "replica")

    output = half(middle + running)
    d_probs = d_gates * chosen
    d_logits = half(route_probs * (d_probs - jnp.sum(route_probs * d_probs, axis=-1, keepdims=True)))
    grad_route = jnp.einsum("td,te->de", normed_two_half, d_logits, preferred_element_type=f32)
    d_normed = d_normed + dot_nt(d_logits, weight_route)
    d_middle, grad_gain_two, grad_bias_two = norm_two_back(d_normed)
    d_middle = d_middle + upstream
    d_branch = half(d_middle)
    grad_proj = jnp.einsum("tc,td->cd", context_half, d_branch, preferred_element_type=f32)
    grad_proj_bias = jnp.sum(d_branch.astype(f32), axis=0)
    d_context = half(dot_nt(d_branch, weight_proj)).reshape(images, PATCHES, heads, HEAD_DIM)
    attn_probs = jnp.exp(scores - log_total)
    d_attn = jnp.einsum("bqhd,bkhd->bhqk", d_context, values, preferred_element_type=f32)
    d_values = jnp.einsum("bhqk,bqhd->bkhd", half(attn_probs), d_context, preferred_element_type=f32)
    d_scores = half(attn_probs * (d_attn - jnp.sum(attn_probs * d_attn, axis=-1, keepdims=True)))
    d_query = jnp.einsum("bhqk,bkhd->bqhd", d_scores, keys, preferred_element_type=f32) * score_scale
    d_keys = jnp.einsum("bhqk,bqhd->bkhd", d_scores, query, preferred_element_type=f32) * score_scale
    d_mixed = half(jnp.stack([d_query, d_keys, d_values], axis=2).reshape(tok_count, 3 * width))
    grad_qkv = jnp.einsum("td,tf->df", normed_one_half, d_mixed, preferred_element_type=f32)
    mixed_sums = jnp.sum(d_mixed.astype(f32), axis=0)
    d_normed_one = dot_nt(d_mixed, weight_qkv)
    d_input, grad_gain_one, grad_bias_one = norm_one_back(d_normed_one)
    input_grad = d_input + d_middle

    columns = jnp.stack((grad_gain_one, grad_bias_one, mixed_sums[:width], mixed_sums[2 * width:], grad_proj_bias,
                         grad_gain_two, grad_bias_two), axis=1)
    dense = half(jnp.concatenate([grad_qkv, grad_proj, columns, grad_route], axis=1))
    mine = width // 2
    keep = lax.dynamic_slice_in_dim(dense, shard * mine, mine, 0)
    give = lax.dynamic_slice_in_dim(dense, (1 - shard) * mine, mine, 0)
    dense = keep.astype(f32) + swap(give).astype(f32)
    bias_row = jnp.concatenate(bias_in_grads + bias_out_grads)
    summed, bias_row = lax.psum((half(dense), bias_row), "replica")
    summed = summed.astype(f32)
    columns = [summed[:, 4 * width + i] for i in range(len(vectors))]
    grad_in_bias = bias_row[:owned * hidden_count].reshape(owned, hidden_count)
    grad_out_bias = bias_row[owned * hidden_count:].reshape(owned, width)
    return (
        output, input_grad, columns[0], columns[1], summed[:, :3 * width], columns[2], columns[3],
        summed[:, 3 * width:4 * width], columns[4], columns[5], columns[6], summed[:, 4 * width + len(vectors):],
        grad_in.astype(f32), grad_in_bias, grad_out.astype(f32), grad_out_bias,
    )


def on_device(*args):
    expert_in, inputs = args[12], args[0]
    planes = lax.axis_size("replica") == 16 and lax.axis_size("shard") == 2
    if planes and inputs.shape == (PATCHES, 512) and expert_in.shape == (2, 512, 2048):
        return fused(*args)
    return general(*args)


def solution(mesh):
    both, split = ("replica", "shard"), "shard"
    return jax.shard_map(
        on_device,
        mesh=mesh,
        in_specs=(
            P(both, None), P(split), P(split), P(split, None), P(split), P(split), P(split, None), P(split), P(split),
            P(split), P(split, None), P(both, None), P(split, None, None), P(split, None), P(split, None, None),
            P(split, None), P(both, None), P(both, None), P(both, None),
        ),
        out_specs=(
            P(both, None), P(both, None), P(split), P(split), P(split, None), P(split), P(split), P(split, None),
            P(split), P(split), P(split), P(split, None), P(split, None, None), P(split, None), P(split, None, None),
            P(split, None),
        ),
        check_vma=False,
    )
```

```python
import functools
from types import SimpleNamespace

import jax
import jax.numpy as jnp
from jax import lax
from jax.experimental import pallas as pl
from jax.experimental.pallas import tpu as pltpu
from jax.sharding import PartitionSpec as P

HEAD_DIM = 64
PATCHES = 197
LN_EPS = 1e-06
MESH = pl.DeviceIdType.MESH
NT = (((1,), (1,)), ((), ()))
GELU_K = 0.7978845608028654
GELU_A = 0.044715
F32 = jnp.float32
BF16 = jnp.bfloat16
ROWS = 256
LATE = 192
BLOCK = 208
STEP = 512
SLICE = 256
PIECE = 128
STEPS = 6
PER = 2 * SLICE // PIECE
PIECES = STEPS * PER
SETS = 2 * PER
HOP = 3
TICKS, LATER = 1, 2
EARLY = 3
BEATS = (1, 1, 1, 1, 1, 0, 1, 1, 0, 1)
PASS = 4


def half(values):
    return values.astype(BF16)


def dot(a, b):
    return jnp.dot(a, b, preferred_element_type=F32)


def dot_nt(a, b):
    return lax.dot_general(a, b, NT, preferred_element_type=F32)


def gelu_parts(x):
    x2 = x * x
    q = 0.5 + 0.5 * jnp.tanh(x * (GELU_K + (GELU_K * GELU_A) * x2))
    h = x * q
    return h, q + (h * (1.0 - q)) * (2 * GELU_K + (6 * GELU_K * GELU_A) * x2)


def iota(shape, dim):
    return lax.broadcasted_iota(jnp.int32, shape, dim)


def many(start, size, unit):
    return pl.ds(pl.multiple_of(start, unit), size)


def normalize(v):
    centered = v - jnp.mean(v, axis=-1, keepdims=True)
    spread = lax.rsqrt(jnp.mean(centered * centered, axis=-1, keepdims=True) + LN_EPS)
    return centered * spread, spread


def norm_back(d, xhat, spread, gain):
    dx = d * gain
    return spread * (dx - jnp.mean(dx, axis=-1, keepdims=True) - xhat * jnp.mean(dx * xhat, axis=-1, keepdims=True))


def column_sum(v):
    return jnp.sum(v, axis=0, keepdims=True)


def place():
    r = lax.axis_index("replica")
    return r // 4, (r // 2) % 2, r % 2, lax.axis_index("shard")


def rep(z, y, x):
    return (z * 2 + y) * 2 + x


class PlaneGather:
    def __init__(self, x_first, rows, at, sems):
        self.rows, self.at = rows, at
        self.send, self.recv, self.core_send, self.core_recv = sems
        z, y, x, c = place()
        near = ((rep(z, y, 1 - x), c), (rep(z, 1 - y, x), c))
        spots = (y * 2 + 1 - x, (1 - y) * 2 + x)
        self.targets = near if x_first else near[::-1]
        self.first, self.second = spots if x_first else spots[::-1]
        self.me, self.diagonal = y * 2 + x, (1 - y) * 2 + 1 - x
        self.core, self.partner = c, (rep(z, y, x), 1 - c)

    def ref(self, spot, core):
        first, size = self.at
        return self.rows.at[many((spot * 2 + core) * BLOCK + first, size, 16), :]

    def link(self, kind, spot):
        ref = self.ref(spot, self.core)
        return remote(ref, ref, self.send.at[kind, spot], self.recv.at[spot], self.targets[kind])

    def across(self, spot, core=None):
        ref = self.ref(spot, self.core if core is None else core)
        return remote(ref, ref, self.core_send.at[spot], self.core_recv.at[spot], self.partner)

    def begin(self, kind):
        self.link(kind, self.me).start()

    def hand(self):
        self.across(self.me).start()

    def turn(self):
        self.link(0, self.first).wait_recv()
        self.link(1, self.first).start()
        self.across(self.first).start()

    def far(self):
        for spot in (self.second, self.diagonal):
            self.link(0, spot).wait_recv()
            self.across(spot).start()

    def from_core(self, spot):
        self.across(spot, 1 - self.core).wait_recv()

    def drain(self):
        for kind, spot in ((0, self.me), (1, self.me), (1, self.first)):
            self.link(kind, spot).wait_send()
        for spot in range(4):
            self.across(spot).wait_send()


class Halves:
    def __init__(self, rows, sems):
        cuts = ((0, 96), (96, LATE - 96), (LATE, BLOCK - LATE))
        self.parts = [PlaneGather(m == 0, rows, cuts[m], [ref.at[m] for ref in sems]) for m in range(3)]

    def begin(self, parts=slice(0, 3)):
        for part in self.parts[parts]:
            part.begin(0)
        for part in self.parts[parts]:
            part.hand()
        for part in self.parts[parts]:
            part.begin(1)

    def turn(self, parts=slice(0, 3)):
        for part in self.parts[parts]:
            part.turn()

    def far(self):
        for part in self.parts:
            part.far()

    def from_core(self, spot):
        for part in self.parts:
            part.from_core(spot)

    def others(self):
        part = self.parts[0]
        return part.first, part.second, part.diagonal

    def drain(self):
        for part in self.parts:
            part.drain()


SCRATCH = (
    ("n_all", (8 * BLOCK, 512), BF16), ("c_all", (8 * BLOCK, 512), BF16), ("g_all", (8, 8 * BLOCK), F32),
    ("wqkv", (512, 1536), BF16), ("wproj", (512, 512), BF16), ("vec", (2, 16, 256), F32), ("binf", (2, 2048), F32),
    ("win", (2, 512, 2048), BF16), ("wout", (2, 2048, 512), BF16),
    ("count_out", (3, 8, 128), F32), ("count_in", (9, 8, 128), F32),
    ("xs", (ROWS, 512), F32), ("pairs", (16, ROWS), F32),
    ("xhat1", (ROWS, 512), F32), ("n1", (ROWS, 512), BF16), ("mixed", (ROWS, 1536), BF16),
    ("probs", (8, ROWS, ROWS), F32), ("ctx", (ROWS, 512), BF16), ("mid", (ROWS, 512), F32), ("xhat2", (ROWS, 512), F32),
    ("chosen", (ROWS, 128), F32), ("rprobs", (ROWS, 128), F32),
    ("res", (2 * BLOCK, 512), F32), ("running", (2 * BLOCK, 512), F32), ("drows", (2 * BLOCK, 512), F32),
    ("dgate", (2 * BLOCK, 128), F32), ("dres", (2 * BLOCK, 512), BF16), ("gcol", (2 * BLOCK, 128), F32),
    ("got_running", (BLOCK, 512), F32), ("got_drows", (BLOCK, 512), F32), ("got_dgate", (BLOCK, 128), F32),
    ("db", (ROWS, 512), BF16), ("dctx", (ROWS, 512), BF16), ("dmixed", (ROWS, 1536), BF16), ("dn", (ROWS, 512), F32),
    ("dense", (512, 2048), BF16), ("dense_in", (256, 2048), BF16), ("extra", (3, 16, 2048), F32),
    ("total", (272, 2048), BF16), ("part_in", (4, 272, 512), BF16), ("z_out", (4, 272, 256), BF16), ("z_in", (4, 272, 256), BF16),
    ("own", (PIECES, PIECE, 512), BF16), ("up_in", (PIECES, PIECE, 512), BF16), ("up_out", (PIECES, PIECE, 512), BF16),
    ("down_in", (PIECES, PIECE, 512), BF16), ("down_out", (PIECES, PIECE, 512), BF16), ("fin", (PIECES, PIECE, 512), BF16),
)
SEMS = (
    ("g_send", (2, 3, 2, 4)), ("g_recv", (2, 3, 4)), ("g_csend", (2, 3, 4)), ("g_crecv", (2, 3, 4)),
    ("load", (4,)), ("w_send", (3,)), ("w_recv", (3,)), ("count_send", (7,)), ("count_recv", (9,)),
    ("p_send", (3,)), ("p_recv", (3,)), ("d_send", (2,)), ("d_recv", (2,)),
    ("ar_send", (12,)), ("ar_recv", (12,)), ("up_recv", (PIECES,)), ("down_recv", (PIECES,)), ("bulk", (9,)),
    ("x_recv", (SETS,)), ("y_recv", (SETS,)),
)
INPUTS = ("x", "cot", "noise_in", "routes_in", "prio", "v0", "v1", "v2", "v3", "v4", "v5", "v6", "route_in", "wqkv_in",
          "wproj_in", "win_in", "wout_in", "bin", "bout")
OUTPUTS = ("out", "igrad", "grads", "final")


def remote(src, dst, send, recv, target):
    return pltpu.make_async_remote_copy(
        src_ref=src, dst_ref=dst, send_sem=send, recv_sem=recv, device_id=target, device_id_type=MESH)


def block_kernel(zs, *refs):
    names = INPUTS + OUTPUTS + tuple(n for n, _, _ in SCRATCH) + tuple(n for n, _ in SEMS)
    r = SimpleNamespace(**dict(zip(names, refs, strict=True)))
    z, y, x, c = place()
    me = rep(z, y, x)
    partner = (me, 1 - c)
    xn, yn = (rep(z, y, 1 - x), c), (rep(z, 1 - y, x), c)
    up, down = (rep(z + 1, y, x), c), (rep(z - 1, y, x), c)
    low_z, high_z = z > 0, z < zs - 1
    tokens = r.x.shape[0]
    devices = 8 * zs
    capacity = 2 * tokens * devices // 4

    bar = pltpu.get_barrier_semaphore()
    for d in range(1, zs):
        peer = (rep(lax.rem(z + d, zs), y, x), c)
        pl.semaphore_signal(bar, inc=1, device_id=peer, device_id_type=MESH)
    for peer in (xn, yn, (rep(z, 1 - y, 1 - x), c), partner):
        pl.semaphore_signal(bar, inc=1, device_id=peer, device_id_type=MESH)

    mine, other = many(c * 256, 256, 16), many((1 - c) * 256, 256, 16)
    halves = [pltpu.make_async_copy(r.wqkv_in, r.wqkv.at[mine, :], r.load.at[2]),
              pltpu.make_async_copy(r.wproj_in, r.wproj.at[mine, :], r.load.at[3])]
    loads = [pltpu.make_async_copy(r.win_in, r.win, r.load.at[0]), pltpu.make_async_copy(r.wout_in, r.wout, r.load.at[1])]
    for copy in halves + loads:
        copy.start()

    r.xs[...] = jnp.zeros_like(r.xs)
    r.xs[0:tokens, :] = r.cot[...].astype(F32)
    own_rows = many(((y * 2 + x) * 2 + c) * BLOCK, BLOCK, 16)
    r.c_all[own_rows, :] = half(r.xs[0:BLOCK, :])
    rows = [ref[...].astype(F32).reshape(1, 256) for ref in (r.v0, r.v1, r.v2, r.v3, r.v4, r.v5, r.v6)]
    rows += [jnp.zeros((1, 256), F32), r.route_in[...].astype(F32), jnp.zeros((4, 256), F32)]
    r.vec[c] = jnp.concatenate(rows, axis=0)
    r.binf[...] = r.bin[...].astype(F32)

    lane, row = iota((ROWS, 128), 1), iota((ROWS, 128), 0)
    r.pairs[0:8, :] = jnp.full((8, ROWS), -1.0, F32)
    r.pairs[8:16, :] = jnp.zeros((8, ROWS), F32)
    r.pairs[0:2, 0:tokens] = r.routes_in[...].astype(F32)
    r.pairs[8:12, 0:tokens] = r.noise_in[...]
    by_token = jnp.concatenate([r.pairs[...], jnp.zeros((112, ROWS), F32)], axis=0).T
    experts = [by_token[:, k:k + 1] for k in range(2)]
    noise = pltpu.roll(by_token, 120, 1)
    onehot = [jnp.where(lane.astype(F32) == experts[k], 1.0, 0.0) for k in range(2)]
    count = jnp.broadcast_to(column_sum(onehot[0] + onehot[1]), (8, 128))

    r.count_out[0] = count

    places = iota((ROWS, r.prio.shape[1]), 1) - 2 * iota((ROWS, r.prio.shape[1]), 0)
    ranks = r.prio[...].astype(F32)
    codes = [experts[k] * 1024.0 + jnp.sum(jnp.where(places == k, ranks, 0.0), axis=1, keepdims=True) for k in range(2)]
    codes = [jnp.where(row[:, 0:1] < tokens, code, -1.0) for code in codes]
    code_rows = jnp.where(lane == 0, codes[0], jnp.where(lane == 1, codes[1], 0.0)).T
    before = []
    for k in range(2):
        floor = experts[k] * 1024.0
        seen = 0.0
        for j in range(2):
            others = code_rows[j:j + 1, :]
            seen = seen + jnp.where((others < codes[k]) & (others >= floor), 1.0, 0.0)
        before.append(jnp.sum(seen, axis=1, keepdims=True))

    def count_copy(stage, i, slot, target):
        return remote(r.count_out.at[stage], r.count_in.at[slot], r.count_send.at[i], r.count_recv.at[slot], target)

    spot = y * 2 + x
    column = [(rep(k, y, x), c) for k in range(zs)]

    def counts_to_plane():
        for d in range(1, 4):
            q = lax.rem(spot + d, 4)
            count_copy(1, d, 1 + spot, (rep(z, q // 2, lax.rem(q, 2)), c)).start()

    def counts_up():
        for k in range(1, zs):
            pl.when(z < k)(lambda k=k: count_copy(2, 3 + k, 5 + z, column[k]).start())

    for copy in halves:
        copy.wait()
    pl.semaphore_wait(bar, zs + 3)

    weights = [remote(ref, ref, r.w_send.at[i], r.w_recv.at[i], partner) for i, ref in enumerate(
        (r.vec.at[c], r.wqkv.at[mine, :], r.wproj.at[mine, :]))]
    for copy in weights:
        copy.start()
    gathers = [Halves((r.n_all, r.c_all)[m], (r.g_send.at[m], r.g_recv.at[m], r.g_csend.at[m], r.g_crecv.at[m]))
               for m in range(2)]
    ga, gb = gathers
    gb.begin()
    count_copy(0, 0, 0, partner).start()

    r.xs[0:tokens, :] = r.x[...].astype(F32)
    xhat, spread1 = normalize(r.xs[...])
    r.xhat1[...] = xhat

    count_copy(0, 0, 0, partner).wait_recv()
    ahead = jnp.where(c == 1, 1.0, 0.0) * r.count_in[0]
    count = count + r.count_in[0]
    r.count_out[1] = count
    counts_to_plane()

    weights[0].wait_send()
    remote(r.vec.at[1 - c], r.vec.at[1 - c], r.w_send.at[0], r.w_recv.at[0], partner).wait_recv()
    vec = jnp.concatenate([r.vec[0], r.vec[1]], axis=1)
    gain1, bias1, bias_q, bias_v, bias_p, gain2, bias2 = [vec[i:i + 1, :] for i in range(7)]
    route_rows = jnp.concatenate([vec[8:16, :], jnp.zeros((120, 512), F32)], axis=0)
    route_t, route = half(route_rows), half(route_rows.T)
    r.n1[...] = half(xhat * gain1 + bias1)

    for i, ref in ((1, r.wqkv), (2, r.wproj)):
        weights[i].wait_send()
        ref = ref.at[other, :]
        remote(ref, ref, r.w_send.at[i], r.w_recv.at[i], partner).wait_recv()
    for i, bias in enumerate((bias_q, None, bias_v)):
        part = dot(r.n1[...], r.wqkv[:, 512 * i:512 * (i + 1)])
        r.mixed[:, 512 * i:512 * (i + 1)] = half(part if bias is None else part + bias)

    for q in range(4):
        pl.when(spot != q)(lambda q=q: count_copy(1, 1, 1 + q, partner).wait_recv())
    for q in range(4):
        ahead = ahead + jnp.where(spot > q, r.count_in[1 + q], 0.0)
        count = count + jnp.where(spot != q, r.count_in[1 + q], 0.0)
    r.count_out[2] = count
    counts_up()

    gb.turn()

    low_lane = lane < HEAD_DIM
    key_kept = iota((ROWS, ROWS), 1) < tokens

    def heads_forward(i, _):
        q, k, v = [r.mixed[:, many(base + 128 * i, 128, 128)] for base in (0, 512, 1024)]
        q = q * BF16(HEAD_DIM ** -0.5)
        parts = []
        for h in range(2):
            s = dot_nt(jnp.where(low_lane == (h == 0), q, jnp.zeros_like(q)), k)
            s = jnp.where(key_kept, s, -1e30)
            e = jnp.exp(s - jnp.max(s, axis=-1, keepdims=True))
            p = e / jnp.sum(e, axis=-1, keepdims=True)
            r.probs[2 * i + h] = p
            parts.append(dot(half(p), v))
        r.ctx[:, many(128 * i, 128, 128)] = half(jnp.where(low_lane, parts[0], parts[1]))
        return 0

    lax.fori_loop(0, 4, heads_forward, 0)

    gb.far()
    middle = r.xs[...] + (dot(r.ctx[...], r.wproj[...]) + bias_p)
    r.mid[...] = middle
    xhat, spread2 = normalize(middle)
    r.xhat2[...] = xhat
    n2 = half(xhat * gain2 + bias2)
    own_first = ((y * 2 + x) * 2 + c) * BLOCK
    r.n_all[many(own_first, LATE, 16), :] = n2[0:LATE, :]
    ga.begin(slice(0, 2))
    for k in range(zs - 1):
        pl.when(z > k)(lambda k=k: count_copy(2, 4, 5 + k, partner).wait_recv())
    for k in range(zs - 1):
        ahead = ahead + jnp.where(z > k, r.count_in[5 + k], 0.0)
    offsets = ahead[0:1, :]
    chosen = 0.0
    for k in range(2):
        slot = before[k] + jnp.sum(onehot[k] * offsets, axis=1, keepdims=True)
        chosen = chosen + onehot[k] * jnp.where(slot < float(capacity), 1.0, 0.0)
    r.chosen[...] = chosen
    logits = jnp.where(lane < 4, dot(n2, route) + noise, -1e30)
    e = jnp.exp(logits - jnp.max(logits, axis=-1, keepdims=True))
    rprobs = e / jnp.sum(e, axis=-1, keepdims=True)
    r.rprobs[...] = rprobs
    gates = rprobs * chosen
    gates_high = half(gates).astype(F32)
    packed = jnp.where(lane < 4, gates_high, pltpu.roll(gates - gates_high, 4, 1)).T
    packed = jnp.concatenate([packed[0:8, :], jnp.zeros((8, 256), F32)], axis=1)
    r.n_all[many(own_first + LATE, BLOCK - LATE, 16), :] = half(jnp.concatenate(
        [n2[LATE:LATE + 8, :].astype(F32), packed], axis=0))
    ga.begin(slice(2, 3))

    pair = many(spot * 2 * BLOCK, 2 * BLOCK, 16)
    for g in gathers:
        g.from_core(spot)
    for j in range(2):
        g8 = r.n_all[many((spot * 2 + j) * BLOCK + 192, 16, 16), 0:256].astype(F32)[8:16, :]
        g8 = g8 + pltpu.roll(g8, 4, 0)
        g8 = jnp.where(c == 0, g8, pltpu.roll(g8, 6, 0))
        r.gcol[j * BLOCK:(j + 1) * BLOCK, :] = jnp.concatenate([g8, jnp.zeros((120, 256), F32)], axis=0).T[0:BLOCK, :]
    for copy in loads:
        copy.wait()
    r.running[...] = jnp.zeros_like(r.running)
    r.drows[...] = jnp.zeros_like(r.drows)
    r.dgate[...] = jnp.zeros_like(r.dgate)
    r.extra[...] = jnp.zeros_like(r.extra)
    pair_lane = iota((2 * BLOCK, 128), 1)
    def expert_pass(e, between):
        gate = r.gcol[:, e:e + 1]
        r.res[...] = jnp.zeros_like(r.res)
        d_result = gate * r.c_all[pair, :].astype(F32)
        r.dres[...] = half(d_result)
        r.extra[0, 2 + e:3 + e, 0:512] = column_sum(r.dres[...].astype(F32))

        def hidden_step(j, _):
            hs = many(j * STEP, STEP, STEP)
            n = r.n_all[pair, :]
            pre = dot(n, r.win[e, :, hs]) + r.bin[e:e + 1, hs].astype(F32)
            hid, slope = gelu_parts(pre)
            r.res[...] += dot(half(hid), r.wout[e, hs, :])
            d_pre = half(slope * dot_nt(r.dres[...], r.wout[e, hs, :]))
            r.extra[0, e:e + 1, hs] = column_sum(d_pre.astype(F32))
            r.drows[...] += dot_nt(d_pre, r.win[e, :, hs])
            return 0

        lax.fori_loop(0, 2, hidden_step, 0)
        between()
        lax.fori_loop(2, 4, hidden_step, 0)
        result = r.res[...] + r.bout[e:e + 1, :].astype(F32)
        r.running[...] += gate * result
        d_gate = jnp.sum(r.c_all[pair, :].astype(F32) * result, axis=1, keepdims=True)
        r.dgate[...] = jnp.where(pair_lane == 2 * c + e, d_gate, r.dgate[...])

    expert_pass(0, ga.turn)
    ga.far()

    for g in gathers:
        for other_spot in g.others():
            g.from_core(other_spot)
    span = 8 * BLOCK
    row = jnp.zeros((8, span), F32)
    for d in range(8):
        g8 = r.n_all[d * BLOCK + 192:(d + 1) * BLOCK, 0:256].astype(F32)[8:16, :]
        g8 = g8 + pltpu.roll(g8, 4, 0)
        g8 = jnp.where(c == 0, g8, pltpu.roll(g8, 6, 0))
        at, shift = d * BLOCK // 128 * 128, d * BLOCK % 128
        width = min(384, span - at)
        g8 = jnp.concatenate([g8, jnp.zeros((8, 128), F32)], axis=1)
        g8 = pltpu.roll(g8, shift, 1) if shift else g8
        pieces = [jnp.zeros((8, at), F32)] if at else []
        pieces += [g8[:, 0:width]] + ([jnp.zeros((8, span - at - width), F32)] if span > at + width else [])
        row = row + jnp.concatenate(pieces, axis=1)
    r.g_all[...] = row

    slot = lax.rem(x + y, 2)

    def where_from(f, slice_of, x_of):
        s, i, kind = f // PER, lax.rem(f, PER) // 2, lax.rem(f, 2)
        t = jnp.maximum(s - 2, 0)
        e = jnp.where(s < 2, s, t // 2)
        start = slice_of * 1024 + jnp.where(s < 2, 512 + x_of * SLICE, lax.rem(t, 2) * SLICE)
        return e, start, i, kind

    def landing(f, slice_of=slot, x_of=x):
        e, start, i, kind = where_from(f, slice_of, x_of)
        return r.grads.at[kind * 2 + e, many(start + i * PIECE, PIECE, PIECE), :]

    def up_copy(src, f):
        return remote(src, r.up_in.at[f], r.bulk.at[0], r.up_recv.at[f], up)

    def down_copy(src, f):
        return remote(src, r.down_in.at[f], r.bulk.at[1], r.down_recv.at[f], down)

    def keep_copy(f):
        return pltpu.make_async_copy(r.fin.at[f], landing(f), r.bulk.at[2])

    def give_x(f, recv, ref=None):
        return remote(r.fin.at[f], landing(f) if ref is None else ref, r.bulk.at[3], recv, xn)

    def give_y(f, recv, ref=None):
        return remote(r.fin.at[f], landing(f) if ref is None else ref, r.bulk.at[4], recv, yn)

    def pass_x(f):
        ref = landing(f, 1 - slot, x)
        return remote(ref, ref, r.bulk.at[5], r.bulk.at[7], xn)

    def pass_y(f):
        ref = landing(f, 1 - slot, 1 - x)
        return remote(ref, ref, r.bulk.at[6], r.bulk.at[8], yn)

    def goes(f):
        late = lax.rem(f // PER, 2)
        return (f < SETS) | (late == 0), (f < SETS) | (late == 1), lax.rem(f, PER) < PER // 2

    def inside(f, count=PIECES):
        return (f >= 0) & (f < count)

    def tick(t):
        u, d, f, w = t - HOP * z, t - HOP * (zs - 1 - z), t - HOP * (zs - 1), t - HOP * (zs - 1) - PASS

        @pl.when(inside(u))
        def _():
            pl.when(z == 0)(lambda: up_copy(r.own.at[u], u).start())

            @pl.when(low_z)
            def _():
                up_copy(r.up_out.at[u], u).wait_recv()

                @pl.when(high_z)
                def _():
                    r.up_out[u] = half(r.own[u].astype(F32) + r.up_in[u].astype(F32))
                    up_copy(r.up_out.at[u], u).start()

        @pl.when(inside(d))
        def _():
            pl.when(z == zs - 1)(lambda: down_copy(r.own.at[d], d).start())

            @pl.when(high_z)
            def _():
                down_copy(r.down_out.at[d], d).wait_recv()

                @pl.when(low_z)
                def _():
                    r.down_out[d] = half(r.own[d].astype(F32) + r.down_in[d].astype(F32))
                    down_copy(r.down_out.at[d], d).start()

        @pl.when(inside(f))
        def _():
            lower = jnp.where(low_z, r.up_in[f].astype(F32), 0.0)
            upper = jnp.where(high_z, r.down_in[f].astype(F32), 0.0)
            r.fin[f] = half(r.own[f].astype(F32) + lower + upper)
            keep_copy(f).start()
            to_x, to_y, by_x = goes(f)
            single = f < SETS
            pl.when(to_x & single & jnp.logical_not(by_x))(lambda: give_x(f, r.x_recv.at[jnp.minimum(f, SETS - 1)]).start())
            pl.when(to_x & jnp.logical_not(single & jnp.logical_not(by_x)))(lambda: give_x(f, r.bulk.at[7]).start())
            pl.when(to_y & single & by_x)(lambda: give_y(f, r.y_recv.at[jnp.minimum(f, SETS - 1)]).start())
            pl.when(to_y & jnp.logical_not(single & by_x))(lambda: give_y(f, r.bulk.at[8]).start())

        @pl.when(inside(w, SETS))
        def _():
            _, _, by_x = goes(w)

            @pl.when(by_x)
            def _():
                give_y(w, r.y_recv.at[w], landing(w, 1 - slot, x)).wait_recv()
                pass_x(w).start()

            @pl.when(jnp.logical_not(by_x))
            def _():
                give_x(w, r.x_recv.at[w], landing(w, 1 - slot, 1 - x)).wait_recv()
                pass_y(w).start()

    def finish_pieces():
        both = PIECES - SETS
        some = SETS + both // 2
        got = both // 2 + SETS
        pl.when(high_z)(lambda: remote(r.own, r.up_in, r.bulk.at[0], r.bulk.at[0], up).wait_send())
        pl.when(low_z)(lambda: remote(r.own, r.down_in, r.bulk.at[1], r.bulk.at[1], down).wait_send())
        pltpu.make_async_copy(r.fin, r.own, r.bulk.at[2]).wait()
        for i, count in ((3, some), (4, some), (5, SETS // 2), (6, SETS // 2)):
            remote(r.fin.at[0:count], r.own.at[0:count], r.bulk.at[i], r.bulk.at[i], xn).wait_send()
        for i in (7, 8):
            remote(r.fin.at[0:got], r.own.at[0:got], r.bulk.at[i], r.bulk.at[i], xn).wait_recv()

    far_half = (1 - x, 1 - y)
    near_half = (x, y)
    quarter = (x * 2 + y, 4 + y * 2 + x)
    near, next_near = (xn, yn), (yn, xn)

    def cols(j, n):
        return many(j * 256, 256 * n, 256)

    def ar(i, src, dst, target):
        return remote(src, dst, r.ar_send.at[i], r.ar_recv.at[i], target)

    def ar_one(s):
        return ar(s, r.total.at[:, cols(4 * s + 2 * far_half[s], 2)], r.part_in.at[s], near[s])

    def ar_two(s):
        give = 4 * s + 2 * near_half[s] + (1 - near_half[1 - s])
        return ar(2 + s, r.total.at[:, cols(give, 1)], r.part_in.at[2 + s, :, 0:256], next_near[s])

    def ar_up(s):
        return ar(4 + s, r.z_out.at[s], r.z_in.at[s], up)

    def ar_down(s):
        return ar(6 + s, r.z_out.at[2 + s], r.z_in.at[2 + s], down)

    def ar_four(s):
        piece = r.final.at[:, cols(quarter[s], 1)]
        return ar(8 + s, piece, piece, next_near[s])

    def ar_four_got(s):
        piece = r.final.at[:, cols(4 * s + 2 * near_half[s] + (1 - near_half[1 - s]), 1)]
        return ar(8 + s, piece, piece, next_near[s])

    def ar_five(s):
        piece = r.final.at[:, cols(4 * s + 2 * near_half[s], 2)]
        return ar(10 + s, piece, piece, near[s])

    def ar_five_got(s):
        piece = r.final.at[:, cols(4 * s + 2 * far_half[s], 2)]
        return ar(10 + s, piece, piece, near[s])

    def add_into(ref, other_part):
        ref[...] = half(ref[...].astype(F32) + other_part.astype(F32))

    def ar_stage1():
        for s in range(2):
            ar_one(s).start()

    def ar_stage2():
        for s in range(2):
            ar_one(s).wait()
            add_into(r.total.at[:, cols(4 * s + 2 * near_half[s], 2)], r.part_in[s])
            ar_two(s).start()

    def ar_stage3():
        for s in range(2):
            ar_two(s).wait()
            add_into(r.total.at[:, cols(quarter[s], 1)], r.part_in[2 + s, :, 0:256])

            @pl.when(z == 0)
            def _():
                r.z_out[s] = r.total[:, cols(quarter[s], 1)]
                ar_up(s).start()

            @pl.when(z == zs - 1)
            def _():
                r.z_out[2 + s] = r.total[:, cols(quarter[s], 1)]
                ar_down(s).start()

    def ar_stage_z(k):
        for s in range(2):
            @pl.when(z == k)
            def _():
                ar_up(s).wait_recv()
                if k < zs - 1:
                    r.z_out[s] = half(r.total[:, cols(quarter[s], 1)].astype(F32) + r.z_in[s].astype(F32))
                    ar_up(s).start()

            @pl.when(z == zs - 1 - k)
            def _():
                ar_down(s).wait_recv()
                if k < zs - 1:
                    r.z_out[2 + s] = half(r.total[:, cols(quarter[s], 1)].astype(F32) + r.z_in[2 + s].astype(F32))
                    ar_down(s).start()

    def ar_stage4():
        for s in range(2):
            lower = jnp.where(low_z, r.z_in[s].astype(F32), 0.0)
            upper = jnp.where(high_z, r.z_in[2 + s].astype(F32), 0.0)
            own = r.total[:, cols(quarter[s], 1)].astype(F32)
            r.final[:, cols(quarter[s], 1)] = half(own + lower + upper)
            ar_four(s).start()

    def ar_stage5():
        for s in range(2):
            ar_four_got(s).wait_recv()
            ar_five(s).start()

    def ar_stage6():
        for s in range(2):
            ar_five_got(s).wait_recv()
            ar_four(s).wait_send()
            ar_five(s).wait_send()
            pl.when(high_z)(lambda s=s: ar_up(s).wait_send())
            pl.when(low_z)(lambda s=s: ar_down(s).wait_send())

    stages_at = {4: ar_stage2, 5: ar_stage3}

    def slice_step(s, _):
        e, start, _, _ = where_from(s * PER, slot, x)
        hs = many(start, SLICE, SLICE)
        wi = half(r.win[e, :, hs].astype(F32).T)
        wo = r.wout[e, hs, :]
        bias = jnp.broadcast_to(r.binf[pl.ds(e, 1), hs], (128, SLICE)).T[:, 0:1]
        n, co, g = r.n_all[...], r.c_all[...], r.g_all[pl.ds(e, 1), :]
        hid, slope = gelu_parts(dot_nt(wi, n) + bias)
        dh = dot_nt(wo, co)
        for kind, grad in ((0, dot(half(slope * (dh * g)), n)), (1, dot(half(hid * g), co))):
            for i in range(SLICE // PIECE):
                r.own[s * PER + i * 2 + kind] = half(grad[i * PIECE:(i + 1) * PIECE, :])
        for at, todo in stages_at.items():
            pl.when(s == at)(todo)
        for k in range(TICKS):
            pl.when(s < EARLY)(lambda k=k: tick(s * TICKS + k))
        for k in range(LATER):
            pl.when(s >= EARLY)(lambda k=k: tick(middle + (s - EARLY) * LATER + k))
        return 0

    middle = EARLY * TICKS + sum(BEATS)
    assert middle <= EARLY * PER

    lax.fori_loop(0, EARLY, slice_step, 0)
    clock, beats = iter(range(EARLY * TICKS, middle)), iter(BEATS)

    def beat():
        for _ in range(next(beats)):
            tick(next(clock))


    expert_pass(1, beat)
    beat()
    theirs, ours = many((1 - c) * BLOCK, BLOCK, 8), many(c * BLOCK, BLOCK, 8)
    partials = [remote(src.at[theirs, :], dst, r.p_send.at[i], r.p_recv.at[i], partner) for i, (src, dst) in enumerate(
        ((r.running, r.got_running), (r.drows, r.got_drows), (r.dgate, r.got_dgate)))]
    for copy in partials:
        copy.start()
    beat()
    for copy in partials:
        copy.wait()

    r.out[...] = half(r.mid[0:BLOCK, :] + (r.running[ours, :] + r.got_running[...]))[0:tokens, :]
    zeros = jnp.zeros((ROWS - BLOCK, 128), F32)
    d_gates = jnp.concatenate([r.dgate[ours, :] + r.got_dgate[...], zeros], axis=0)
    rprobs, chosen = r.rprobs[...], r.chosen[...]
    d_probs = d_gates * chosen
    d_logits = half(rprobs * (d_probs - jnp.sum(rprobs * d_probs, axis=-1, keepdims=True)))
    r.dn[0:BLOCK, :] = r.drows[ours, :] + r.got_drows[...]
    r.dn[BLOCK:ROWS, :] = jnp.zeros((ROWS - BLOCK, 512), F32)
    beat()
    dn = r.dn[...] + dot(d_logits, route_t)
    xhat = r.xhat2[...]
    n2 = half(xhat * gain2 + bias2)
    grad_route = dot(half(d_logits.astype(F32).T), n2)
    vector_rows = {5: column_sum(dn * xhat), 6: column_sum(dn)}
    r.xs[...] = jnp.zeros_like(r.xs)
    r.xs[0:tokens, :] = r.cot[...].astype(F32)
    d_middle = r.xs[...] + norm_back(dn, xhat, spread2, gain2)
    r.mid[...] = d_middle
    r.db[...] = half(d_middle)
    db = r.db[...]
    vector_rows[4] = column_sum(db.astype(F32))
    r.dense[:, 1536:2048] = half(dot(half(r.ctx[...].astype(F32).T), db))
    r.dctx[...] = half(dot_nt(db, r.wproj[...]))
    beat()

    def heads_back(i, _):
        q, k, v = [r.mixed[:, many(base + 128 * i, 128, 128)] for base in (0, 512, 1024)]
        q = q * BF16(HEAD_DIM ** -0.5)
        do = r.dctx[:, many(128 * i, 128, 128)]
        parts = []
        for h in range(2):
            p = r.probs[2 * i + h]
            dp = dot_nt(jnp.where(low_lane == (h == 0), do, jnp.zeros_like(do)), v)
            ds = p * (dp - jnp.sum(p * dp, axis=-1, keepdims=True))
            parts.append((dot(half(ds), k) * HEAD_DIM ** -0.5, dot(half(ds.T), q), dot(half(p.T), do)))
        for j, base in enumerate((0, 512, 1024)):
            r.dmixed[:, many(base + 128 * i, 128, 128)] = half(jnp.where(low_lane, parts[0][j], parts[1][j]))
        return 0

    beat()
    lax.fori_loop(0, 4, heads_back, 0)
    beat()
    n1_t = half(r.n1[...].astype(F32).T)
    dn = 0.0
    for i in range(3):
        part = r.dmixed[:, 512 * i:512 * (i + 1)]
        if i != 1:
            vector_rows[2 + i // 2] = column_sum(part.astype(F32))
        r.dense[:, 512 * i:512 * (i + 1)] = half(dot(n1_t, part))
        dn = dn + dot_nt(part, r.wqkv[:, 512 * i:512 * (i + 1)])
        beat()
    xhat = r.xhat1[...]
    vector_rows[0] = column_sum(dn * xhat)
    vector_rows[1] = column_sum(dn)
    r.igrad[...] = (r.mid[...] + norm_back(dn, xhat, spread1, gain1))[0:tokens, :]

    vectors = jnp.concatenate([grad_route[0:4, :]] + [vector_rows[i] for i in range(7)] + [jnp.zeros((5, 512), F32)], axis=0)
    r.dn[0:16, :] = vectors
    low_half, high_half = r.dn[0:16, 0:256], r.dn[0:16, 256:512]
    r.extra[1, :, 0:256] = jnp.where(c == 0, high_half, low_half)
    own_half = jnp.where(c == 0, low_half, high_half)
    swaps = [remote(r.dense.at[other, :], r.dense_in, r.d_send.at[0], r.d_recv.at[0], partner),
             remote(r.extra.at[1], r.extra.at[2], r.d_send.at[1], r.d_recv.at[1], partner)]
    for copy in swaps:
        copy.start()
    for copy in swaps:
        copy.wait()
    r.total[0:256, :] = half(r.dense[mine, :].astype(F32) + r.dense_in[...].astype(F32))
    sums = own_half + r.extra[2, :, 0:256]
    small = jnp.concatenate([r.extra[0, 0:4, :], jnp.zeros((12, 2048), F32)], axis=0)
    shifted = jnp.concatenate([jnp.zeros((4, 256), F32), sums[0:12, :]], axis=0)
    r.total[256:272, :] = half(small + jnp.concatenate([shifted, jnp.zeros((16, 1792), F32)], axis=1))

    ar_stage1()

    lax.fori_loop(EARLY, STEPS, slice_step, 0)
    start, ends = middle + (STEPS - EARLY) * LATER, PIECES + HOP * (zs - 1)
    stages = {0: lambda: ar_stage_z(1), 3: lambda: ar_stage_z(2), 6: lambda: ar_stage_z(3), 8: ar_stage4, 11: ar_stage5}

    def last_ticks(t, _):
        for at, stage in stages.items():
            pl.when(t == start + at)(stage)
        tick(t)
        return 0

    lax.fori_loop(start, ends, last_ticks, 0)
    ar_stage6()
    finish_pieces()
    for g in gathers:
        g.drain()
    for i in range(4):
        count_copy(min(i, 1), i, 0, partner).wait_send()
    for k in range(1, zs):
        pl.when(z < k)(lambda k=k: count_copy(2, 3 + k, 0, partner).wait_send())


def block_call(zs, *args):
    tokens, width = args[0].shape
    vm, hbm = pl.BlockSpec(memory_space=pltpu.VMEM), pl.BlockSpec(memory_space=pl.ANY)
    shape = jax.ShapeDtypeStruct
    in_specs = [hbm if name in ("win_in", "wout_in", "wqkv_in", "wproj_in") else vm for name in INPUTS]
    scratch = [pltpu.VMEM(dims, dtype) for _, dims, dtype in SCRATCH]
    scratch += [pltpu.SemaphoreType.DMA(dims) for _, dims in SEMS]
    return pl.pallas_call(
        functools.partial(block_kernel, zs),
        out_shape=(shape((tokens, width), BF16), shape((tokens, width), F32), shape((4, 2048, 512), BF16), shape((272, 2048), BF16)),
        in_specs=in_specs,
        out_specs=(vm, vm, hbm, vm),
        scratch_shapes=scratch,
        compiler_params=pltpu.CompilerParams(collective_id=0, has_side_effects=True, vmem_limit_bytes=63 << 20),
        name="encoder_block",
    )(*args)


def finish_kernel(grads, summed, out_in, igrad_in, grad_in, grad_out, qkv, proj, igrad, out, route, bias_in, bias_out, *rest):
    vectors, (got, done_in, done_out, sums, wide, narrow, igrad_now, got_sem, done_sem, sem) = rest[:7], rest[7:]
    n = done_in.shape[0]

    def source(k, i):
        return pltpu.make_async_copy(
            grads.at[2 * k + i // 4, many(lax.rem(i, 4) * STEP, STEP, STEP), :], got.at[k * n + i], got_sem.at[k * n + i])

    def results(i):
        where = many(lax.rem(i, 4) * STEP, STEP, STEP)
        return (pltpu.make_async_copy(done_in.at[i], grad_in.at[i // 4, :, where], done_sem.at[i]),
                pltpu.make_async_copy(done_out.at[i], grad_out.at[i // 4, where, :], done_sem.at[n + i]))

    def fetch(i, _):
        source(1, i).start()
        source(0, i).start()
        return 0

    arrivals = [pltpu.make_async_copy(summed, sums, sem.at[0]), pltpu.make_async_copy(igrad_in, igrad_now, sem.at[1])]
    others = [pltpu.make_async_copy(wide, qkv, sem.at[2]), pltpu.make_async_copy(narrow, proj, sem.at[3]),
              pltpu.make_async_copy(igrad_now, igrad, sem.at[4])]
    lax.fori_loop(0, 2, fetch, 0)
    for copy in arrivals:
        copy.start()
    lax.fori_loop(2, n, fetch, 0)

    def convert(i, _):
        to_in, to_out = results(i)
        source(1, i).wait()
        done_out[i] = got[n + i].astype(F32)
        to_out.start()
        source(0, i).wait()
        done_in[i] = got[i].astype(F32).T
        to_in.start()
        return 0

    lax.fori_loop(0, n - 2, convert, 0)
    for copy in arrivals:
        copy.wait()
    wide[...] = sums[0:256, 0:1536].astype(F32)
    narrow[...] = sums[0:256, 1536:2048].astype(F32)
    for copy in others:
        copy.start()
    lax.fori_loop(n - 2, n, convert, 0)
    out[...] = out_in[...]
    rows = sums[256:272, :].astype(F32)
    bias_in[...] = rows[0:2, :]
    bias_out[...] = rows[2:4, 0:512]
    route[...] = rows[4:8, 0:256]
    for i, ref in enumerate(vectors):
        ref[...] = rows[8 + i, 0:256]

    def settle(i, _):
        for copy in results(i):
            copy.wait()
        return 0

    lax.fori_loop(0, n, settle, 0)
    for copy in others:
        copy.wait()


def finish(grads, summed, out, igrad):
    shape = jax.ShapeDtypeStruct
    vm, hbm = pl.BlockSpec(memory_space=pltpu.VMEM), pl.BlockSpec(memory_space=pl.ANY)
    large = [shape((2, 512, 2048), F32), shape((2, 2048, 512), F32), shape((256, 1536), F32), shape((256, 512), F32),
             shape(igrad.shape, igrad.dtype)]
    small = [shape(out.shape, out.dtype), shape((4, 256), F32), shape((2, 2048), F32), shape((2, 512), F32)] + [shape((256,), F32)] * 7
    n = 8
    return pl.pallas_call(
        finish_kernel,
        out_shape=large + small,
        in_specs=[hbm, hbm, vm, hbm],
        out_specs=[hbm] * len(large) + [vm] * len(small),
        scratch_shapes=[
            pltpu.VMEM((2 * n, STEP, 512), BF16), pltpu.VMEM((n, 512, STEP), F32), pltpu.VMEM((n, STEP, 512), F32),
            pltpu.VMEM(summed.shape, BF16), pltpu.VMEM((256, 1536), F32), pltpu.VMEM((256, 512), F32),
            pltpu.VMEM(igrad.shape, igrad.dtype),
            pltpu.SemaphoreType.DMA((2 * n,)), pltpu.SemaphoreType.DMA((2 * n,)), pltpu.SemaphoreType.DMA((5,)),
        ],
        compiler_params=pltpu.CompilerParams(vmem_limit_bytes=60 << 20),
        name="finish",
    )(grads, summed, out, igrad)


def swap(v):
    return lax.ppermute(v, "shard", [(0, 1), (1, 0)])


def fused(inputs, norm1_gain, norm1_bias, qkv_weight, query_bias, value_bias, out_weight, out_bias, norm2_gain, norm2_bias,
          router_weight, noise, expert_in, expert_in_bias, expert_out, expert_out_bias, routes, priority, cotangent):
    out, igrad, grads, summed = block_call(
        lax.axis_size("replica") // 4, inputs, cotangent, noise.T, routes.T, priority, norm1_gain, norm1_bias, query_bias,
        value_bias, out_bias, norm2_gain, norm2_bias, router_weight.T, qkv_weight, out_weight, expert_in, expert_out,
        expert_in_bias, expert_out_bias)
    grad_in, grad_out, qkv, proj, igrad, out, route, bias_in, bias_out, *cols = finish(grads, summed, out, igrad)
    return (out, igrad, cols[0], cols[1], qkv, cols[2], cols[3], proj, cols[4], cols[5], cols[6], route.T,
            grad_in, bias_in, grad_out, bias_out)


def layer_norm(values, gain_vector, bias_vector):
    centered = values - jnp.mean(values, axis=-1, keepdims=True)
    spread = lax.rsqrt(jnp.mean(centered * centered, axis=-1, keepdims=True) + LN_EPS)
    return centered * spread * gain_vector + bias_vector


def kept_gates(pair_expert, ranks, offsets, capacity, expert_count):
    same = pair_expert[:, None] == pair_expert[None, :]
    earlier = ranks[None, :] < ranks[:, None]
    before = jnp.sum(jnp.where(same & earlier, 1, 0).astype(jnp.int32), axis=1)
    onehot = pair_expert[:, None] == jnp.arange(expert_count, dtype=jnp.int32)[None, :]
    first_slot = jnp.sum(jnp.where(onehot, offsets[None, :], 0).astype(jnp.int32), axis=1)
    keep = before + first_slot < capacity
    picked = jnp.where(onehot & keep[:, None], 1.0, 0.0).astype(jnp.float32)
    return jnp.sum(picked.reshape(-1, 2, expert_count), axis=1)


def general(
    inputs, norm1_gain, norm1_bias, qkv_weight, query_bias, value_bias, out_weight, out_bias, norm2_gain, norm2_bias,
    router_weight, noise, expert_in, expert_in_bias, expert_out, expert_out_bias, routes, priority, cotangent,
):
    tok_count, width = inputs.shape
    replicas, cores = lax.axis_size("replica"), lax.axis_size("shard")
    shard = lax.axis_index("shard")
    images = tok_count // PATCHES
    heads = width // HEAD_DIM
    owned, _, hidden_count = expert_in.shape
    expert_count = owned * cores
    score_scale = HEAD_DIM ** (-0.5)
    f32 = jnp.float32

    vectors = (norm1_gain, norm1_bias, query_bias, value_bias, out_bias, norm2_gain, norm2_bias)
    packed = jnp.concatenate(
        [qkv_weight, out_weight, jnp.stack(vectors, axis=1), router_weight], axis=1)
    packed = lax.all_gather(packed, "shard", axis=0, tiled=True)
    weight_qkv = packed[:, :3 * width]
    weight_proj = packed[:, 3 * width:4 * width]
    small = packed[:, 4 * width:]
    gain_one, bias_one, bias_query, bias_value, bias_proj, gain_two, bias_two = [
        small[:, i].astype(f32) for i in range(len(vectors))]
    weight_route = small[:, len(vectors):]

    pair_expert = routes.reshape(-1)
    onehot_pairs = (pair_expert[:, None] == jnp.arange(expert_count, dtype=jnp.int32)[None, :]).astype(jnp.int32)
    load = jnp.sum(onehot_pairs, axis=0)
    loads = lax.all_gather(load, ("replica", "shard"))
    position = lax.axis_index("replica") * cores + shard
    ahead = jnp.arange(replicas * cores)[:, None] < position
    offsets = jnp.sum(jnp.where(ahead, loads, 0), axis=0)
    capacity = 2 * tok_count * replicas * cores // expert_count
    chosen = kept_gates(pair_expert, priority.reshape(-1), offsets, capacity, expert_count)

    residual_in = inputs.astype(f32)
    normed_one, norm_one_back = jax.vjp(layer_norm, residual_in, gain_one, bias_one)
    normed_one_half = half(normed_one)
    qkv_bias = jnp.concatenate([bias_query, jnp.zeros_like(bias_query), bias_value])
    mixed = half(dot(normed_one_half, weight_qkv) + qkv_bias)
    shaped = mixed.reshape(images, PATCHES, 3, heads, HEAD_DIM)
    query, keys, values = (shaped[:, :, 0], shaped[:, :, 1], shaped[:, :, 2])
    scores = jnp.einsum("bqhd,bkhd->bhqk", query, keys, preferred_element_type=f32) * score_scale
    row_max = jnp.max(scores, axis=-1, keepdims=True)
    log_total = row_max + jnp.log(jnp.sum(jnp.exp(scores - row_max), axis=-1, keepdims=True))
    context = jnp.einsum(
        "bhqk,bkhd->bqhd", half(jnp.exp(scores - log_total)), values, preferred_element_type=f32)
    context_half = half(context.reshape(tok_count, width))
    middle = residual_in + (dot(context_half, weight_proj) + bias_proj)
    normed_two, norm_two_back = jax.vjp(layer_norm, middle, gain_two, bias_two)
    normed_two_half = half(normed_two)
    logits = dot(normed_two_half, weight_route) + noise
    route_probs = jax.nn.softmax(logits, axis=-1)
    gate_weights = route_probs * chosen
    upstream = cotangent.astype(f32)

    pair_n = jnp.concatenate([normed_two_half, swap(normed_two_half)], axis=0)
    pair_c = jnp.concatenate([cotangent, swap(cotangent)], axis=0)
    own_gates = lax.dynamic_slice_in_dim(gate_weights, shard * owned, owned, 1)
    other_gates = swap(lax.dynamic_slice_in_dim(gate_weights, (1 - shard) * owned, owned, 1))
    pair_g = jnp.concatenate([own_gates, other_gates], axis=0)
    pair_up = pair_c.astype(f32)
    running = jnp.zeros((2 * tok_count, width), f32)
    d_rows = jnp.zeros((2 * tok_count, width), f32)
    gate_columns, bias_in_grads, bias_out_grads, in_grads, out_grads = [], [], [], [], []
    for e in range(owned):
        gate = pair_g[:, e:e + 1]
        pre = dot(pair_n, expert_in[e]) + expert_in_bias[e].astype(f32)
        act, slope = gelu_parts(pre)
        hid = half(act)
        result = dot(hid, expert_out[e]) + expert_out_bias[e].astype(f32)
        running = running + gate * result
        gate_columns.append(jnp.sum(pair_up * result, axis=1))
        d_result = half(gate * pair_up)
        d_pre = half(slope * dot_nt(d_result, expert_out[e]))
        d_rows = d_rows + dot_nt(d_pre, expert_in[e])
        bias_in_grads.append(jnp.sum(d_pre.astype(f32), axis=0))
        bias_out_grads.append(jnp.sum(d_result.astype(f32), axis=0))
        in_grads.append(jnp.einsum("td,th->dh", pair_n, d_pre, preferred_element_type=f32))
        out_grads.append(jnp.einsum("th,td->hd", hid, d_result, preferred_element_type=f32))
    d_gate_part = jnp.stack(gate_columns, axis=1)
    running = running[:tok_count] + swap(running[tok_count:])
    d_normed = d_rows[:tok_count] + swap(d_rows[tok_count:])
    d_gate_other = swap(d_gate_part[tok_count:])
    d_gate_own = d_gate_part[:tok_count]
    d_gates = jnp.where(shard == 0, jnp.concatenate([d_gate_own, d_gate_other], axis=1),
                        jnp.concatenate([d_gate_other, d_gate_own], axis=1))

    grad_in = lax.psum(half(jnp.stack(in_grads, axis=0)), "replica")
    grad_out = lax.psum(half(jnp.stack(out_grads, axis=0)), "replica")

    output = half(middle + running)
    d_probs = d_gates * chosen
    d_logits = half(route_probs * (d_probs - jnp.sum(route_probs * d_probs, axis=-1, keepdims=True)))
    grad_route = jnp.einsum("td,te->de", normed_two_half, d_logits, preferred_element_type=f32)
    d_normed = d_normed + dot_nt(d_logits, weight_route)
    d_middle, grad_gain_two, grad_bias_two = norm_two_back(d_normed)
    d_middle = d_middle + upstream
    d_branch = half(d_middle)
    grad_proj = jnp.einsum("tc,td->cd", context_half, d_branch, preferred_element_type=f32)
    grad_proj_bias = jnp.sum(d_branch.astype(f32), axis=0)
    d_context = half(dot_nt(d_branch, weight_proj)).reshape(images, PATCHES, heads, HEAD_DIM)
    attn_probs = jnp.exp(scores - log_total)
    d_attn = jnp.einsum("bqhd,bkhd->bhqk", d_context, values, preferred_element_type=f32)
    d_values = jnp.einsum("bhqk,bqhd->bkhd", half(attn_probs), d_context, preferred_element_type=f32)
    d_scores = half(attn_probs * (d_attn - jnp.sum(attn_probs * d_attn, axis=-1, keepdims=True)))
    d_query = jnp.einsum("bhqk,bkhd->bqhd", d_scores, keys, preferred_element_type=f32) * score_scale
    d_keys = jnp.einsum("bhqk,bqhd->bkhd", d_scores, query, preferred_element_type=f32) * score_scale
    d_mixed = half(jnp.stack([d_query, d_keys, d_values], axis=2).reshape(tok_count, 3 * width))
    grad_qkv = jnp.einsum("td,tf->df", normed_one_half, d_mixed, preferred_element_type=f32)
    mixed_sums = jnp.sum(d_mixed.astype(f32), axis=0)
    d_normed_one = dot_nt(d_mixed, weight_qkv)
    d_input, grad_gain_one, grad_bias_one = norm_one_back(d_normed_one)
    input_grad = d_input + d_middle

    columns = jnp.stack((grad_gain_one, grad_bias_one, mixed_sums[:width], mixed_sums[2 * width:], grad_proj_bias,
                         grad_gain_two, grad_bias_two), axis=1)
    dense = half(jnp.concatenate([grad_qkv, grad_proj, columns, grad_route], axis=1))
    mine = width // 2
    keep = lax.dynamic_slice_in_dim(dense, shard * mine, mine, 0)
    give = lax.dynamic_slice_in_dim(dense, (1 - shard) * mine, mine, 0)
    dense = keep.astype(f32) + swap(give).astype(f32)
    bias_row = jnp.concatenate(bias_in_grads + bias_out_grads)
    summed, bias_row = lax.psum((half(dense), bias_row), "replica")
    summed = summed.astype(f32)
    columns = [summed[:, 4 * width + i] for i in range(len(vectors))]
    grad_in_bias = bias_row[:owned * hidden_count].reshape(owned, hidden_count)
    grad_out_bias = bias_row[owned * hidden_count:].reshape(owned, width)
    return (
        output, input_grad, columns[0], columns[1], summed[:, :3 * width], columns[2], columns[3],
        summed[:, 3 * width:4 * width], columns[4], columns[5], columns[6], summed[:, 4 * width + len(vectors):],
        grad_in.astype(f32), grad_in_bias, grad_out.astype(f32), grad_out_bias,
    )


def on_device(*args):
    expert_in, inputs = args[12], args[0]
    planes = lax.axis_size("replica") == 16 and lax.axis_size("shard") == 2
    if planes and inputs.shape == (PATCHES, 512) and expert_in.shape == (2, 512, 2048):
        return fused(*args)
    return general(*args)


def solution(mesh):
    both, split = ("replica", "shard"), "shard"
    return jax.shard_map(
        on_device,
        mesh=mesh,
        in_specs=(
            P(both, None), P(split), P(split), P(split, None), P(split), P(split), P(split, None), P(split), P(split),
            P(split), P(split, None), P(both, None), P(split, None, None), P(split, None), P(split, None, None),
            P(split, None), P(both, None), P(both, None), P(both, None),
        ),
        out_specs=(
            P(both, None), P(both, None), P(split), P(split), P(split, None), P(split), P(split), P(split, None),
            P(split), P(split), P(split), P(split, None), P(split, None, None), P(split, None), P(split, None, None),
            P(split, None),
        ),
        check_vma=False,
    )
```

```python
import functools
from types import SimpleNamespace

import jax
import jax.numpy as jnp
from jax import lax
from jax.experimental import pallas as pl
from jax.experimental.pallas import tpu as pltpu
from jax.sharding import PartitionSpec as P

HEAD_DIM = 64
PATCHES = 197
LN_EPS = 1e-06
MESH = pl.DeviceIdType.MESH
NT = (((1,), (1,)), ((), ()))
GELU_K = 0.7978845608028654
GELU_A = 0.044715
F32 = jnp.float32
BF16 = jnp.bfloat16
ROWS = 256
LATE = 192
BLOCK = 208
STEP = 512
SLICE = 256
PIECE = 128
STEPS = 6
PER = 2 * SLICE // PIECE
PIECES = STEPS * PER
SETS = 2 * PER
HOP = 3
TICKS, LATER = 1, 2
EARLY = 3
BEATS = (1, 1, 1, 1, 1, 0, 1, 1, 0, 1)
PASS = 4


def half(values):
    return values.astype(BF16)


def dot(a, b):
    return jnp.dot(a, b, preferred_element_type=F32)


def dot_nt(a, b):
    return lax.dot_general(a, b, NT, preferred_element_type=F32)


def gelu_parts(x):
    x2 = x * x
    q = 0.5 + 0.5 * jnp.tanh(x * (GELU_K + (GELU_K * GELU_A) * x2))
    h = x * q
    return h, q + (h * (1.0 - q)) * (2 * GELU_K + (6 * GELU_K * GELU_A) * x2)


def iota(shape, dim):
    return lax.broadcasted_iota(jnp.int32, shape, dim)


def many(start, size, unit):
    return pl.ds(pl.multiple_of(start, unit), size)


def normalize(v):
    centered = v - jnp.mean(v, axis=-1, keepdims=True)
    spread = lax.rsqrt(jnp.mean(centered * centered, axis=-1, keepdims=True) + LN_EPS)
    return centered * spread, spread


def norm_back(d, xhat, spread, gain):
    dx = d * gain
    return spread * (dx - jnp.mean(dx, axis=-1, keepdims=True) - xhat * jnp.mean(dx * xhat, axis=-1, keepdims=True))


def column_sum(v):
    return jnp.sum(v, axis=0, keepdims=True)


def place():
    r = lax.axis_index("replica")
    return r // 4, (r // 2) % 2, r % 2, lax.axis_index("shard")


def rep(z, y, x):
    return (z * 2 + y) * 2 + x


class PlaneGather:
    def __init__(self, x_first, rows, at, sems):
        self.rows, self.at = rows, at
        self.send, self.recv, self.core_send, self.core_recv = sems
        z, y, x, c = place()
        near = ((rep(z, y, 1 - x), c), (rep(z, 1 - y, x), c))
        spots = (y * 2 + 1 - x, (1 - y) * 2 + x)
        self.targets = near if x_first else near[::-1]
        self.first, self.second = spots if x_first else spots[::-1]
        self.me, self.diagonal = y * 2 + x, (1 - y) * 2 + 1 - x
        self.core, self.partner = c, (rep(z, y, x), 1 - c)

    def ref(self, spot, core):
        first, size = self.at
        return self.rows.at[many((spot * 2 + core) * BLOCK + first, size, 16), :]

    def link(self, kind, spot):
        ref = self.ref(spot, self.core)
        return remote(ref, ref, self.send.at[kind, spot], self.recv.at[spot], self.targets[kind])

    def across(self, spot, core=None):
        ref = self.ref(spot, self.core if core is None else core)
        return remote(ref, ref, self.core_send.at[spot], self.core_recv.at[spot], self.partner)

    def begin(self, kind):
        self.link(kind, self.me).start()

    def hand(self):
        self.across(self.me).start()

    def turn(self):
        self.link(0, self.first).wait_recv()
        self.link(1, self.first).start()
        self.across(self.first).start()

    def far(self):
        for spot in (self.second, self.diagonal):
            self.link(0, spot).wait_recv()
            self.across(spot).start()

    def from_core(self, spot):
        self.across(spot, 1 - self.core).wait_recv()

    def drain(self):
        for kind, spot in ((0, self.me), (1, self.me), (1, self.first)):
            self.link(kind, spot).wait_send()
        for spot in range(4):
            self.across(spot).wait_send()


class Halves:
    def __init__(self, rows, sems):
        cuts = ((0, 96), (96, LATE - 96), (LATE, BLOCK - LATE))
        self.parts = [PlaneGather(m == 0, rows, cuts[m], [ref.at[m] for ref in sems]) for m in range(3)]

    def begin(self, parts=slice(0, 3)):
        for part in self.parts[parts]:
            part.begin(0)
        for part in self.parts[parts]:
            part.hand()
        for part in self.parts[parts]:
            part.begin(1)

    def turn(self, parts=slice(0, 3)):
        for part in self.parts[parts]:
            part.turn()

    def far(self):
        for part in self.parts:
            part.far()

    def from_core(self, spot):
        for part in self.parts:
            part.from_core(spot)

    def others(self):
        part = self.parts[0]
        return part.first, part.second, part.diagonal

    def drain(self):
        for part in self.parts:
            part.drain()


SCRATCH = (
    ("n_all", (8 * BLOCK, 512), BF16), ("c_all", (8 * BLOCK, 512), BF16), ("g_all", (8, 8 * BLOCK), F32),
    ("wqkv", (512, 1536), BF16), ("wproj", (512, 512), BF16), ("vec", (2, 16, 256), F32), ("binf", (2, 2048), F32),
    ("win", (2, 512, 2048), BF16), ("wout", (2, 2048, 512), BF16),
    ("count_out", (3, 8, 128), F32), ("count_in", (9, 8, 128), F32),
    ("xs", (ROWS, 512), F32), ("pairs", (16, ROWS), F32),
    ("xhat1", (ROWS, 512), F32), ("n1", (ROWS, 512), BF16), ("mixed", (ROWS, 1536), BF16),
    ("probs", (8, ROWS, ROWS), F32), ("ctx", (ROWS, 512), BF16), ("mid", (ROWS, 512), F32), ("xhat2", (ROWS, 512), F32),
    ("chosen", (ROWS, 128), F32), ("rprobs", (ROWS, 128), F32),
    ("res", (2 * BLOCK, 512), F32), ("running", (2 * BLOCK, 512), F32), ("drows", (2 * BLOCK, 512), F32),
    ("dgate", (2 * BLOCK, 128), F32), ("dres", (2 * BLOCK, 512), BF16), ("gcol", (2 * BLOCK, 128), F32),
    ("got_running", (BLOCK, 512), F32), ("got_drows", (BLOCK, 512), F32), ("got_dgate", (BLOCK, 128), F32),
    ("db", (ROWS, 512), BF16), ("dctx", (ROWS, 512), BF16), ("dmixed", (ROWS, 1536), BF16), ("dn", (ROWS, 512), F32),
    ("dense", (512, 2048), BF16), ("dense_in", (256, 2048), BF16), ("extra", (3, 16, 2048), F32),
    ("total", (272, 2048), BF16), ("part_in", (4, 272, 512), BF16), ("z_out", (4, 272, 256), BF16), ("z_in", (4, 272, 256), BF16),
    ("own", (PIECES, PIECE, 512), BF16), ("up_in", (PIECES, PIECE, 512), BF16), ("up_out", (PIECES, PIECE, 512), BF16),
    ("down_in", (PIECES, PIECE, 512), BF16), ("down_out", (PIECES, PIECE, 512), BF16), ("fin", (PIECES, PIECE, 512), BF16),
)
SEMS = (
    ("g_send", (2, 3, 2, 4)), ("g_recv", (2, 3, 4)), ("g_csend", (2, 3, 4)), ("g_crecv", (2, 3, 4)),
    ("load", (4,)), ("w_send", (3,)), ("w_recv", (3,)), ("count_send", (7,)), ("count_recv", (9,)),
    ("p_send", (3,)), ("p_recv", (3,)), ("d_send", (2,)), ("d_recv", (2,)),
    ("ar_send", (12,)), ("ar_recv", (12,)), ("up_recv", (PIECES,)), ("down_recv", (PIECES,)), ("bulk", (9,)),
    ("x_recv", (SETS,)), ("y_recv", (SETS,)),
)
INPUTS = ("x", "cot", "noise_in", "routes_in", "prio", "v0", "v1", "v2", "v3", "v4", "v5", "v6", "route_in", "wqkv_in",
          "wproj_in", "win_in", "wout_in", "bin", "bout")
OUTPUTS = ("out", "igrad", "grads", "final")


def remote(src, dst, send, recv, target):
    return pltpu.make_async_remote_copy(
        src_ref=src, dst_ref=dst, send_sem=send, recv_sem=recv, device_id=target, device_id_type=MESH)


def block_kernel(zs, *refs):
    names = INPUTS + OUTPUTS + tuple(n for n, _, _ in SCRATCH) + tuple(n for n, _ in SEMS)
    r = SimpleNamespace(**dict(zip(names, refs, strict=True)))
    z, y, x, c = place()
    me = rep(z, y, x)
    partner = (me, 1 - c)
    xn, yn = (rep(z, y, 1 - x), c), (rep(z, 1 - y, x), c)
    up, down = (rep(z + 1, y, x), c), (rep(z - 1, y, x), c)
    low_z, high_z = z > 0, z < zs - 1
    tokens = r.x.shape[0]
    devices = 8 * zs
    capacity = 2 * tokens * devices // 4

    bar = pltpu.get_barrier_semaphore()
    for d in range(1, zs):
        peer = (rep(lax.rem(z + d, zs), y, x), c)
        pl.semaphore_signal(bar, inc=1, device_id=peer, device_id_type=MESH)
    for peer in (xn, yn, (rep(z, 1 - y, 1 - x), c), partner):
        pl.semaphore_signal(bar, inc=1, device_id=peer, device_id_type=MESH)

    mine, other = many(c * 256, 256, 16), many((1 - c) * 256, 256, 16)
    halves = [pltpu.make_async_copy(r.wqkv_in, r.wqkv.at[mine, :], r.load.at[2]),
              pltpu.make_async_copy(r.wproj_in, r.wproj.at[mine, :], r.load.at[3])]
    loads = [pltpu.make_async_copy(r.win_in, r.win, r.load.at[0]), pltpu.make_async_copy(r.wout_in, r.wout, r.load.at[1])]
    for copy in halves + loads:
        copy.start()

    r.xs[...] = jnp.zeros_like(r.xs)
    r.xs[0:tokens, :] = r.cot[...].astype(F32)
    own_rows = many(((y * 2 + x) * 2 + c) * BLOCK, BLOCK, 16)
    r.c_all[own_rows, :] = half(r.xs[0:BLOCK, :])
    rows = [ref[...].astype(F32).reshape(1, 256) for ref in (r.v0, r.v1, r.v2, r.v3, r.v4, r.v5, r.v6)]
    rows += [jnp.zeros((1, 256), F32), r.route_in[...].astype(F32), jnp.zeros((4, 256), F32)]
    r.vec[c] = jnp.concatenate(rows, axis=0)
    r.binf[...] = r.bin[...].astype(F32)

    lane, row = iota((ROWS, 128), 1), iota((ROWS, 128), 0)
    r.pairs[0:8, :] = jnp.full((8, ROWS), -1.0, F32)
    r.pairs[8:16, :] = jnp.zeros((8, ROWS), F32)
    r.pairs[0:2, 0:tokens] = r.routes_in[...].astype(F32)
    r.pairs[8:12, 0:tokens] = r.noise_in[...]
    by_token = jnp.concatenate([r.pairs[...], jnp.zeros((112, ROWS), F32)], axis=0).T
    experts = [by_token[:, k:k + 1] for k in range(2)]
    noise = pltpu.roll(by_token, 120, 1)
    onehot = [jnp.where(lane.astype(F32) == experts[k], 1.0, 0.0) for k in range(2)]
    count = jnp.broadcast_to(column_sum(onehot[0] + onehot[1]), (8, 128))

    r.count_out[0] = count

    places = iota((ROWS, r.prio.shape[1]), 1) - 2 * iota((ROWS, r.prio.shape[1]), 0)
    ranks = r.prio[...].astype(F32)
    codes = [experts[k] * 1024.0 + jnp.sum(jnp.where(places == k, ranks, 0.0), axis=1, keepdims=True) for k in range(2)]
    codes = [jnp.where(row[:, 0:1] < tokens, code, -1.0) for code in codes]
    code_rows = jnp.where(lane == 0, codes[0], jnp.where(lane == 1, codes[1], 0.0)).T
    before = []
    for k in range(2):
        floor = experts[k] * 1024.0
        seen = 0.0
        for j in range(2):
            others = code_rows[j:j + 1, :]
            seen = seen + jnp.where((others < codes[k]) & (others >= floor), 1.0, 0.0)
        before.append(jnp.sum(seen, axis=1, keepdims=True))

    def count_copy(stage, i, slot, target):
        return remote(r.count_out.at[stage], r.count_in.at[slot], r.count_send.at[i], r.count_recv.at[slot], target)

    spot = y * 2 + x
    column = [(rep(k, y, x), c) for k in range(zs)]

    def counts_to_plane():
        for d in range(1, 4):
            q = lax.rem(spot + d, 4)
            count_copy(1, d, 1 + spot, (rep(z, q // 2, lax.rem(q, 2)), c)).start()

    def counts_up():
        for k in range(1, zs):
            pl.when(z < k)(lambda k=k: count_copy(2, 3 + k, 5 + z, column[k]).start())

    for copy in halves:
        copy.wait()
    pl.semaphore_wait(bar, zs + 3)

    weights = [remote(ref, ref, r.w_send.at[i], r.w_recv.at[i], partner) for i, ref in enumerate(
        (r.vec.at[c], r.wqkv.at[mine, :], r.wproj.at[mine, :]))]
    for copy in weights:
        copy.start()
    gathers = [Halves((r.n_all, r.c_all)[m], (r.g_send.at[m], r.g_recv.at[m], r.g_csend.at[m], r.g_crecv.at[m]))
               for m in range(2)]
    ga, gb = gathers
    gb.begin()
    count_copy(0, 0, 0, partner).start()

    r.xs[0:tokens, :] = r.x[...].astype(F32)
    xhat, spread1 = normalize(r.xs[...])
    r.xhat1[...] = xhat

    count_copy(0, 0, 0, partner).wait_recv()
    ahead = jnp.where(c == 1, 1.0, 0.0) * r.count_in[0]
    count = count + r.count_in[0]
    r.count_out[1] = count
    counts_to_plane()

    weights[0].wait_send()
    remote(r.vec.at[1 - c], r.vec.at[1 - c], r.w_send.at[0], r.w_recv.at[0], partner).wait_recv()
    vec = jnp.concatenate([r.vec[0], r.vec[1]], axis=1)
    gain1, bias1, bias_q, bias_v, bias_p, gain2, bias2 = [vec[i:i + 1, :] for i in range(7)]
    route_rows = jnp.concatenate([vec[8:16, :], jnp.zeros((120, 512), F32)], axis=0)
    route_t, route = half(route_rows), half(route_rows.T)
    r.n1[...] = half(xhat * gain1 + bias1)

    for i, ref in ((1, r.wqkv), (2, r.wproj)):
        weights[i].wait_send()
        ref = ref.at[other, :]
        remote(ref, ref, r.w_send.at[i], r.w_recv.at[i], partner).wait_recv()
    for i, bias in enumerate((bias_q, None, bias_v)):
        part = dot(r.n1[...], r.wqkv[:, 512 * i:512 * (i + 1)])
        r.mixed[:, 512 * i:512 * (i + 1)] = half(part if bias is None else part + bias)

    for q in range(4):
        pl.when(spot != q)(lambda q=q: count_copy(1, 1, 1 + q, partner).wait_recv())
    for q in range(4):
        ahead = ahead + jnp.where(spot > q, r.count_in[1 + q], 0.0)
        count = count + jnp.where(spot != q, r.count_in[1 + q], 0.0)
    r.count_out[2] = count
    counts_up()

    gb.turn()

    low_lane = lane < HEAD_DIM
    key_kept = iota((ROWS, ROWS), 1) < tokens

    def heads_forward(i, _):
        q, k, v = [r.mixed[:, many(base + 128 * i, 128, 128)] for base in (0, 512, 1024)]
        q = q * BF16(HEAD_DIM ** -0.5)
        parts = []
        for h in range(2):
            s = dot_nt(jnp.where(low_lane == (h == 0), q, jnp.zeros_like(q)), k)
            s = jnp.where(key_kept, s, -1e30)
            e = jnp.exp(s - jnp.max(s, axis=-1, keepdims=True))
            p = e / jnp.sum(e, axis=-1, keepdims=True)
            r.probs[2 * i + h] = p
            parts.append(dot(half(p), v))
        r.ctx[:, many(128 * i, 128, 128)] = half(jnp.where(low_lane, parts[0], parts[1]))
        return 0

    lax.fori_loop(0, 4, heads_forward, 0)

    gb.far()
    middle = r.xs[...] + (dot(r.ctx[...], r.wproj[...]) + bias_p)
    r.mid[...] = middle
    xhat, spread2 = normalize(middle)
    r.xhat2[...] = xhat
    n2 = half(xhat * gain2 + bias2)
    own_first = ((y * 2 + x) * 2 + c) * BLOCK
    r.n_all[many(own_first, LATE, 16), :] = n2[0:LATE, :]
    ga.begin(slice(0, 2))
    for k in range(zs - 1):
        pl.when(z > k)(lambda k=k: count_copy(2, 4, 5 + k, partner).wait_recv())
    for k in range(zs - 1):
        ahead = ahead + jnp.where(z > k, r.count_in[5 + k], 0.0)
    offsets = ahead[0:1, :]
    chosen = 0.0
    for k in range(2):
        slot = before[k] + jnp.sum(onehot[k] * offsets, axis=1, keepdims=True)
        chosen = chosen + onehot[k] * jnp.where(slot < float(capacity), 1.0, 0.0)
    r.chosen[...] = chosen
    logits = jnp.where(lane < 4, dot(n2, route) + noise, -1e30)
    e = jnp.exp(logits - jnp.max(logits, axis=-1, keepdims=True))
    rprobs = e / jnp.sum(e, axis=-1, keepdims=True)
    r.rprobs[...] = rprobs
    gates = rprobs * chosen
    gates_high = half(gates).astype(F32)
    packed = jnp.where(lane < 4, gates_high, pltpu.roll(gates - gates_high, 4, 1)).T
    packed = jnp.concatenate([packed[0:8, :], jnp.zeros((8, 256), F32)], axis=1)
    r.n_all[many(own_first + LATE, BLOCK - LATE, 16), :] = half(jnp.concatenate(
        [n2[LATE:LATE + 8, :].astype(F32), packed], axis=0))
    ga.begin(slice(2, 3))

    pair = many(spot * 2 * BLOCK, 2 * BLOCK, 16)
    for g in gathers:
        g.from_core(spot)
    for j in range(2):
        g8 = r.n_all[many((spot * 2 + j) * BLOCK + 192, 16, 16), 0:256].astype(F32)[8:16, :]
        g8 = g8 + pltpu.roll(g8, 4, 0)
        g8 = jnp.where(c == 0, g8, pltpu.roll(g8, 6, 0))
        r.gcol[j * BLOCK:(j + 1) * BLOCK, :] = jnp.concatenate([g8, jnp.zeros((120, 256), F32)], axis=0).T[0:BLOCK, :]
    for copy in loads:
        copy.wait()
    r.running[...] = jnp.zeros_like(r.running)
    r.drows[...] = jnp.zeros_like(r.drows)
    r.dgate[...] = jnp.zeros_like(r.dgate)
    r.extra[...] = jnp.zeros_like(r.extra)
    pair_lane = iota((2 * BLOCK, 128), 1)
    def expert_pass(e, between):
        gate = r.gcol[:, e:e + 1]
        r.res[...] = jnp.zeros_like(r.res)
        d_result = gate * r.c_all[pair, :].astype(F32)
        r.dres[...] = half(d_result)
        r.extra[0, 2 + e:3 + e, 0:512] = column_sum(r.dres[...].astype(F32))

        def hidden_step(j, _):
            hs = many(j * STEP, STEP, STEP)
            n = r.n_all[pair, :]
            pre = dot(n, r.win[e, :, hs]) + r.bin[e:e + 1, hs].astype(F32)
            hid, slope = gelu_parts(pre)
            r.res[...] += dot(half(hid), r.wout[e, hs, :])
            d_pre = half(slope * dot_nt(r.dres[...], r.wout[e, hs, :]))
            r.extra[0, e:e + 1, hs] = column_sum(d_pre.astype(F32))
            r.drows[...] += dot_nt(d_pre, r.win[e, :, hs])
            return 0

        lax.fori_loop(0, 2, hidden_step, 0)
        between()
        lax.fori_loop(2, 4, hidden_step, 0)
        result = r.res[...] + r.bout[e:e + 1, :].astype(F32)
        r.running[...] += gate * result
        d_gate = jnp.sum(r.c_all[pair, :].astype(F32) * result, axis=1, keepdims=True)
        r.dgate[...] = jnp.where(pair_lane == 2 * c + e, d_gate, r.dgate[...])

    expert_pass(0, ga.turn)
    ga.far()

    for g in gathers:
        for other_spot in g.others():
            g.from_core(other_spot)
    span = 8 * BLOCK
    row = jnp.zeros((8, span), F32)
    for d in range(8):
        g8 = r.n_all[d * BLOCK + 192:(d + 1) * BLOCK, 0:256].astype(F32)[8:16, :]
        g8 = g8 + pltpu.roll(g8, 4, 0)
        g8 = jnp.where(c == 0, g8, pltpu.roll(g8, 6, 0))
        at, shift = d * BLOCK // 128 * 128, d * BLOCK % 128
        width = min(384, span - at)
        g8 = jnp.concatenate([g8, jnp.zeros((8, 128), F32)], axis=1)
        g8 = pltpu.roll(g8, shift, 1) if shift else g8
        pieces = [jnp.zeros((8, at), F32)] if at else []
        pieces += [g8[:, 0:width]] + ([jnp.zeros((8, span - at - width), F32)] if span > at + width else [])
        row = row + jnp.concatenate(pieces, axis=1)
    r.g_all[...] = row

    slot = lax.rem(x + y, 2)

    def where_from(f, slice_of, x_of):
        s, i, kind = f // PER, lax.rem(f, PER) // 2, lax.rem(f, 2)
        t = jnp.maximum(s - 2, 0)
        e = jnp.where(s < 2, s, t // 2)
        start = slice_of * 1024 + jnp.where(s < 2, 512 + x_of * SLICE, lax.rem(t, 2) * SLICE)
        return e, start, i, kind

    def landing(f, slice_of=slot, x_of=x):
        e, start, i, kind = where_from(f, slice_of, x_of)
        return r.grads.at[kind * 2 + e, many(start + i * PIECE, PIECE, PIECE), :]

    def up_copy(src, f):
        return remote(src, r.up_in.at[f], r.bulk.at[0], r.up_recv.at[f], up)

    def down_copy(src, f):
        return remote(src, r.down_in.at[f], r.bulk.at[1], r.down_recv.at[f], down)

    def keep_copy(f):
        return pltpu.make_async_copy(r.fin.at[f], landing(f), r.bulk.at[2])

    def give_x(f, recv, ref=None):
        return remote(r.fin.at[f], landing(f) if ref is None else ref, r.bulk.at[3], recv, xn)

    def give_y(f, recv, ref=None):
        return remote(r.fin.at[f], landing(f) if ref is None else ref, r.bulk.at[4], recv, yn)

    def pass_x(f):
        ref = landing(f, 1 - slot, x)
        return remote(ref, ref, r.bulk.at[5], r.bulk.at[7], xn)

    def pass_y(f):
        ref = landing(f, 1 - slot, 1 - x)
        return remote(ref, ref, r.bulk.at[6], r.bulk.at[8], yn)

    def goes(f):
        late = lax.rem(f // PER, 2)
        return (f < SETS) | (late == 0), (f < SETS) | (late == 1), lax.rem(f, PER) < PER // 2

    def inside(f, count=PIECES):
        return (f >= 0) & (f < count)

    def tick(t):
        u, d, f, w = t - HOP * z, t - HOP * (zs - 1 - z), t - HOP * (zs - 1), t - HOP * (zs - 1) - PASS

        @pl.when(inside(u))
        def _():
            pl.when(z == 0)(lambda: up_copy(r.own.at[u], u).start())

            @pl.when(low_z)
            def _():
                up_copy(r.up_out.at[u], u).wait_recv()

                @pl.when(high_z)
                def _():
                    r.up_out[u] = half(r.own[u].astype(F32) + r.up_in[u].astype(F32))
                    up_copy(r.up_out.at[u], u).start()

        @pl.when(inside(d))
        def _():
            pl.when(z == zs - 1)(lambda: down_copy(r.own.at[d], d).start())

            @pl.when(high_z)
            def _():
                down_copy(r.down_out.at[d], d).wait_recv()

                @pl.when(low_z)
                def _():
                    r.down_out[d] = half(r.own[d].astype(F32) + r.down_in[d].astype(F32))
                    down_copy(r.down_out.at[d], d).start()

        @pl.when(inside(f))
        def _():
            lower = jnp.where(low_z, r.up_in[f].astype(F32), 0.0)
            upper = jnp.where(high_z, r.down_in[f].astype(F32), 0.0)
            r.fin[f] = half(r.own[f].astype(F32) + lower + upper)
            keep_copy(f).start()
            to_x, to_y, by_x = goes(f)
            single = f < SETS
            pl.when(to_x & single & jnp.logical_not(by_x))(lambda: give_x(f, r.x_recv.at[jnp.minimum(f, SETS - 1)]).start())
            pl.when(to_x & jnp.logical_not(single & jnp.logical_not(by_x)))(lambda: give_x(f, r.bulk.at[7]).start())
            pl.when(to_y & single & by_x)(lambda: give_y(f, r.y_recv.at[jnp.minimum(f, SETS - 1)]).start())
            pl.when(to_y & jnp.logical_not(single & by_x))(lambda: give_y(f, r.bulk.at[8]).start())

        @pl.when(inside(w, SETS))
        def _():
            _, _, by_x = goes(w)

            @pl.when(by_x)
            def _():
                give_y(w, r.y_recv.at[w], landing(w, 1 - slot, x)).wait_recv()
                pass_x(w).start()

            @pl.when(jnp.logical_not(by_x))
            def _():
                give_x(w, r.x_recv.at[w], landing(w, 1 - slot, 1 - x)).wait_recv()
                pass_y(w).start()

    def finish_pieces():
        both = PIECES - SETS
        some = SETS + both // 2
        got = both // 2 + SETS
        pl.when(high_z)(lambda: remote(r.own, r.up_in, r.bulk.at[0], r.bulk.at[0], up).wait_send())
        pl.when(low_z)(lambda: remote(r.own, r.down_in, r.bulk.at[1], r.bulk.at[1], down).wait_send())
        pltpu.make_async_copy(r.fin, r.own, r.bulk.at[2]).wait()
        for i, count in ((3, some), (4, some), (5, SETS // 2), (6, SETS // 2)):
            remote(r.fin.at[0:count], r.own.at[0:count], r.bulk.at[i], r.bulk.at[i], xn).wait_send()
        for i in (7, 8):
            remote(r.fin.at[0:got], r.own.at[0:got], r.bulk.at[i], r.bulk.at[i], xn).wait_recv()

    far_half = (1 - x, 1 - y)
    near_half = (x, y)
    quarter = (x * 2 + y, 4 + y * 2 + x)
    near, next_near = (xn, yn), (yn, xn)

    def cols(j, n):
        return many(j * 256, 256 * n, 256)

    def ar(i, src, dst, target):
        return remote(src, dst, r.ar_send.at[i], r.ar_recv.at[i], target)

    def ar_one(s):
        return ar(s, r.total.at[:, cols(4 * s + 2 * far_half[s], 2)], r.part_in.at[s], near[s])

    def ar_two(s):
        give = 4 * s + 2 * near_half[s] + (1 - near_half[1 - s])
        return ar(2 + s, r.total.at[:, cols(give, 1)], r.part_in.at[2 + s, :, 0:256], next_near[s])

    def ar_up(s):
        return ar(4 + s, r.z_out.at[s], r.z_in.at[s], up)

    def ar_down(s):
        return ar(6 + s, r.z_out.at[2 + s], r.z_in.at[2 + s], down)

    def ar_four(s):
        piece = r.final.at[:, cols(quarter[s], 1)]
        return ar(8 + s, piece, piece, next_near[s])

    def ar_four_got(s):
        piece = r.final.at[:, cols(4 * s + 2 * near_half[s] + (1 - near_half[1 - s]), 1)]
        return ar(8 + s, piece, piece, next_near[s])

    def ar_five(s):
        piece = r.final.at[:, cols(4 * s + 2 * near_half[s], 2)]
        return ar(10 + s, piece, piece, near[s])

    def ar_five_got(s):
        piece = r.final.at[:, cols(4 * s + 2 * far_half[s], 2)]
        return ar(10 + s, piece, piece, near[s])

    def add_into(ref, other_part):
        ref[...] = half(ref[...].astype(F32) + other_part.astype(F32))

    def ar_stage1():
        for s in range(2):
            ar_one(s).start()

    def ar_stage2():
        for s in range(2):
            ar_one(s).wait()
            add_into(r.total.at[:, cols(4 * s + 2 * near_half[s], 2)], r.part_in[s])
            ar_two(s).start()

    def ar_stage3():
        for s in range(2):
            ar_two(s).wait()
            add_into(r.total.at[:, cols(quarter[s], 1)], r.part_in[2 + s, :, 0:256])

            @pl.when(z == 0)
            def _():
                r.z_out[s] = r.total[:, cols(quarter[s], 1)]
                ar_up(s).start()

            @pl.when(z == zs - 1)
            def _():
                r.z_out[2 + s] = r.total[:, cols(quarter[s], 1)]
                ar_down(s).start()

    def ar_stage_z(k):
        for s in range(2):
            @pl.when(z == k)
            def _():
                ar_up(s).wait_recv()
                if k < zs - 1:
                    r.z_out[s] = half(r.total[:, cols(quarter[s], 1)].astype(F32) + r.z_in[s].astype(F32))
                    ar_up(s).start()

            @pl.when(z == zs - 1 - k)
            def _():
                ar_down(s).wait_recv()
                if k < zs - 1:
                    r.z_out[2 + s] = half(r.total[:, cols(quarter[s], 1)].astype(F32) + r.z_in[2 + s].astype(F32))
                    ar_down(s).start()

    def ar_stage4():
        for s in range(2):
            lower = jnp.where(low_z, r.z_in[s].astype(F32), 0.0)
            upper = jnp.where(high_z, r.z_in[2 + s].astype(F32), 0.0)
            own = r.total[:, cols(quarter[s], 1)].astype(F32)
            r.final[:, cols(quarter[s], 1)] = half(own + lower + upper)
            ar_four(s).start()

    def ar_stage5():
        for s in range(2):
            ar_four_got(s).wait_recv()
            ar_five(s).start()

    def ar_stage6():
        for s in range(2):
            ar_five_got(s).wait_recv()
            ar_four(s).wait_send()
            ar_five(s).wait_send()
            pl.when(high_z)(lambda s=s: ar_up(s).wait_send())
            pl.when(low_z)(lambda s=s: ar_down(s).wait_send())

    stages_at = {4: ar_stage2, 5: ar_stage3}

    def slice_step(s, _):
        e, start, _, _ = where_from(s * PER, slot, x)
        hs = many(start, SLICE, SLICE)
        wi = half(r.win[e, :, hs].astype(F32).T)
        wo = r.wout[e, hs, :]
        bias = jnp.broadcast_to(r.binf[pl.ds(e, 1), hs], (128, SLICE)).T[:, 0:1]
        n, co, g = r.n_all[...], r.c_all[...], r.g_all[pl.ds(e, 1), :]
        hid, slope = gelu_parts(dot_nt(wi, n) + bias)
        dh = dot_nt(wo, co)
        for kind, grad in ((0, dot(half(slope * (dh * g)), n)), (1, dot(half(hid * g), co))):
            for i in range(SLICE // PIECE):
                r.own[s * PER + i * 2 + kind] = half(grad[i * PIECE:(i + 1) * PIECE, :])
        for at, todo in stages_at.items():
            pl.when(s == at)(todo)
        for k in range(TICKS):
            pl.when(s < EARLY)(lambda k=k: tick(s * TICKS + k))
        for k in range(LATER):
            pl.when(s >= EARLY)(lambda k=k: tick(middle + (s - EARLY) * LATER + k))
        return 0

    middle = EARLY * TICKS + sum(BEATS)
    assert middle <= EARLY * PER

    lax.fori_loop(0, EARLY, slice_step, 0)
    clock, beats = iter(range(EARLY * TICKS, middle)), iter(BEATS)

    def beat():
        for _ in range(next(beats)):
            tick(next(clock))


    expert_pass(1, beat)
    beat()
    theirs, ours = many((1 - c) * BLOCK, BLOCK, 8), many(c * BLOCK, BLOCK, 8)
    partials = [remote(src.at[theirs, :], dst, r.p_send.at[i], r.p_recv.at[i], partner) for i, (src, dst) in enumerate(
        ((r.running, r.got_running), (r.drows, r.got_drows), (r.dgate, r.got_dgate)))]
    for copy in partials:
        copy.start()
    beat()
    for copy in partials:
        copy.wait()

    r.out[...] = half(r.mid[0:BLOCK, :] + (r.running[ours, :] + r.got_running[...]))[0:tokens, :]
    zeros = jnp.zeros((ROWS - BLOCK, 128), F32)
    d_gates = jnp.concatenate([r.dgate[ours, :] + r.got_dgate[...], zeros], axis=0)
    rprobs, chosen = r.rprobs[...], r.chosen[...]
    d_probs = d_gates * chosen
    d_logits = half(rprobs * (d_probs - jnp.sum(rprobs * d_probs, axis=-1, keepdims=True)))
    r.dn[0:BLOCK, :] = r.drows[ours, :] + r.got_drows[...]
    r.dn[BLOCK:ROWS, :] = jnp.zeros((ROWS - BLOCK, 512), F32)
    beat()
    dn = r.dn[...] + dot(d_logits, route_t)
    xhat = r.xhat2[...]
    n2 = half(xhat * gain2 + bias2)
    grad_route = dot(half(d_logits.astype(F32).T), n2)
    vector_rows = {5: column_sum(dn * xhat), 6: column_sum(dn)}
    r.xs[...] = jnp.zeros_like(r.xs)
    r.xs[0:tokens, :] = r.cot[...].astype(F32)
    d_middle = r.xs[...] + norm_back(dn, xhat, spread2, gain2)
    r.mid[...] = d_middle
    r.db[...] = half(d_middle)
    db = r.db[...]
    vector_rows[4] = column_sum(db.astype(F32))
    r.dense[:, 1536:2048] = half(dot(half(r.ctx[...].astype(F32).T), db))
    r.dctx[...] = half(dot_nt(db, r.wproj[...]))
    beat()

    def heads_back(i, _):
        q, k, v = [r.mixed[:, many(base + 128 * i, 128, 128)] for base in (0, 512, 1024)]
        q = q * BF16(HEAD_DIM ** -0.5)
        do = r.dctx[:, many(128 * i, 128, 128)]
        parts = []
        for h in range(2):
            p = r.probs[2 * i + h]
            dp = dot_nt(jnp.where(low_lane == (h == 0), do, jnp.zeros_like(do)), v)
            ds = p * (dp - jnp.sum(p * dp, axis=-1, keepdims=True))
            parts.append((dot(half(ds), k) * HEAD_DIM ** -0.5, dot(half(ds.T), q), dot(half(p.T), do)))
        for j, base in enumerate((0, 512, 1024)):
            r.dmixed[:, many(base + 128 * i, 128, 128)] = half(jnp.where(low_lane, parts[0][j], parts[1][j]))
        return 0

    beat()
    lax.fori_loop(0, 4, heads_back, 0)
    beat()
    n1_t = half(r.n1[...].astype(F32).T)
    dn = 0.0
    for i in range(3):
        part = r.dmixed[:, 512 * i:512 * (i + 1)]
        if i != 1:
            vector_rows[2 + i // 2] = column_sum(part.astype(F32))
        r.dense[:, 512 * i:512 * (i + 1)] = half(dot(n1_t, part))
        dn = dn + dot_nt(part, r.wqkv[:, 512 * i:512 * (i + 1)])
        beat()
    xhat = r.xhat1[...]
    vector_rows[0] = column_sum(dn * xhat)
    vector_rows[1] = column_sum(dn)
    r.igrad[...] = (r.mid[...] + norm_back(dn, xhat, spread1, gain1))[0:tokens, :]

    vectors = jnp.concatenate([grad_route[0:4, :]] + [vector_rows[i] for i in range(7)] + [jnp.zeros((5, 512), F32)], axis=0)
    r.dn[0:16, :] = vectors
    low_half, high_half = r.dn[0:16, 0:256], r.dn[0:16, 256:512]
    r.extra[1, :, 0:256] = jnp.where(c == 0, high_half, low_half)
    own_half = jnp.where(c == 0, low_half, high_half)
    swaps = [remote(r.dense.at[other, :], r.dense_in, r.d_send.at[0], r.d_recv.at[0], partner),
             remote(r.extra.at[1], r.extra.at[2], r.d_send.at[1], r.d_recv.at[1], partner)]
    for copy in swaps:
        copy.start()
    for copy in swaps:
        copy.wait()
    r.total[0:256, :] = half(r.dense[mine, :].astype(F32) + r.dense_in[...].astype(F32))
    sums = own_half + r.extra[2, :, 0:256]
    small = jnp.concatenate([r.extra[0, 0:4, :], jnp.zeros((12, 2048), F32)], axis=0)
    shifted = jnp.concatenate([jnp.zeros((4, 256), F32), sums[0:12, :]], axis=0)
    r.total[256:272, :] = half(small + jnp.concatenate([shifted, jnp.zeros((16, 1792), F32)], axis=1))

    ar_stage1()

    lax.fori_loop(EARLY, STEPS, slice_step, 0)
    start, ends = middle + (STEPS - EARLY) * LATER, PIECES + HOP * (zs - 1)
    stages = {0: lambda: ar_stage_z(1), 3: lambda: ar_stage_z(2), 6: lambda: ar_stage_z(3), 8: ar_stage4, 11: ar_stage5}

    def last_ticks(t, _):
        tick(t)
        for at, stage in stages.items():
            pl.when(t == start + at)(stage)
        return 0

    lax.fori_loop(start, ends, last_ticks, 0)
    ar_stage6()
    finish_pieces()
    for g in gathers:
        g.drain()
    for i in range(4):
        count_copy(min(i, 1), i, 0, partner).wait_send()
    for k in range(1, zs):
        pl.when(z < k)(lambda k=k: count_copy(2, 3 + k, 0, partner).wait_send())


def block_call(zs, *args):
    tokens, width = args[0].shape
    vm, hbm = pl.BlockSpec(memory_space=pltpu.VMEM), pl.BlockSpec(memory_space=pl.ANY)
    shape = jax.ShapeDtypeStruct
    in_specs = [hbm if name in ("win_in", "wout_in", "wqkv_in", "wproj_in") else vm for name in INPUTS]
    scratch = [pltpu.VMEM(dims, dtype) for _, dims, dtype in SCRATCH]
    scratch += [pltpu.SemaphoreType.DMA(dims) for _, dims in SEMS]
    return pl.pallas_call(
        functools.partial(block_kernel, zs),
        out_shape=(shape((tokens, width), BF16), shape((tokens, width), F32), shape((4, 2048, 512), BF16), shape((272, 2048), BF16)),
        in_specs=in_specs,
        out_specs=(vm, vm, hbm, vm),
        scratch_shapes=scratch,
        compiler_params=pltpu.CompilerParams(collective_id=0, has_side_effects=True, vmem_limit_bytes=63 << 20),
        name="encoder_block",
    )(*args)


def finish_kernel(grads, summed, out_in, igrad_in, grad_in, grad_out, qkv, proj, igrad, out, route, bias_in, bias_out, *rest):
    vectors, (got, done_in, done_out, sums, wide, narrow, igrad_now, got_sem, done_sem, sem) = rest[:7], rest[7:]
    n = done_in.shape[0]

    def source(k, i):
        return pltpu.make_async_copy(
            grads.at[2 * k + i // 4, many(lax.rem(i, 4) * STEP, STEP, STEP), :], got.at[k * n + i], got_sem.at[k * n + i])

    def results(i):
        where = many(lax.rem(i, 4) * STEP, STEP, STEP)
        return (pltpu.make_async_copy(done_in.at[i], grad_in.at[i // 4, :, where], done_sem.at[i]),
                pltpu.make_async_copy(done_out.at[i], grad_out.at[i // 4, where, :], done_sem.at[n + i]))

    def fetch(i, _):
        source(1, i).start()
        source(0, i).start()
        return 0

    arrivals = [pltpu.make_async_copy(summed, sums, sem.at[0]), pltpu.make_async_copy(igrad_in, igrad_now, sem.at[1])]
    others = [pltpu.make_async_copy(wide, qkv, sem.at[2]), pltpu.make_async_copy(narrow, proj, sem.at[3]),
              pltpu.make_async_copy(igrad_now, igrad, sem.at[4])]
    lax.fori_loop(0, 2, fetch, 0)
    for copy in arrivals:
        copy.start()
    lax.fori_loop(2, n, fetch, 0)

    def convert(i, _):
        to_in, to_out = results(i)
        source(1, i).wait()
        done_out[i] = got[n + i].astype(F32)
        to_out.start()
        source(0, i).wait()
        done_in[i] = got[i].astype(F32).T
        to_in.start()
        return 0

    lax.fori_loop(0, n - 2, convert, 0)
    for copy in arrivals:
        copy.wait()
    wide[...] = sums[0:256, 0:1536].astype(F32)
    narrow[...] = sums[0:256, 1536:2048].astype(F32)
    for copy in others:
        copy.start()
    lax.fori_loop(n - 2, n, convert, 0)
    out[...] = out_in[...]
    rows = sums[256:272, :].astype(F32)
    bias_in[...] = rows[0:2, :]
    bias_out[...] = rows[2:4, 0:512]
    route[...] = rows[4:8, 0:256]
    for i, ref in enumerate(vectors):
        ref[...] = rows[8 + i, 0:256]

    def settle(i, _):
        for copy in results(i):
            copy.wait()
        return 0

    lax.fori_loop(0, n, settle, 0)
    for copy in others:
        copy.wait()


def finish(grads, summed, out, igrad):
    shape = jax.ShapeDtypeStruct
    vm, hbm = pl.BlockSpec(memory_space=pltpu.VMEM), pl.BlockSpec(memory_space=pl.ANY)
    large = [shape((2, 512, 2048), F32), shape((2, 2048, 512), F32), shape((256, 1536), F32), shape((256, 512), F32),
             shape(igrad.shape, igrad.dtype)]
    small = [shape(out.shape, out.dtype), shape((4, 256), F32), shape((2, 2048), F32), shape((2, 512), F32)] + [shape((256,), F32)] * 7
    n = 8
    return pl.pallas_call(
        finish_kernel,
        out_shape=large + small,
        in_specs=[hbm, hbm, vm, hbm],
        out_specs=[hbm] * len(large) + [vm] * len(small),
        scratch_shapes=[
            pltpu.VMEM((2 * n, STEP, 512), BF16), pltpu.VMEM((n, 512, STEP), F32), pltpu.VMEM((n, STEP, 512), F32),
            pltpu.VMEM(summed.shape, BF16), pltpu.VMEM((256, 1536), F32), pltpu.VMEM((256, 512), F32),
            pltpu.VMEM(igrad.shape, igrad.dtype),
            pltpu.SemaphoreType.DMA((2 * n,)), pltpu.SemaphoreType.DMA((2 * n,)), pltpu.SemaphoreType.DMA((5,)),
        ],
        compiler_params=pltpu.CompilerParams(vmem_limit_bytes=60 << 20),
        name="finish",
    )(grads, summed, out, igrad)


def swap(v):
    return lax.ppermute(v, "shard", [(0, 1), (1, 0)])


def fused(inputs, norm1_gain, norm1_bias, qkv_weight, query_bias, value_bias, out_weight, out_bias, norm2_gain, norm2_bias,
          router_weight, noise, expert_in, expert_in_bias, expert_out, expert_out_bias, routes, priority, cotangent):
    out, igrad, grads, summed = block_call(
        lax.axis_size("replica") // 4, inputs, cotangent, noise.T, routes.T, priority, norm1_gain, norm1_bias, query_bias,
        value_bias, out_bias, norm2_gain, norm2_bias, router_weight.T, qkv_weight, out_weight, expert_in, expert_out,
        expert_in_bias, expert_out_bias)
    grad_in, grad_out, qkv, proj, igrad, out, route, bias_in, bias_out, *cols = finish(grads, summed, out, igrad)
    return (out, igrad, cols[0], cols[1], qkv, cols[2], cols[3], proj, cols[4], cols[5], cols[6], route.T,
            grad_in, bias_in, grad_out, bias_out)


def layer_norm(values, gain_vector, bias_vector):
    centered = values - jnp.mean(values, axis=-1, keepdims=True)
    spread = lax.rsqrt(jnp.mean(centered * centered, axis=-1, keepdims=True) + LN_EPS)
    return centered * spread * gain_vector + bias_vector


def kept_gates(pair_expert, ranks, offsets, capacity, expert_count):
    same = pair_expert[:, None] == pair_expert[None, :]
    earlier = ranks[None, :] < ranks[:, None]
    before = jnp.sum(jnp.where(same & earlier, 1, 0).astype(jnp.int32), axis=1)
    onehot = pair_expert[:, None] == jnp.arange(expert_count, dtype=jnp.int32)[None, :]
    first_slot = jnp.sum(jnp.where(onehot, offsets[None, :], 0).astype(jnp.int32), axis=1)
    keep = before + first_slot < capacity
    picked = jnp.where(onehot & keep[:, None], 1.0, 0.0).astype(jnp.float32)
    return jnp.sum(picked.reshape(-1, 2, expert_count), axis=1)


def general(
    inputs, norm1_gain, norm1_bias, qkv_weight, query_bias, value_bias, out_weight, out_bias, norm2_gain, norm2_bias,
    router_weight, noise, expert_in, expert_in_bias, expert_out, expert_out_bias, routes, priority, cotangent,
):
    tok_count, width = inputs.shape
    replicas, cores = lax.axis_size("replica"), lax.axis_size("shard")
    shard = lax.axis_index("shard")
    images = tok_count // PATCHES
    heads = width // HEAD_DIM
    owned, _, hidden_count = expert_in.shape
    expert_count = owned * cores
    score_scale = HEAD_DIM ** (-0.5)
    f32 = jnp.float32

    vectors = (norm1_gain, norm1_bias, query_bias, value_bias, out_bias, norm2_gain, norm2_bias)
    packed = jnp.concatenate(
        [qkv_weight, out_weight, jnp.stack(vectors, axis=1), router_weight], axis=1)
    packed = lax.all_gather(packed, "shard", axis=0, tiled=True)
    weight_qkv = packed[:, :3 * width]
    weight_proj = packed[:, 3 * width:4 * width]
    small = packed[:, 4 * width:]
    gain_one, bias_one, bias_query, bias_value, bias_proj, gain_two, bias_two = [
        small[:, i].astype(f32) for i in range(len(vectors))]
    weight_route = small[:, len(vectors):]

    pair_expert = routes.reshape(-1)
    onehot_pairs = (pair_expert[:, None] == jnp.arange(expert_count, dtype=jnp.int32)[None, :]).astype(jnp.int32)
    load = jnp.sum(onehot_pairs, axis=0)
    loads = lax.all_gather(load, ("replica", "shard"))
    position = lax.axis_index("replica") * cores + shard
    ahead = jnp.arange(replicas * cores)[:, None] < position
    offsets = jnp.sum(jnp.where(ahead, loads, 0), axis=0)
    capacity = 2 * tok_count * replicas * cores // expert_count
    chosen = kept_gates(pair_expert, priority.reshape(-1), offsets, capacity, expert_count)

    residual_in = inputs.astype(f32)
    normed_one, norm_one_back = jax.vjp(layer_norm, residual_in, gain_one, bias_one)
    normed_one_half = half(normed_one)
    qkv_bias = jnp.concatenate([bias_query, jnp.zeros_like(bias_query), bias_value])
    mixed = half(dot(normed_one_half, weight_qkv) + qkv_bias)
    shaped = mixed.reshape(images, PATCHES, 3, heads, HEAD_DIM)
    query, keys, values = (shaped[:, :, 0], shaped[:, :, 1], shaped[:, :, 2])
    scores = jnp.einsum("bqhd,bkhd->bhqk", query, keys, preferred_element_type=f32) * score_scale
    row_max = jnp.max(scores, axis=-1, keepdims=True)
    log_total = row_max + jnp.log(jnp.sum(jnp.exp(scores - row_max), axis=-1, keepdims=True))
    context = jnp.einsum(
        "bhqk,bkhd->bqhd", half(jnp.exp(scores - log_total)), values, preferred_element_type=f32)
    context_half = half(context.reshape(tok_count, width))
    middle = residual_in + (dot(context_half, weight_proj) + bias_proj)
    normed_two, norm_two_back = jax.vjp(layer_norm, middle, gain_two, bias_two)
    normed_two_half = half(normed_two)
    logits = dot(normed_two_half, weight_route) + noise
    route_probs = jax.nn.softmax(logits, axis=-1)
    gate_weights = route_probs * chosen
    upstream = cotangent.astype(f32)

    pair_n = jnp.concatenate([normed_two_half, swap(normed_two_half)], axis=0)
    pair_c = jnp.concatenate([cotangent, swap(cotangent)], axis=0)
    own_gates = lax.dynamic_slice_in_dim(gate_weights, shard * owned, owned, 1)
    other_gates = swap(lax.dynamic_slice_in_dim(gate_weights, (1 - shard) * owned, owned, 1))
    pair_g = jnp.concatenate([own_gates, other_gates], axis=0)
    pair_up = pair_c.astype(f32)
    running = jnp.zeros((2 * tok_count, width), f32)
    d_rows = jnp.zeros((2 * tok_count, width), f32)
    gate_columns, bias_in_grads, bias_out_grads, in_grads, out_grads = [], [], [], [], []
    for e in range(owned):
        gate = pair_g[:, e:e + 1]
        pre = dot(pair_n, expert_in[e]) + expert_in_bias[e].astype(f32)
        act, slope = gelu_parts(pre)
        hid = half(act)
        result = dot(hid, expert_out[e]) + expert_out_bias[e].astype(f32)
        running = running + gate * result
        gate_columns.append(jnp.sum(pair_up * result, axis=1))
        d_result = half(gate * pair_up)
        d_pre = half(slope * dot_nt(d_result, expert_out[e]))
        d_rows = d_rows + dot_nt(d_pre, expert_in[e])
        bias_in_grads.append(jnp.sum(d_pre.astype(f32), axis=0))
        bias_out_grads.append(jnp.sum(d_result.astype(f32), axis=0))
        in_grads.append(jnp.einsum("td,th->dh", pair_n, d_pre, preferred_element_type=f32))
        out_grads.append(jnp.einsum("th,td->hd", hid, d_result, preferred_element_type=f32))
    d_gate_part = jnp.stack(gate_columns, axis=1)
    running = running[:tok_count] + swap(running[tok_count:])
    d_normed = d_rows[:tok_count] + swap(d_rows[tok_count:])
    d_gate_other = swap(d_gate_part[tok_count:])
    d_gate_own = d_gate_part[:tok_count]
    d_gates = jnp.where(shard == 0, jnp.concatenate([d_gate_own, d_gate_other], axis=1),
                        jnp.concatenate([d_gate_other, d_gate_own], axis=1))

    grad_in = lax.psum(half(jnp.stack(in_grads, axis=0)), "replica")
    grad_out = lax.psum(half(jnp.stack(out_grads, axis=0)), "replica")

    output = half(middle + running)
    d_probs = d_gates * chosen
    d_logits = half(route_probs * (d_probs - jnp.sum(route_probs * d_probs, axis=-1, keepdims=True)))
    grad_route = jnp.einsum("td,te->de", normed_two_half, d_logits, preferred_element_type=f32)
    d_normed = d_normed + dot_nt(d_logits, weight_route)
    d_middle, grad_gain_two, grad_bias_two = norm_two_back(d_normed)
    d_middle = d_middle + upstream
    d_branch = half(d_middle)
    grad_proj = jnp.einsum("tc,td->cd", context_half, d_branch, preferred_element_type=f32)
    grad_proj_bias = jnp.sum(d_branch.astype(f32), axis=0)
    d_context = half(dot_nt(d_branch, weight_proj)).reshape(images, PATCHES, heads, HEAD_DIM)
    attn_probs = jnp.exp(scores - log_total)
    d_attn = jnp.einsum("bqhd,bkhd->bhqk", d_context, values, preferred_element_type=f32)
    d_values = jnp.einsum("bhqk,bqhd->bkhd", half(attn_probs), d_context, preferred_element_type=f32)
    d_scores = half(attn_probs * (d_attn - jnp.sum(attn_probs * d_attn, axis=-1, keepdims=True)))
    d_query = jnp.einsum("bhqk,bkhd->bqhd", d_scores, keys, preferred_element_type=f32) * score_scale
    d_keys = jnp.einsum("bhqk,bqhd->bkhd", d_scores, query, preferred_element_type=f32) * score_scale
    d_mixed = half(jnp.stack([d_query, d_keys, d_values], axis=2).reshape(tok_count, 3 * width))
    grad_qkv = jnp.einsum("td,tf->df", normed_one_half, d_mixed, preferred_element_type=f32)
    mixed_sums = jnp.sum(d_mixed.astype(f32), axis=0)
    d_normed_one = dot_nt(d_mixed, weight_qkv)
    d_input, grad_gain_one, grad_bias_one = norm_one_back(d_normed_one)
    input_grad = d_input + d_middle

    columns = jnp.stack((grad_gain_one, grad_bias_one, mixed_sums[:width], mixed_sums[2 * width:], grad_proj_bias,
                         grad_gain_two, grad_bias_two), axis=1)
    dense = half(jnp.concatenate([grad_qkv, grad_proj, columns, grad_route], axis=1))
    mine = width // 2
    keep = lax.dynamic_slice_in_dim(dense, shard * mine, mine, 0)
    give = lax.dynamic_slice_in_dim(dense, (1 - shard) * mine, mine, 0)
    dense = keep.astype(f32) + swap(give).astype(f32)
    bias_row = jnp.concatenate(bias_in_grads + bias_out_grads)
    summed, bias_row = lax.psum((half(dense), bias_row), "replica")
    summed = summed.astype(f32)
    columns = [summed[:, 4 * width + i] for i in range(len(vectors))]
    grad_in_bias = bias_row[:owned * hidden_count].reshape(owned, hidden_count)
    grad_out_bias = bias_row[owned * hidden_count:].reshape(owned, width)
    return (
        output, input_grad, columns[0], columns[1], summed[:, :3 * width], columns[2], columns[3],
        summed[:, 3 * width:4 * width], columns[4], columns[5], columns[6], summed[:, 4 * width + len(vectors):],
        grad_in.astype(f32), grad_in_bias, grad_out.astype(f32), grad_out_bias,
    )


def on_device(*args):
    expert_in, inputs = args[12], args[0]
    planes = lax.axis_size("replica") == 16 and lax.axis_size("shard") == 2
    if planes and inputs.shape == (PATCHES, 512) and expert_in.shape == (2, 512, 2048):
        return fused(*args)
    return general(*args)


def solution(mesh):
    both, split = ("replica", "shard"), "shard"
    return jax.shard_map(
        on_device,
        mesh=mesh,
        in_specs=(
            P(both, None), P(split), P(split), P(split, None), P(split), P(split), P(split, None), P(split), P(split),
            P(split), P(split, None), P(both, None), P(split, None, None), P(split, None), P(split, None, None),
            P(split, None), P(both, None), P(both, None), P(both, None),
        ),
        out_specs=(
            P(both, None), P(both, None), P(split), P(split), P(split, None), P(split), P(split), P(split, None),
            P(split), P(split), P(split), P(split, None), P(split, None, None), P(split, None), P(split, None, None),
            P(split, None),
        ),
        check_vma=False,
    )
```
